32 devices in a mesh: wide: 16 (over z, y, core), narrow: 2 (over x).
Axes of the slice: x: 2, y: 2, z: 4, core: 2. Of those that a mesh axis runs over, the one named last changes fastest.
Arguments:
- features: bfloat16 [16, 384, 1024], P('wide', 'narrow'), may hold values from -6 to 6
- embedding: bfloat16 [16, 768], P('wide'), may hold values from -6 to 6
- valid_mask: int32 [16, 1024], P('wide'), may hold values from 0 to 1, as said below
- cotangent: bfloat16 [16, 384, 1024], P('wide', 'narrow'), may hold values from -6 to 6
- conv_first: float32 [3456, 384], P('wide', 'narrow'), may hold values from -0.109375 to 0.109375
- conv_first_moment: float32 [3456, 384], P('wide', 'narrow'), may hold values from -48 to 48
- conv_first_square: float32 [3456, 384], P('wide', 'narrow'), may hold values from 5.0176 to 20.0704
- conv_second: float32 [3456, 384], P('wide', 'narrow'), may hold values from -0.109375 to 0.109375
- conv_second_moment: float32 [3456, 384], P('wide', 'narrow'), may hold values from -48 to 48
- conv_second_square: float32 [3456, 384], P('wide', 'narrow'), may hold values from 5.0176 to 20.0704
- film_weight: float32 [768, 2, 384], P('wide', None, 'narrow'), may hold values from -0.21875 to 0.21875
- film_weight_moment: float32 [768, 2, 384], P('wide', None, 'narrow'), may hold values from -20 to 20
- film_weight_square: float32 [768, 2, 384], P('wide', None, 'narrow'), may hold values from 0.9216 to 3.6864
- attend_in: float32 [384, 3, 384], P('wide', None, 'narrow'), may hold values from -0.3125 to 0.3125
- attend_in_moment: float32 [384, 3, 384], P('wide', None, 'narrow'), may hold values from -64 to 64
- attend_in_square: float32 [384, 3, 384], P('wide', None, 'narrow'), may hold values from 10.24 to 40.96
- attend_out: float32 [384, 384], P('wide', 'narrow'), may hold values from -2.5 to 2.5
- attend_out_moment: float32 [384, 384], P('wide', 'narrow'), may hold values from -5 to 5
- attend_out_square: float32 [384, 384], P('wide', 'narrow'), may hold values from 0.1024 to 0.4096
- vectors: float32 [13, 384], P(None, 'narrow')
- vectors_moment: float32 [13, 384], P(None, 'narrow'), may hold values from -48 to 48
- vectors_square: float32 [13, 384], P(None, 'narrow'), may hold values from 5.0176 to 20.0704
Outputs:
- output: bfloat16 [16, 384, 1024], P('wide', 'narrow')
- input_gradient: bfloat16 [16, 384, 1024], P('wide', 'narrow')
- conv_first_gradient: float32 [3456, 384], P('wide', 'narrow')
- conv_first_new: float32 [3456, 384], P('wide', 'narrow')
- conv_first_moment_new: float32 [3456, 384], P('wide', 'narrow')
- conv_first_square_new: float32 [3456, 384], P('wide', 'narrow')
- conv_second_gradient: float32 [3456, 384], P('wide', 'narrow')
- conv_second_new: float32 [3456, 384], P('wide', 'narrow')
- conv_second_moment_new: float32 [3456, 384], P('wide', 'narrow')
- conv_second_square_new: float32 [3456, 384], P('wide', 'narrow')
- film_weight_gradient: float32 [768, 2, 384], P('wide', None, 'narrow')
- film_weight_new: float32 [768, 2, 384], P('wide', None, 'narrow')
- film_weight_moment_new: float32 [768, 2, 384], P('wide', None, 'narrow')
- film_weight_square_new: float32 [768, 2, 384], P('wide', None, 'narrow')
- attend_in_gradient: float32 [384, 3, 384], P('wide', None, 'narrow')
- attend_in_new: float32 [384, 3, 384], P('wide', None, 'narrow')
- attend_in_moment_new: float32 [384, 3, 384], P('wide', None, 'narrow')
- attend_in_square_new: float32 [384, 3, 384], P('wide', None, 'narrow')
- attend_out_gradient: float32 [384, 384], P('wide', 'narrow')
- attend_out_new: float32 [384, 384], P('wide', 'narrow')
- attend_out_moment_new: float32 [384, 384], P('wide', 'narrow')
- attend_out_square_new: float32 [384, 384], P('wide', 'narrow')
- vectors_gradient: float32 [13, 384], P(None, 'narrow')
- vectors_new: float32 [13, 384], P(None, 'narrow')
- vectors_moment_new: float32 [13, 384], P(None, 'narrow')
- vectors_square_new: float32 [13, 384], P(None, 'narrow')
The draws below stay inside these ranges and needn't reach their ends.
Inputs may be any that keep to these rules, and one draw needn't show every extreme that they name: `valid_mask`: each sample's mask is either all ones or ones exactly on a 16 x 16 square of pixels.
All inputs are finite; a program needn't handle non-finite values.
Results may differ from the reference program's by a relative error of at most 0.02.
Values may be sent and summed in bfloat16 or wider, within the bound.
No kernel may reach another device: no remote copies, remote signals or barrier semaphores. Data moves between devices by JAX's collectives and lax.ppermute only.
A program may use at most 128 MiB of HBM per device.

```python
import math
import jax
import jax.numpy as jnp
from jax import lax

C = 384
HEADS = 4
GROUPS = 32
EMB = 768
SIDE = 32
WINDOW = 16
STEP = 10
NV = 13
PIXELS = 1024
SAMPLES = 16


def draw_valid_mask(key, part):
    key = jax.random.fold_in(key, 11)
    key_whole, key_row, key_col = jax.random.split(key, 3)
    whole = jax.random.randint(key_whole, (SAMPLES,), 0, 2)
    row_start = jax.random.randint(key_row, (SAMPLES,), 0, SIDE - WINDOW + 1)
    col_start = jax.random.randint(key_col, (SAMPLES,), 0, SIDE - WINDOW + 1)
    row_index = jnp.arange(SIDE, dtype=jnp.int32)[None, :, None]
    col_index = jnp.arange(SIDE, dtype=jnp.int32)[None, None, :]
    inside_rows = (row_index >= row_start[:, None, None]) & (row_index < row_start[:, None, None] + WINDOW)
    inside_cols = (col_index >= col_start[:, None, None]) & (col_index < col_start[:, None, None] + WINDOW)
    inside = (inside_rows & inside_cols).astype(jnp.int32)
    result = jnp.where(whole[:, None, None] > 0, jnp.ones_like(inside), inside)
    return result.reshape(SAMPLES, SIDE * SIDE).astype(jnp.int32)


def draw_vectors(key, part):
    key = jax.random.fold_in(key, 23)
    key_gain, key_bias = jax.random.split(key, 2)
    gain_rows = jax.random.uniform(key_gain, (NV, C), jnp.float32, 0.6, 1.4)
    bias_rows = 0.3 * jax.random.normal(key_bias, (NV, C), jnp.float32)
    row_index = jnp.arange(NV)[:, None]
    is_gain = (row_index == 0) | (row_index == 3) | (row_index == 6)
    return jnp.where(is_gain, gain_rows, bias_rows).astype(jnp.float32)


def steps_of(own_key, dims, shards, least, largest):
    def one(position, blocks):
        draws = jax.random.uniform(jax.random.fold_in(jax.random.fold_in(own_key, 6), position), (blocks,), jnp.float32, least / len(shards), largest / len(shards))
        return jnp.repeat(jnp.exp(draws), dims[position] // blocks).reshape((-1,) + (1,) * (len(dims) - position - 1))

    gain = one(*shards[0])
    for cut in shards[1:]:
        gain = gain * one(*cut)
    return gain


def noise(key, shape, spread, limit, shards=(), kind=jnp.bfloat16):
    values = spread * jax.random.normal(key, shape, jnp.float32)
    if shards:
        values = values * steps_of(key, shape, shards, -0.22, 0.18)
    return jnp.clip(values, -limit, limit).astype(kind)


def setup_inputs(seed: int = 0) -> dict:
    key_list = jax.random.split(jax.random.key(seed), 23)
    features = noise(key_list[0], (SAMPLES, C, PIXELS), 1.0, 6.0, ((0, 16), (1, 2)))
    embedding = noise(key_list[1], (SAMPLES, EMB), 1.0, 6.0, ((0, 16),))
    valid_mask = draw_valid_mask(jax.random.fold_in(key_list[22], 71), 0)
    cotangent = noise(key_list[3], (SAMPLES, C, PIXELS), 1.0, 6.0, ((0, 16), (1, 2)))
    conv_first = noise(key_list[4], (9 * C, C), (9 * C) ** -0.5, 0.109375, ((0, 16), (1, 2)), jnp.float32)
    conv_first_moment = noise(key_list[5], (9 * C, C), (0.111 * (0.245 * (SIDE * SIDE + WINDOW * WINDOW) * SAMPLES) ** 0.5), 48.0, ((0, 16), (1, 2)), jnp.float32)
    conv_first_square = jnp.clip(jnp.exp(math.log(20.0704) - 1.3862944 * jax.random.uniform(key_list[6], (9 * C, C), jnp.float32) ** steps_of(key_list[6], (9 * C, C), ((0, 16), (1, 2)), -0.2, 0.2)), 5.0176, 20.0704)
    conv_second = noise(key_list[7], (9 * C, C), (9 * C) ** -0.5, 0.109375, ((0, 16), (1, 2)), jnp.float32)
    conv_second_moment = noise(key_list[8], (9 * C, C), (0.111 * (0.245 * (SIDE * SIDE + WINDOW * WINDOW) * SAMPLES) ** 0.5), 48.0, ((0, 16), (1, 2)), jnp.float32)
    conv_second_square = jnp.clip(jnp.exp(math.log(20.0704) - 1.3862944 * jax.random.uniform(key_list[9], (9 * C, C), jnp.float32) ** steps_of(key_list[9], (9 * C, C), ((0, 16), (1, 2)), -0.2, 0.2)), 5.0176, 20.0704)
    film_weight = noise(key_list[10], (EMB, 2, C), EMB ** -0.5, 0.21875, ((0, 16), (2, 2)), jnp.float32)
    film_weight_moment = noise(key_list[11], (EMB, 2, C), (0.111 * (0.045 * (SIDE * SIDE + WINDOW * WINDOW) * SAMPLES) ** 0.5), 20.0, ((0, 16), (2, 2)), jnp.float32)
    film_weight_square = jnp.clip(jnp.exp(math.log(3.6864) - 1.3862944 * jax.random.uniform(key_list[12], (EMB, 2, C), jnp.float32) ** steps_of(key_list[12], (EMB, 2, C), ((0, 16), (2, 2)), -0.2, 0.2)), 0.9216, 3.6864)
    attend_in = noise(key_list[13], (C, 3, C), C ** -0.5, 0.3125, ((0, 16), (2, 2)), jnp.float32)
    attend_in_moment = noise(key_list[14], (C, 3, C), (0.111 * (0.5 * (SIDE * SIDE + WINDOW * WINDOW) * SAMPLES) ** 0.5), 64.0, ((0, 16), (2, 2)), jnp.float32)
    attend_in_square = jnp.clip(jnp.exp(math.log(40.96) - 1.3862944 * jax.random.uniform(key_list[15], (C, 3, C), jnp.float32) ** steps_of(key_list[15], (C, 3, C), ((0, 16), (2, 2)), -0.2, 0.2)), 10.24, 40.96)
    attend_out = noise(key_list[16], (C, C), (C // 64) ** -0.5, 2.5, ((0, 16), (1, 2)), jnp.float32)
    attend_out_moment = noise(key_list[17], (C, C), (0.111 * (0.005 * (SIDE * SIDE + WINDOW * WINDOW) * SAMPLES) ** 0.5), 5.0, ((0, 16), (1, 2)), jnp.float32)
    attend_out_square = jnp.clip(jnp.exp(math.log(0.4096) - 1.3862944 * jax.random.uniform(key_list[18], (C, C), jnp.float32) ** steps_of(key_list[18], (C, C), ((0, 16), (1, 2)), -0.2, 0.2)), 0.1024, 0.4096)
    vectors = draw_vectors(jax.random.fold_in(key_list[22], 71), 0)
    vectors_moment = noise(key_list[20], (NV, C), (0.111 * (0.245 * (SIDE * SIDE + WINDOW * WINDOW) * SAMPLES) ** 0.5), 48.0, ((1, 2),), jnp.float32)
    vectors_square = jnp.clip(jnp.exp(math.log(20.0704) - 1.3862944 * jax.random.uniform(key_list[21], (NV, C), jnp.float32) ** steps_of(key_list[21], (NV, C), ((1, 2),), -0.2, 0.2)), 5.0176, 20.0704)
    return dict(features=features, embedding=embedding, valid_mask=valid_mask, cotangent=cotangent, conv_first=conv_first, conv_first_moment=conv_first_moment, conv_first_square=conv_first_square, conv_second=conv_second, conv_second_moment=conv_second_moment, conv_second_square=conv_second_square, film_weight=film_weight, film_weight_moment=film_weight_moment, film_weight_square=film_weight_square, attend_in=attend_in, attend_in_moment=attend_in_moment, attend_in_square=attend_in_square, attend_out=attend_out, attend_out_moment=attend_out_moment, attend_out_square=attend_out_square, vectors=vectors, vectors_moment=vectors_moment, vectors_square=vectors_square)


@jax.custom_vjp
def low(v):
    return lax.optimization_barrier(v.astype(jnp.bfloat16)).astype(jnp.float32)

@jax.custom_vjp
def low_back(v):
    return v

def low_keep(v):
    return (low(v), None)

def low_pass(kept, grad):
    return (grad,)

def back_keep(v):
    return (v, None)

def back_low(kept, grad):
    return (low(grad),)
low.defvjp(low_keep, low_pass)
low_back.defvjp(back_keep, back_low)
beta_one = 0.9
beta_two = 0.999
adam_eps = 1e-08
decay_rate = 0.01
norm_eps = 1e-05
masked_score = -1e+30

def step_rates():
    return (2.0 * (9 * C) ** (-0.5), 2.0 * (9 * C) ** (-0.5), 2.0 * EMB ** (-0.5), 2.0 * C ** (-0.5), 2.0 * (C // 64) ** (-0.5), 0.5)

def norm_forward(inputs, validity, gain_row, shift_row):
    samples, pixels, channels = inputs.shape
    per_group = C // GROUPS
    grouped = inputs.reshape(samples, pixels, channels // per_group, per_group)
    weight = validity.reshape(samples, pixels, 1, 1)
    tallies = lax.optimization_barrier(jnp.sum(weight, axis=(1, 3), keepdims=True)) * per_group
    average = lax.optimization_barrier(jnp.sum(grouped * weight, axis=(1, 3), keepdims=True)) / tallies
    centred = grouped - average
    variance = lax.optimization_barrier(jnp.sum(centred * centred * weight, axis=(1, 3), keepdims=True)) / tallies
    normed = (centred * lax.rsqrt(variance + norm_eps)).reshape(samples, pixels, channels)
    return (normed * gain_row + shift_row) * validity[:, :, None]

def convolve(inputs, kernel):
    samples = inputs.shape[0]
    channels = inputs.shape[2]
    picture = inputs.reshape(samples, SIDE, SIDE, channels)
    result = lax.conv_general_dilated(picture, kernel.reshape(3, 3, channels, kernel.shape[1]), (1, 1), 'SAME', dimension_numbers=('NHWC', 'HWIO', 'NHWC'), precision=lax.Precision.HIGHEST)
    return result.reshape(samples, SIDE * SIDE, kernel.shape[1])

def attend_one(pieces):
    queries, key_rows, values, validity = pieces
    head_size = C // HEADS
    query_heads = queries.reshape(PIXELS, HEADS, head_size)
    key_heads = key_rows.reshape(PIXELS, HEADS, head_size)
    value_heads = values.reshape(PIXELS, HEADS, head_size)
    scores = jnp.einsum('qhd,khd->hqk', query_heads, key_heads, precision=lax.Precision.HIGHEST) * head_size ** (-0.5)
    scores = low_back(jnp.where(validity[None, None, :] > 0, scores, masked_score))
    highest = lax.optimization_barrier(jnp.max(scores, axis=2, keepdims=True))
    exponent = jnp.exp(scores - highest)
    weights = low(exponent / lax.optimization_barrier(jnp.sum(exponent, axis=2, keepdims=True)))
    mixture = jnp.einsum('hqk,khd->qhd', weights, value_heads, precision=lax.Precision.HIGHEST)
    return mixture.reshape(PIXELS, C)

def forward(params, inputs, soft_embed, validity):
    conv_first, conv_second, film_weight, attend_in, attend_out, vectors = params
    samples = inputs.shape[0]
    valid_col = validity[:, :, None]
    hidden_one = low(jax.nn.silu(norm_forward(inputs, validity, vectors[0], vectors[1])))
    conv_out_one = low_back(convolve(hidden_one, low(conv_first)) + vectors[2])
    film_terms = jnp.dot(soft_embed, low(film_weight).reshape(EMB, 2 * C), precision=lax.Precision.HIGHEST)
    film_terms = low_back(film_terms.reshape(samples, 2, C) + vectors[11:13])
    norm_two = norm_forward(conv_out_one, validity, vectors[3], vectors[4])
    modulated = norm_two * (1.0 + film_terms[:, None, 0]) + film_terms[:, None, 1]
    hidden_two = low(jax.nn.silu(modulated) * valid_col)
    conv_out_two = low_back(convolve(hidden_two, low(conv_second)) + vectors[5])
    residual = (inputs + conv_out_two) * valid_col
    norm_three = low(norm_forward(residual, validity, vectors[6], vectors[7]))
    triple_low = low(attend_in)
    flat_rows = norm_three.reshape(-1, C)
    queries = low_back(low(jnp.dot(flat_rows, triple_low[:, 0], precision=lax.Precision.HIGHEST) + vectors[8]))
    key_rows = low_back(low(jnp.dot(flat_rows, triple_low[:, 1], precision=lax.Precision.HIGHEST)))
    values = low_back(low(jnp.dot(flat_rows, triple_low[:, 2], precision=lax.Precision.HIGHEST) + vectors[9]))
    shape_three = (samples, PIXELS, C)
    attended = lax.map(jax.checkpoint(attend_one), (queries.reshape(shape_three), key_rows.reshape(shape_three), values.reshape(shape_three), validity))
    attended = low_back(low(attended))
    projected = jnp.dot(attended.reshape(-1, C), low(attend_out), precision=lax.Precision.HIGHEST).reshape(shape_three)
    return residual + (projected + vectors[10]) * valid_col

def adam_update(weight, gradient, moment, square, step_rate):
    moment_new = beta_one * moment + (1.0 - beta_one) * gradient
    square_new = beta_two * square + (1.0 - beta_two) * gradient * gradient
    ratio = moment_new / (1.0 - beta_one ** STEP) / (jnp.sqrt(square_new / (1.0 - beta_two ** STEP)) + adam_eps)
    return (weight - step_rate * (ratio + decay_rate * weight), moment_new, square_new)

def reference(features, embedding, valid_mask, cotangent, conv_first, conv_first_moment, conv_first_square, conv_second, conv_second_moment, conv_second_square, film_weight, film_weight_moment, film_weight_square, attend_in, attend_in_moment, attend_in_square, attend_out, attend_out_moment, attend_out_square, vectors, vectors_moment, vectors_square):
    validity = valid_mask.astype(jnp.float32)
    soft_embed = low(jax.nn.silu(embedding.astype(jnp.float32)))
    inputs = jnp.transpose(features.astype(jnp.float32), (0, 2, 1))
    params = (conv_first, conv_second, film_weight, attend_in, attend_out, vectors)
    output, pullback = jax.vjp(lambda weights, activations: forward(weights, activations, soft_embed, validity), params, inputs)
    weight_grads, input_grad = pullback(jnp.transpose(cotangent.astype(jnp.float32), (0, 2, 1)))
    moments = (conv_first_moment, conv_second_moment, film_weight_moment, attend_in_moment, attend_out_moment, vectors_moment)
    squares = (conv_first_square, conv_second_square, film_weight_square, attend_in_square, attend_out_square, vectors_square)
    rates = step_rates()
    results = [jnp.transpose(output.astype(jnp.bfloat16), (0, 2, 1)), jnp.transpose(input_grad.astype(jnp.bfloat16), (0, 2, 1))]
    for index in range(6):
        new_weight, moment_new, square_new = adam_update(params[index], weight_grads[index], moments[index], squares[index], rates[index])
        results = results + [weight_grads[index], new_weight, moment_new, square_new]
    return tuple(results)
```

```python
import jax
import jax.numpy as jnp
from jax import lax
from jax.experimental import pallas as pl
from jax.experimental.pallas import tpu as pltpu
from jax.sharding import PartitionSpec as P

C = 384
HEADS = 4
GROUPS = 32
EMB = 768
SIDE = 32
STEP = 10
PIX = SIDE * SIDE
HALF = C // 2
PADDED = PIX + 2 * SIDE
HEAD = C // HEADS
ROWS = 216
CHUNK = 64

beta_one = 0.9
beta_two = 0.999
adam_eps = 1e-08
decay_rate = 0.01
norm_eps = 1e-05
masked_score = -1e30
score_scale = HEAD ** (-0.5)
exponent_scale = score_scale * 1.4426950408889634

f32 = jnp.float32
bf16 = jnp.bfloat16
ON_LAST = (((1,), (1,)), ((), ()))
ON_FIRST = (((0,), (0,)), ((), ()))
VMEM_BYTES = 56 * 1024 * 1024


def step_rates():
    return (
        2.0 * (9 * C) ** (-0.5),
        2.0 * (9 * C) ** (-0.5),
        2.0 * EMB ** (-0.5),
        2.0 * C ** (-0.5),
        2.0 * (C // 64) ** (-0.5),
        0.5,
    )


def spec():
    return pl.BlockSpec(memory_space=pltpu.VMEM)


def call(body, outs, ins, scalars, scratch=(), flops=0):
    moved = sum(a.size * a.dtype.itemsize for a in list(ins) + list(outs))
    return pl.pallas_call(
        body,
        out_shape=tuple(outs),
        in_specs=[pl.BlockSpec(memory_space=pltpu.SMEM)] + [spec() for _ in ins],
        out_specs=tuple(spec() for _ in outs),
        scratch_shapes=list(scratch),
        compiler_params=pltpu.CompilerParams(vmem_limit_bytes=VMEM_BYTES),
        cost_estimate=pl.CostEstimate(flops=flops, bytes_accessed=moved, transcendentals=0),
    )(scalars, *ins)


def shaped(shape, kind):
    return jax.ShapeDtypeStruct(shape, kind)


def aligned(value, by):
    return pl.multiple_of(value, by)


def wide_mask(mask_ref, start, count):
    part = mask_ref[pl.ds(start, count), :]
    return jnp.concatenate((part, part, part), axis=1)


def group_sum(row):
    first = (lax.broadcasted_iota(jnp.int32, (C, C), 0) * 5462) >> 16
    second = (lax.broadcasted_iota(jnp.int32, (C, C), 1) * 5462) >> 16
    member = jnp.where(first == second, 1.0, 0.0).astype(f32)
    spread = jnp.broadcast_to(row, (8, C))
    return jnp.dot(
        spread, member, preferred_element_type=f32, precision=lax.Precision.HIGHEST
    )[0:1]


def fold(block):
    return jnp.sum(block.reshape(block.shape[0] // 8, 8, block.shape[1]), axis=0)


def total(acc):
    return jnp.sum(acc, axis=0, keepdims=True)


def chunks(step, init):
    def body(index, carry):
        return step(aligned(index * CHUNK, CHUNK), carry)

    return lax.fori_loop(0, PIX // CHUNK, body, init, unroll=2)


def norm_stats(source_ref, mask_ref):
    zero = jnp.zeros((8, C), f32)

    def first(start, carry):
        sums, count = carry
        valid = wide_mask(mask_ref, start, CHUNK)
        return (sums + fold(source_ref[pl.ds(start, CHUNK), :] * valid), count + fold(valid))

    sums, count = chunks(first, (zero, zero))
    tally = total(count) * float(C // GROUPS)
    mean = group_sum(total(sums)) / tally

    def second(start, carry):
        valid = wide_mask(mask_ref, start, CHUNK)
        centred = source_ref[pl.ds(start, CHUNK), :] - mean
        return carry + fold(centred * centred * valid)

    variance = group_sum(total(chunks(second, zero))) / tally
    return mean, lax.rsqrt(variance + norm_eps), tally


def keep_stats(stat_ref, mean, inverse, tally):
    stat_ref[0:1, :] = mean
    stat_ref[1:2, :] = inverse
    stat_ref[2:3, :] = tally


def column_index(count):
    return lax.broadcasted_iota(jnp.int32, (count, 1), 0) & (SIDE - 1)


def write_taps(rows_ref, taps_ref):
    blank = jnp.zeros((SIDE, 3 * C), bf16)
    taps_ref[0:SIDE, :] = blank
    taps_ref[SIDE + PIX : PADDED, :] = blank
    column = column_index(CHUNK)
    for index in range(PIX // CHUNK):
        start = index * CHUNK
        here = pl.ds(SIDE + start, CHUNK)
        left = rows_ref[pl.ds(7 + start, CHUNK), :]
        right = rows_ref[pl.ds(9 + start, CHUNK), :]
        taps_ref[here, 0:C] = jnp.where(column == 0, 0.0, left).astype(bf16)
        taps_ref[here, C : 2 * C] = rows_ref[pl.ds(8 + start, CHUNK), :].astype(bf16)
        taps_ref[here, 2 * C : 3 * C] = jnp.where(column == SIDE - 1, 0.0, right).astype(bf16)


def lane(count):
    return lax.broadcasted_iota(jnp.int32, (count, 128), 1)


def own_half(block, narrow):
    one, two, three = block[:, 0:128], block[:, 128:256], block[:, 256:384]
    turned_two, turned_three = pltpu.roll(two, 64, 1), pltpu.roll(three, 64, 1)
    upper = jnp.where(lane(block.shape[0]) < 64, turned_two, turned_three)
    return jnp.concatenate(
        (jnp.where(narrow == 0, one, upper), jnp.where(narrow == 0, two, turned_three)), axis=1
    )


def write_own(rows_ref, own_ref, narrow):
    blank = jnp.zeros((SIDE, 256), bf16)
    own_ref[0:SIDE, :] = blank
    own_ref[SIDE + PIX : PADDED, :] = blank
    for index in range(PIX // CHUNK):
        start = index * CHUNK
        block = rows_ref[pl.ds(8 + start, CHUNK), :]
        own_ref[pl.ds(SIDE + start, CHUNK), :] = own_half(block, narrow).astype(bf16)


def convolve(taps_ref, kernel_ref, done, block=512):
    for index in range(PIX // block):
        start = index * block
        acc = None
        for tap in range(3):
            part = jnp.dot(
                taps_ref[pl.ds(start + SIDE * tap, block), :],
                kernel_ref[tap * 3 * C : (tap + 1) * 3 * C, :],
                preferred_element_type=f32,
            )
            acc = part if acc is None else acc + part
        done(start, block, acc)


def convolve_back(taps_ref, kernel_ref, done, block=512):
    for index in range(PIX // block):
        start = index * block
        acc = None
        for tap in range(9):
            tap_row, tap_col = tap // 3, tap % 3
            flipped = 8 - tap
            part = lax.dot_general(
                taps_ref[pl.ds(start + SIDE * tap_row, block), tap_col * C : (tap_col + 1) * C],
                kernel_ref[flipped * C : (flipped + 1) * C, :],
                ON_LAST,
                preferred_element_type=f32,
            )
            acc = part if acc is None else acc + part
        done(start, block, acc)


def kernel_terms(taps_ref, own_ref, terms_ref):
    for tap_col in range(3):
        for tap_row in range(3):
            tap = 3 * tap_row + tap_col
            first = 2 * SIDE - SIDE * tap_row
            terms_ref[tap * C : (tap + 1) * C, :] = lax.dot_general(
                taps_ref[SIDE : SIDE + PIX, tap_col * C : (tap_col + 1) * C],
                own_ref[first : first + PIX, :],
                ON_FIRST,
                preferred_element_type=f32,
            )


def slope(value):
    logistic = lax.logistic(value)
    return logistic * (1.0 + value * (1.0 - logistic))


def tile_parts(block, narrow):
    rows = block.shape[0]
    one = block[:, 0:128]
    two = jnp.concatenate((block[:, 128:192], jnp.zeros((rows, 64), f32)), axis=1)
    turned = jnp.where(lane(rows) < 64, pltpu.roll(one, 64, 1), pltpu.roll(two, 64, 1))
    return jnp.where(narrow == 0, one, turned), jnp.where(narrow == 0, two, one)


def pair_rows(block, top):
    rows = block.shape[0]
    low = block[top:rows]
    if rows < 2 * top:
        low = jnp.concatenate((low, jnp.zeros((2 * top - rows, 128), f32)), axis=0)
    return jnp.where(lane(top) < 64, block[0:top], pltpu.roll(low, 64, 1))


def pad_rows(block, rows):
    if block.shape[0] == rows:
        return block
    return jnp.concatenate((block, jnp.zeros((rows - block.shape[0], block.shape[1]), f32)), axis=0)


def middle(first, second, top, rows):
    one = jnp.where(lane(top) < 64, first, pltpu.roll(second, 64, 1))
    two = jnp.where(lane(top) < 64, pltpu.roll(first, 64, 1), second)
    return jnp.concatenate((one, two[0 : rows - top]), axis=0)


def pack_first(at, conv_ref, out_ref):
    part, shared = tile_parts(conv_ref[...], at[0])
    out_ref[0:224, :] = pad_rows(part, 224).astype(bf16)
    out_ref[224:336, :] = pair_rows(shared, 112).astype(bf16)


FILM_AT, SHARED_AT = 224, 320
FILM_SHARED, IN_AT, IN_SHARED, OUT_AT, OUT_SHARED, SECOND_ROWS = 112, 160, 240, 288, 320, 336


def pack_second(at, conv_ref, film_ref, in_ref, out_weight_ref, out_ref):
    narrow = at[0]

    def put(start, block):
        rows = -(-block.shape[0] // 16) * 16
        out_ref[start : start + rows, :] = pad_rows(block, rows).astype(bf16)

    part, shared = tile_parts(conv_ref[...], narrow)
    put(0, part)
    put(SHARED_AT, pair_rows(shared, 112))
    part, shared = tile_parts(jnp.concatenate((film_ref[0], film_ref[1]), axis=0), narrow)
    put(FILM_AT, part)
    put(SHARED_AT + FILM_SHARED, pair_rows(shared, 48))
    part, shared = tile_parts(jnp.concatenate((in_ref[0], in_ref[1], in_ref[2]), axis=0), narrow)
    put(SHARED_AT + IN_AT, part)
    put(SHARED_AT + IN_SHARED, pair_rows(shared, 40))
    part, shared = tile_parts(out_weight_ref[...], narrow)
    put(SHARED_AT + OUT_AT, part)
    put(SHARED_AT + OUT_SHARED, pair_rows(shared, 16))


class Gathered:
    def __init__(self, at, refs):
        self.narrow, self.core, self.side, self.depth = at[0], at[1], at[2], at[3]
        keys = ((0, 0), (1, 0), (0, 1), (1, 1))
        self.own = dict(zip(keys, refs[:4]))
        self.other = dict(zip(keys, refs[4:]))

    def chips(self):
        for differs in (0, 1):
            for step in range(4):
                yield differs, step, (self.depth ^ step) * 2 + (self.side ^ differs)

    def cores(self, differs, step, start, rows):
        upto = -(-rows // 16) * 16
        found = []
        for across in (0, 1):
            own = self.own[differs, across][step, start : start + upto, :].astype(f32)[0:rows]
            other = self.other[differs, across][step, start : start + upto, :].astype(f32)[0:rows]
            found.append(
                (jnp.where(self.core == 0, own, other), jnp.where(self.core == 0, other, own))
            )
        here, there = found
        return tuple(
            tuple(
                jnp.where((self.narrow == 0) == (tile == 0), here[core], there[core])
                for core in (0, 1)
            )
            for tile in (0, 1)
        )


def place_conv(whole, shared, shared_at, kernel_ref):
    for differs, step, chip in whole.chips():
        rows = pl.ds(aligned(chip * (2 * ROWS), 16), 2 * ROWS)
        low, high = whole.cores(differs, step, 0, ROWS)
        kernel_ref[rows, 0:128] = jnp.concatenate(low, axis=0).astype(bf16)
        kernel_ref[rows, 256:384] = jnp.concatenate(high, axis=0).astype(bf16)
        low, high = shared.cores(differs, step, shared_at, 112)
        kernel_ref[rows, 128:256] = jnp.concatenate(
            [middle(low[core], high[core], 112, ROWS) for core in (0, 1)], axis=0
        ).astype(bf16)


def place_film(whole, shared, film_ref):
    for differs, step, chip in whole.chips():
        rows = pl.ds(aligned(chip * 96, 16), 96)
        low, high = whole.cores(differs, step, FILM_AT, 96)
        for index in (0, 1):
            part = slice(48 * index, 48 * index + 48)
            film_ref[rows, index * C : index * C + 128] = jnp.concatenate(
                [low[core][part] for core in (0, 1)], axis=0
            ).astype(bf16)
            film_ref[rows, index * C + 256 : index * C + 384] = jnp.concatenate(
                [high[core][part] for core in (0, 1)], axis=0
            ).astype(bf16)
        low, high = shared.cores(differs, step, FILM_SHARED, 48)
        both = [middle(low[core], high[core], 48, 96) for core in (0, 1)]
        for index in (0, 1):
            part = slice(48 * index, 48 * index + 48)
            film_ref[rows, index * C + 128 : index * C + 256] = jnp.concatenate(
                [both[core][part] for core in (0, 1)], axis=0
            ).astype(bf16)


def place_attention(shared, in_ref, out_ref):
    for differs, step, chip in shared.chips():
        rows = pl.ds(aligned(chip * 48, 16), 48)
        low, high = shared.cores(differs, step, IN_AT, 72)
        near, far = shared.cores(differs, step, IN_SHARED, 40)
        both = [middle(near[core], far[core], 40, 72) for core in (0, 1)]
        for index in range(3):
            part = slice(24 * index, 24 * index + 24)
            for tile, source in ((0, low), (1, both), (2, high)):
                in_ref[rows, index * C + 128 * tile : index * C + 128 * tile + 128] = (
                    jnp.concatenate([source[core][part] for core in (0, 1)], axis=0)
                )
        low, high = shared.cores(differs, step, OUT_AT, 24)
        near, far = shared.cores(differs, step, OUT_SHARED, 16)
        both = [middle(near[core], far[core], 16, 24) for core in (0, 1)]
        for tile, source in ((0, low), (1, both), (2, high)):
            out_ref[rows, 128 * tile : 128 * tile + 128] = jnp.concatenate(source, axis=0)


def spread_heads(block):
    one, two, three = block[:, 0:128], block[:, 128:256], block[:, 256:384]
    place = lane(block.shape[0])

    def cut(value):
        return jnp.where(place < HEAD, value, 0.0)

    return jnp.concatenate(
        (
            cut(one),
            cut(jnp.where(place < 32, pltpu.roll(one, 32, 1), pltpu.roll(two, 32, 1))),
            cut(jnp.where(place < 64, pltpu.roll(two, 64, 1), pltpu.roll(three, 64, 1))),
            cut(pltpu.roll(three, 96, 1)),
        ),
        axis=1,
    )


def join_heads(block):
    one, two = block[:, 0:128], pltpu.roll(block[:, 128:256], HEAD, 1)
    return jnp.concatenate((jnp.where(lane(block.shape[0]) < HEAD, one, two), two), axis=1)


def first_norm(at, own_ref, other_ref, mask_ref, vec_ref, turned_ref, taps_ref, stat_ref, rows_ref, raw_ref):
    narrow = at[0]
    own = own_ref[...].astype(f32)
    other = other_ref[...].astype(f32)
    low = jnp.where(narrow == 0, own, other)
    high = jnp.where(narrow == 0, other, own)
    for index in range(PIX // 128):
        here = slice(128 * index, 128 * index + 128)
        block = jnp.concatenate((low[:, here], high[:, here]), axis=0).T
        raw_ref[here, :] = block
        turned_ref[here, :] = block.astype(bf16)
    mean, inverse, tally = norm_stats(raw_ref, mask_ref)
    keep_stats(stat_ref, mean, inverse, tally)
    gain, shift = vec_ref[0:1, :], vec_ref[1:2, :]

    def apply(start, carry):
        valid = wide_mask(mask_ref, start, CHUNK)
        normed = (raw_ref[pl.ds(start, CHUNK), :] - mean) * inverse
        value = (normed * gain + shift) * valid
        rows_ref[pl.ds(start + 8, CHUNK), :] = value * lax.logistic(value)
        return carry

    chunks(apply, 0)
    write_taps(rows_ref, taps_ref)


def conv_then_stats(taps_ref, kernel_ref, mask_ref, vec_ref, out_ref, stat_ref):
    bias = vec_ref[2:3, :]

    def done(start, count, acc):
        out_ref[pl.ds(start, count), :] = acc + bias

    convolve(taps_ref, kernel_ref, done)
    keep_stats(stat_ref, *norm_stats(out_ref, mask_ref))


def first_conv(at, taps_ref, mask_ref, vec_ref, *refs):
    whole = Gathered(at, refs[0:8])
    shared = Gathered(at, refs[8:16])
    out_ref, kernel_ref, stat_ref = refs[16:]
    place_conv(whole, shared, 0, kernel_ref)
    conv_then_stats(taps_ref, kernel_ref, mask_ref, vec_ref, out_ref, stat_ref)


def first_conv_plain(at, taps_ref, mask_ref, vec_ref, kernel_ref, out_ref, stat_ref):
    conv_then_stats(taps_ref, kernel_ref, mask_ref, vec_ref, out_ref, stat_ref)


def film_to_third_norm(
    one_ref, stat_two_ref, turned_ref, mask_ref, vec_ref, embed_ref, kernel_ref, film_ref,
    taps_ref, residual_ref, hidden_ref, stat_ref, film_rows_ref, soft_ref, rows_ref,
):
    embed = embed_ref[...].astype(f32)
    soft = (embed * lax.logistic(embed)).astype(bf16)
    soft_ref[...] = jnp.broadcast_to(soft.astype(f32), soft_ref.shape)
    rounded = soft_ref[...].astype(bf16)
    scale = 1.0 + (
        jnp.dot(rounded, film_ref[:, 0:C], preferred_element_type=f32)[0:1] + vec_ref[11:12, :]
    )
    shift = jnp.dot(rounded, film_ref[:, C : 2 * C], preferred_element_type=f32)[0:1] + vec_ref[12:13, :]
    film_rows_ref[0:1, :] = scale
    film_rows_ref[1:2, :] = shift
    mean, inverse = stat_two_ref[0:1, :], stat_two_ref[1:2, :]
    gain_two, shift_two = vec_ref[3:4, :], vec_ref[4:5, :]

    def modulate(start, carry):
        valid = wide_mask(mask_ref, start, CHUNK)
        normed = (one_ref[pl.ds(start, CHUNK), :] - mean) * inverse
        value = (normed * gain_two + shift_two) * valid * scale + shift
        rows_ref[pl.ds(start + 8, CHUNK), :] = value * lax.logistic(value) * valid
        return carry

    chunks(modulate, 0)
    write_taps(rows_ref, taps_ref)
    bias = vec_ref[5:6, :]

    def done(start, count, acc):
        here = pl.ds(start, count)
        valid = wide_mask(mask_ref, start, count)
        residual_ref[here, :] = (turned_ref[here, :].astype(f32) + (acc + bias)) * valid

    convolve(taps_ref, kernel_ref, done)
    mean, inverse, tally = norm_stats(residual_ref, mask_ref)
    keep_stats(stat_ref, mean, inverse, tally)
    gain, shift_three = vec_ref[6:7, :], vec_ref[7:8, :]

    def apply(start, carry):
        valid = wide_mask(mask_ref, start, CHUNK)
        normed = (residual_ref[pl.ds(start, CHUNK), :] - mean) * inverse
        hidden_ref[pl.ds(start, CHUNK), :] = ((normed * gain + shift_three) * valid).astype(bf16)
        return carry

    chunks(apply, 0)


def second_conv(at, one_ref, stat_two_ref, turned_ref, mask_ref, vec_ref, embed_ref, *refs):
    whole = Gathered(at, refs[0:8])
    shared = Gathered(at, refs[8:16])
    taps_ref, residual_ref, hidden_ref, stat_ref, film_rows_ref, kernel_ref = refs[16:22]
    soft_ref, rows_ref, film_ref = refs[22:]
    place_film(whole, shared, film_ref)
    place_conv(whole, shared, 0, kernel_ref)
    film_to_third_norm(
        one_ref, stat_two_ref, turned_ref, mask_ref, vec_ref, embed_ref, kernel_ref, film_ref,
        taps_ref, residual_ref, hidden_ref, stat_ref, film_rows_ref, soft_ref, rows_ref,
    )


def second_conv_plain(
    at, one_ref, stat_two_ref, turned_ref, mask_ref, vec_ref, embed_ref, kernel_ref, film_ref,
    taps_ref, residual_ref, hidden_ref, stat_ref, film_rows_ref, soft_ref, rows_ref,
):
    film_to_third_norm(
        one_ref, stat_two_ref, turned_ref, mask_ref, vec_ref, embed_ref, kernel_ref, film_ref,
        taps_ref, residual_ref, hidden_ref, stat_ref, film_rows_ref, soft_ref, rows_ref,
    )


QUERY = 256


def attention_both(q_ref, k_ref, v_ref, up_ref, out_ref, dq_ref, dk_ref, dv_ref, dk_acc, dv_acc):
    place = lane(QUERY)
    for head in range(HEADS):
        columns = slice(128 * head, 128 * head + 128)
        dk_acc[...] = jnp.zeros_like(dk_acc)
        dv_acc[...] = jnp.zeros_like(dv_acc)

        def block(index, carry):
            rows = pl.ds(aligned(index * QUERY, QUERY), QUERY)
            queries, keys, values = q_ref[rows, columns], k_ref[:, columns], v_ref[:, columns]
            scores = lax.dot_general(queries, keys, ON_LAST, preferred_element_type=f32)
            highest = jnp.max(scores, axis=1, keepdims=True)
            raised = jnp.exp2((scores - highest) * exponent_scale)
            raised_low = raised.astype(bf16)
            mixture = jnp.dot(raised_low, values, preferred_element_type=f32)
            inverse = 1.0 / mixture[:, HEAD : HEAD + 1]
            mixture = mixture * inverse
            out_ref[rows, columns] = mixture.astype(bf16)
            up = (up_ref[rows, columns].astype(f32) * inverse).astype(bf16)
            wide_up = up.astype(f32)
            both = jnp.sum(wide_up * mixture, axis=1, keepdims=True)
            coarse = both.astype(bf16).astype(f32)
            wide_up = jnp.where(place == HEAD, -coarse, wide_up)
            wide_up = jnp.where(place == HEAD + 1, coarse - both, wide_up)
            slopes = lax.dot_general(
                wide_up.astype(bf16), values, ON_LAST, preferred_element_type=f32
            )
            slopes = (raised * slopes).astype(bf16)
            dq_ref[rows, columns] = (
                jnp.dot(slopes, keys, preferred_element_type=f32) * score_scale
            ).astype(bf16)
            dk_acc[...] += lax.dot_general(slopes, queries, ON_FIRST, preferred_element_type=f32)
            dv_acc[...] += lax.dot_general(raised_low, up, ON_FIRST, preferred_element_type=f32)
            return carry

        lax.fori_loop(0, PIX // QUERY, block, 0, unroll=True)
        dk_ref[:, columns] = (dk_acc[...] * score_scale).astype(bf16)
        dv_ref[:, columns] = dv_acc[...].astype(bf16)


def attention_body(
    at, hidden_ref, residual_ref, stat_ref, mask_ref, vec_ref, own_ref, other_ref,
    out_ref, direct_ref, taps_ref, back_ref, vec_grad_ref, in_nat, out_nat,
    in_ref, weight_ref, q_ref, k_ref, v_ref, up_ref, mix_ref, dq_ref, dk_ref, dv_ref,
    dk_acc, dv_acc, cot_ref, rows_ref, turn_ref, own_cot,
):
    narrow = at[0]
    for index in range(3):
        in_ref[:, 512 * index : 512 * index + 512] = spread_heads(
            in_nat[:, C * index : C * index + C]
        ).astype(bf16)
    blank = jnp.zeros((32, C), bf16)
    for head in range(HEADS):
        weight_ref[128 * head : 128 * head + HEAD, :] = out_nat[HEAD * head : HEAD * head + HEAD, :].astype(bf16)
        weight_ref[128 * head + HEAD : 128 * head + 128, :] = blank
    own = own_ref[...].astype(f32)
    other = other_ref[...].astype(f32)
    low = jnp.where(narrow == 0, own, other)
    high = jnp.where(narrow == 0, other, own)
    zero = jnp.zeros((8, C), f32)
    bias_out = zero
    for index in range(PIX // 128):
        here = slice(128 * index, 128 * index + 128)
        block = jnp.concatenate((low[:, here], high[:, here]), axis=0).T
        rows_ref[pl.ds(8 + 128 * index, 128), :] = block
        part = block * wide_mask(mask_ref, 128 * index, 128)
        bias_out = bias_out + fold(part)
        cot_ref[here, :] = part.astype(bf16)
        own_cot[here, :] = own_half(part, narrow).astype(bf16)
    bias_q = spread_heads(jnp.broadcast_to(vec_ref[8:9, :], (8, C)))[0:1]
    bias_v = spread_heads(jnp.broadcast_to(vec_ref[9:10, :], (8, C)))[0:1]
    block_rows = 256
    spare = lax.broadcasted_iota(jnp.int32, (block_rows, 512), 1) & 127
    for index in range(PIX // block_rows):
        here = slice(block_rows * index, block_rows * index + block_rows)
        hidden = hidden_ref[here, :]
        value = jnp.dot(hidden, in_ref[:, 0:512], preferred_element_type=f32) + bias_q
        q_ref[here, :] = jnp.where(spare == HEAD, 1.0, value).astype(bf16)
        value = jnp.dot(hidden, in_ref[:, 512:1024], preferred_element_type=f32)
        valid = mask_ref[here, :]
        barred = jnp.where(valid > 0, 0.0, masked_score)
        barred = jnp.concatenate((barred, barred, barred, barred), axis=1)
        k_ref[here, :] = jnp.where(spare == HEAD, barred, value).astype(bf16)
        value = jnp.dot(hidden, in_ref[:, 1024:1536], preferred_element_type=f32) + bias_v
        v_ref[here, :] = jnp.where((spare == HEAD) | (spare == HEAD + 1), 1.0, value).astype(bf16)
        up_ref[here, :] = lax.dot_general(
            cot_ref[here, :], weight_ref[...], ON_LAST, preferred_element_type=f32
        ).astype(bf16)
    attention_both(q_ref, k_ref, v_ref, up_ref, mix_ref, dq_ref, dk_ref, dv_ref, dk_acc, dv_acc)
    bias = vec_ref[10:11, :]
    for index in range(PIX // 128):
        here = slice(128 * index, 128 * index + 128)
        value = jnp.dot(mix_ref[here, :], weight_ref[...], preferred_element_type=f32) + bias
        valid = wide_mask(mask_ref, 128 * index, 128)
        turn_ref[:, here] = (residual_ref[here, :] + value * valid).T
    out_ref[...] = turn_ref[pl.ds(aligned(narrow * HALF, 16), HALF), :].astype(bf16)
    heads_here = pl.ds(aligned(narrow * 256, 128), 256)
    terms = lax.dot_general(mix_ref[...], own_cot[...], ON_FIRST, preferred_element_type=f32)
    for head in range(HEADS):
        out_nat[HEAD * head : HEAD * head + HEAD, 0:256] = terms[128 * head : 128 * head + HEAD]
    sums = []
    for index, source in enumerate((dq_ref, dk_ref, dv_ref)):
        terms = lax.dot_general(
            hidden_ref[...], source[:, heads_here], ON_FIRST, preferred_element_type=f32
        )
        in_nat[:, 256 * index : 256 * index + 256] = join_heads(terms)
        acc = jnp.zeros((8, 512), f32)
        if index != 1:
            for part in range(PIX // 128):
                acc = acc + fold(source[128 * part : 128 * part + 128, :].astype(f32))
        sums.append(acc)
    mean, inverse, tally = stat_ref[0:1, :], stat_ref[1:2, :], stat_ref[2:3, :]
    gain = vec_ref[6:7, :]
    acc_shift, acc_gain = zero, zero
    for index in range(PIX // 256):
        here = slice(256 * index, 256 * index + 256)
        value = None
        for part, source in enumerate((dq_ref, dk_ref, dv_ref)):
            term = lax.dot_general(
                source[here, :], in_ref[:, 512 * part : 512 * part + 512], ON_LAST,
                preferred_element_type=f32,
            )
            value = term if value is None else value + term
        value = value * wide_mask(mask_ref, 256 * index, 256)
        normed = (residual_ref[here, :] - mean) * inverse
        acc_shift = acc_shift + fold(value)
        acc_gain = acc_gain + fold(value * normed)
        direct_ref[here, :] = value
    shift_grad, gain_grad = total(acc_shift), total(acc_gain)
    first_mean = group_sum(gain * shift_grad) / tally
    second_mean = group_sum(gain * gain_grad) / tally

    def back(start, carry):
        valid = wide_mask(mask_ref, start, CHUNK)
        here = pl.ds(start, CHUNK)
        normed = (residual_ref[here, :] - mean) * inverse
        extra = (direct_ref[here, :] * gain - first_mean - normed * second_mean) * inverse
        value = (rows_ref[pl.ds(start + 8, CHUNK), :] + extra) * valid
        direct_ref[here, :] = value
        low = value.astype(bf16).astype(f32)
        rows_ref[pl.ds(start + 8, CHUNK), :] = low
        return carry + fold(low)

    bias_two = chunks(back, zero)
    write_taps(rows_ref, taps_ref)
    write_own(rows_ref, back_ref, narrow)
    vec_grad_ref[...] = jnp.zeros_like(vec_grad_ref)
    vec_grad_ref[5:6, :] = total(bias_two)
    vec_grad_ref[6:7, :] = gain_grad
    vec_grad_ref[7:8, :] = shift_grad
    for row, acc in ((8, sums[0]), (9, sums[2])):
        pair_one, pair_two = join_heads(acc[:, 0:256]), join_heads(acc[:, 256:512])
        turned = pltpu.roll(pair_two[:, 0:128], 64, 1)
        natural = jnp.concatenate(
            (
                pair_one[:, 0:128],
                jnp.where(lane(8) < 64, pair_one[:, 128:256], turned),
                jnp.where(lane(8) < 64, turned, pltpu.roll(pair_two[:, 128:256], 64, 1)),
            ),
            axis=1,
        )
        vec_grad_ref[row : row + 1, :] = total(natural)
    vec_grad_ref[10:11, :] = total(bias_out)


def unit_rows(grad, chip, core):
    return pl.ds(aligned(chip * 2 * grad + core * grad, 8), grad)


def attention(at, hidden_ref, residual_ref, stat_ref, mask_ref, vec_ref, own_ref, other_ref, *refs):
    shared = Gathered(at, refs[0:8])
    out_ref, direct_ref, taps_ref, back_ref, vec_grad_ref, keep_ref, send_ref = refs[8:15]
    in_nat, out_nat = refs[15:17]
    place_attention(shared, in_nat, out_nat)
    attention_body(
        at, hidden_ref, residual_ref, stat_ref, mask_ref, vec_ref, own_ref, other_ref,
        out_ref, direct_ref, taps_ref, back_ref, vec_grad_ref, *refs[15:],
    )
    for chip in range(8):
        for target, core in ((keep_ref, at[1]), (send_ref, 1 - at[1])):
            rows = unit_rows(24, chip, core)
            block = jnp.concatenate(
                [in_nat[rows, 256 * index : 256 * index + 256] for index in range(3)], axis=0
            )
            target[chip, 0:80, :] = pad_rows(block[:, 0:128], 80).astype(bf16)
            target[chip, 80:128, :] = pad_rows(pair_rows(block[:, 128:256], 40), 48).astype(bf16)
            block = out_nat[rows, 0:256]
            target[chip, 128:160, :] = pad_rows(block[:, 0:128], 32).astype(bf16)
            target[chip, 160:176, :] = pair_rows(block[:, 128:256], 16).astype(bf16)


def attention_plain(
    at, hidden_ref, residual_ref, stat_ref, mask_ref, vec_ref, own_ref, other_ref,
    in_given, out_given, out_ref, direct_ref, taps_ref, back_ref, vec_grad_ref,
    in_term_ref, out_term_ref, *refs,
):
    in_nat, out_nat = refs[0:2]
    in_nat[...] = in_given[...].astype(f32)
    out_nat[...] = out_given[...].astype(f32)
    attention_body(
        at, hidden_ref, residual_ref, stat_ref, mask_ref, vec_ref, own_ref, other_ref,
        out_ref, direct_ref, taps_ref, back_ref, vec_grad_ref, *refs,
    )
    in_term_ref[...] = in_nat[:, 0:768]
    out_term_ref[...] = out_nat[:, 0:256]


def pack_units(terms_ref, at, keep_ref, send_ref):
    for chip in range(8):
        for target, core in ((keep_ref, at[1]), (send_ref, 1 - at[1])):
            rows = unit_rows(ROWS, chip, core)
            target[chip, 0:224, :] = pad_rows(terms_ref[rows, 0:128], 224).astype(bf16)
            target[chip, 224:336, :] = pair_rows(terms_ref[rows, 128:256], 112).astype(bf16)


def conv_terms(at, taps_ref, own_ref, keep_ref, send_ref, terms_ref):
    kernel_terms(taps_ref, own_ref, terms_ref)
    pack_units(terms_ref, at, keep_ref, send_ref)


def conv_terms_plain(at, taps_ref, own_ref, terms_ref):
    kernel_terms(taps_ref, own_ref, terms_ref)


def second_back(
    at, taps_ref, kernel_ref, one_ref, stat_ref, film_rows_ref, mask_ref, vec_ref, vec_in_ref,
    back_taps_ref, back_ref, vec_grad_ref, grad_ref, rows_ref,
):
    def done(start, count, acc):
        grad_ref[pl.ds(start, count), :] = acc

    convolve_back(taps_ref, kernel_ref, done)
    mean, inverse, tally = stat_ref[0:1, :], stat_ref[1:2, :], stat_ref[2:3, :]
    gain, shift = vec_ref[3:4, :], vec_ref[4:5, :]
    scale, offset = film_rows_ref[0:1, :], film_rows_ref[1:2, :]
    zero = jnp.zeros((8, C), f32)

    def gather(start, carry):
        plain, with_normed = carry
        valid = wide_mask(mask_ref, start, CHUNK)
        here = pl.ds(start, CHUNK)
        normed = (one_ref[here, :] - mean) * inverse
        value = grad_ref[here, :] * valid * slope((normed * gain + shift) * valid * scale + offset)
        grad_ref[here, :] = value
        return (plain + fold(value), with_normed + fold(value * normed))

    plain, with_normed = chunks(gather, (zero, zero))
    plain, with_normed = total(plain), total(with_normed)
    gain_grad, shift_grad = scale * with_normed, scale * plain
    first_mean = group_sum(gain * shift_grad) / tally
    second_mean = group_sum(gain * gain_grad) / tally
    joint = scale * gain

    def back(start, carry):
        valid = wide_mask(mask_ref, start, CHUNK)
        here = pl.ds(start, CHUNK)
        normed = (one_ref[here, :] - mean) * inverse
        value = (grad_ref[here, :] * joint - first_mean - normed * second_mean) * inverse * valid
        low = value.astype(bf16).astype(f32)
        rows_ref[pl.ds(start + 8, CHUNK), :] = low
        return carry + fold(low)

    bias = chunks(back, zero)
    write_taps(rows_ref, back_taps_ref)
    write_own(rows_ref, back_ref, at[0])
    vec_grad_ref[...] = vec_in_ref[...]
    vec_grad_ref[2:3, :] = total(bias)
    vec_grad_ref[3:4, :] = gain_grad
    vec_grad_ref[4:5, :] = shift_grad
    vec_grad_ref[11:12, :] = (gain * with_normed + shift * plain).astype(bf16).astype(f32)
    vec_grad_ref[12:13, :] = plain.astype(bf16).astype(f32)


def first_back(
    at, taps_ref, kernel_ref, turned_ref, stat_ref, direct_ref, mask_ref, vec_ref, vec_in_ref,
    out_ref, vec_grad_ref, grad_ref, turn_ref,
):
    def done(start, count, acc):
        grad_ref[pl.ds(start, count), :] = acc

    convolve_back(taps_ref, kernel_ref, done)
    mean, inverse, tally = stat_ref[0:1, :], stat_ref[1:2, :], stat_ref[2:3, :]
    gain, shift = vec_ref[0:1, :], vec_ref[1:2, :]
    zero = jnp.zeros((8, C), f32)

    def gather(start, carry):
        plain, with_normed = carry
        valid = wide_mask(mask_ref, start, CHUNK)
        here = pl.ds(start, CHUNK)
        normed = (turned_ref[here, :].astype(f32) - mean) * inverse
        value = grad_ref[here, :] * slope((normed * gain + shift) * valid) * valid
        grad_ref[here, :] = value
        return (plain + fold(value), with_normed + fold(value * normed))

    plain, with_normed = chunks(gather, (zero, zero))
    shift_grad, gain_grad = total(plain), total(with_normed)
    first_mean = group_sum(gain * shift_grad) / tally
    second_mean = group_sum(gain * gain_grad) / tally
    for index in range(PIX // 128):
        here = slice(128 * index, 128 * index + 128)
        valid = wide_mask(mask_ref, 128 * index, 128)
        normed = (turned_ref[here, :].astype(f32) - mean) * inverse
        value = (grad_ref[here, :] * gain - first_mean - normed * second_mean) * inverse * valid
        turn_ref[:, here] = (value + direct_ref[here, :]).T
    out_ref[...] = turn_ref[pl.ds(aligned(at[0] * HALF, 16), HALF), :].astype(bf16)
    vec_grad_ref[...] = vec_in_ref[...]
    vec_grad_ref[0:1, :] = gain_grad
    vec_grad_ref[1:2, :] = shift_grad


def add_cores(at, keep_ref, back_ref, own_ref, across_ref):
    for depth in range(4):
        for target, side in ((own_ref, at[2]), (across_ref, 1 - at[2])):
            chip = depth * 2 + side
            target[depth] = (keep_ref[chip].astype(f32) + back_ref[chip].astype(f32)).astype(bf16)


def add_sides(at, own_ref, back_ref, mine_ref, *across):
    for step, target in enumerate((mine_ref,) + across):
        depth = at[3] ^ step
        target[...] = (own_ref[depth].astype(f32) + back_ref[depth].astype(f32)).astype(bf16)


def adam_update(weight, gradient, moment, square, step_rate):
    moment_new = beta_one * moment + (1.0 - beta_one) * gradient
    square_new = beta_two * square + (1.0 - beta_two) * gradient * gradient
    ratio = (
        moment_new
        / (1.0 - beta_one**STEP)
        / (jnp.sqrt(square_new / (1.0 - beta_two**STEP)) + adam_eps)
    )
    return (weight - step_rate * (ratio + decay_rate * weight), moment_new, square_new)


def unpair_rows(block, rows):
    top = block.shape[0]
    return jnp.concatenate((block, pltpu.roll(block, 64, 1)[0 : rows - top]), axis=0)


def conv_adam(parts, weight_ref, moment_ref, square_ref, outs, rate):
    def summed(start, stop):
        return sum(part[start:stop, :].astype(f32) for part in parts[1:]) + parts[0][
            start:stop, :
        ].astype(f32)

    low = summed(0, 224)[0:ROWS]
    high = unpair_rows(summed(224, 336), ROWS)
    for columns, gradient in ((slice(0, 128), low), (slice(128, 192), high[:, 0:64])):
        results = adam_update(
            weight_ref[:, columns], gradient, moment_ref[:, columns], square_ref[:, columns], rate
        )
        for out, value in zip(outs, (gradient,) + results):
            out[:, columns] = value
    return summed


def finish_first(at, *refs):
    conv_adam(refs[0:4], *refs[4:7], refs[7:11], step_rates()[0])


def finish_second(at, *refs):
    summed = conv_adam(refs[0:4], *refs[4:7], refs[7:11], step_rates()[1])
    in_ref, out_ref = refs[11:]
    low = summed(336, 416)[0:72]
    high = unpair_rows(summed(416, 464)[0:40], 72)
    for index in range(3):
        part = slice(24 * index, 24 * index + 24)
        in_ref[index, :, 0:128] = low[part]
        in_ref[index, :, 128:192] = high[part, 0:64]
    out_ref[:, 0:128] = summed(464, 496)[0:24]
    out_ref[:, 128:192] = unpair_rows(summed(496, 512), 24)[:, 0:64]


def gather_units(unit, cut, wide):
    core_swap = [(i, i ^ 1) for i in range(wide)]
    side_swap = [(i, i ^ 2) for i in range(wide)]
    flip = [(0, 1), (1, 0)]
    column = [unit] + [
        lax.ppermute(unit, "wide", [(i, i ^ (4 * step)) for i in range(wide)])
        for step in (1, 2, 3)
    ]
    one = jnp.stack([part[:cut] for part in column])
    two = jnp.stack([part[cut:] for part in column])
    side_one, side_two = (lax.ppermute(v, "wide", side_swap) for v in (one, two))
    over_one, over_two = (lax.ppermute(v, "narrow", flip) for v in (one, two))
    far_one = lax.ppermute(over_one, "wide", side_swap)
    far_two = lax.ppermute(side_two, "narrow", flip)
    ones = [one, side_one, over_one, far_one]
    twos = [two, side_two, over_two, far_two]
    ones = ones + [lax.ppermute(v, "wide", core_swap) for v in ones]
    twos = twos + [lax.ppermute(v, "wide", core_swap) for v in twos]
    return ones, twos


def reduce_units(keep, send, scalars, wide):
    rows = keep.shape[1]
    back = lax.ppermute(send, "wide", [(i, i ^ 1) for i in range(wide)])
    four = shaped((4, rows, 128), bf16)
    one = shaped((rows, 128), bf16)
    own, across = call(add_cores, (four, four), (keep, back), scalars)
    back = lax.ppermute(across, "wide", [(i, i ^ 2) for i in range(wide)])
    parts = call(add_sides, (one,) * 4, (own, back), scalars)
    return [parts[0]] + [
        lax.ppermute(parts[step], "wide", [(i, i ^ (4 * step)) for i in range(wide)])
        for step in (1, 2, 3)
    ]


def sum_vectors(terms, wide):
    for step in (1, 2, 4, 8):
        terms = terms + lax.ppermute(terms, "wide", [(i, i ^ step) for i in range(wide)])
    return terms


def per_device(
    features,
    embedding,
    valid_mask,
    cotangent,
    conv_first,
    conv_first_moment,
    conv_first_square,
    conv_second,
    conv_second_moment,
    conv_second_square,
    film_weight,
    film_weight_moment,
    film_weight_square,
    attend_in,
    attend_in_moment,
    attend_in_square,
    attend_out,
    attend_out_moment,
    attend_out_square,
    vectors,
    vectors_moment,
    vectors_square,
):
    wide = lax.axis_size("wide")
    unit_path = wide == 16
    narrow_at = lax.axis_index("narrow").astype(jnp.int32)
    wide_at = lax.axis_index("wide").astype(jnp.int32)
    scalars = jnp.stack((narrow_at, wide_at & 1, (wide_at >> 1) & 1, wide_at >> 2))
    flip = [(0, 1), (1, 0)]
    plane = shaped((PIX, C), f32)
    low_plane = shaped((PIX, C), bf16)
    taps = shaped((PADDED, 3 * C), bf16)
    back_half = shaped((PADDED, 256), bf16)
    kernel = shaped((9 * C, C), bf16)
    stats = shaped((8, C), f32)
    vec_rows = shaped((16, C), f32)
    half_plane = shaped((HALF, PIX), bf16)
    rows_scratch = pltpu.VMEM((PIX + 16, C), f32)

    vec_half = jnp.pad(vectors, ((0, 3), (0, 0)))
    vec_other = lax.ppermute(vec_half, "narrow", flip)
    vecs = jnp.where(
        narrow_at == 0,
        jnp.concatenate((vec_half, vec_other), axis=1),
        jnp.concatenate((vec_other, vec_half), axis=1),
    )
    mask = jnp.broadcast_to(valid_mask[0].astype(f32)[:, None], (PIX, 128))
    own_features = features[0]
    own_cotangent = cotangent[0]
    other_features = lax.ppermute(own_features, "narrow", flip)

    if unit_path:
        (unit_first,) = call(
            pack_first, (shaped((336, 128), bf16),), (conv_first,), scalars
        )
        first_ones, first_twos = gather_units(unit_first, 224, wide)
        (unit_second,) = call(
            pack_second,
            (shaped((SHARED_AT + SECOND_ROWS, 128), bf16),),
            (
                conv_second,
                jnp.transpose(film_weight, (1, 0, 2)),
                jnp.transpose(attend_in, (1, 0, 2)),
                attend_out,
            ),
            scalars,
        )
        second_ones, second_twos = gather_units(unit_second, SHARED_AT, wide)
    else:

        def whole(array, axis):
            array = lax.all_gather(array.astype(bf16), "wide", axis=0, tiled=True)
            return lax.all_gather(array, "narrow", axis=axis, tiled=True)

        first_full, second_full = whole(conv_first, 1), whole(conv_second, 1)
        film_full = whole(film_weight, 2).reshape(EMB, 2 * C)
        in_full = whole(attend_in, 2).reshape(C, 3 * C)
        out_full = whole(attend_out, 1)
    other_cotangent = lax.ppermute(own_cotangent, "narrow", flip)

    turned, taps_one, stat_one = call(
        first_norm,
        (low_plane, taps, stats),
        (own_features, other_features, mask, vecs),
        scalars,
        (rows_scratch, pltpu.VMEM((PIX, C), f32)),
    )
    if unit_path:
        out_one, kernel_one, stat_two = call(
            first_conv,
            (plane, kernel, stats),
            (taps_one, mask, vecs, *first_ones, *first_twos),
            scalars,
            flops=2 * 9 * C * C * PIX,
        )
    else:
        kernel_one = first_full
        out_one, stat_two = call(
            first_conv_plain, (plane, stats), (taps_one, mask, vecs, kernel_one), scalars
        )
    common = (out_one, stat_two, turned, mask, vecs, embedding)
    scratch = (pltpu.VMEM((16, EMB), f32), rows_scratch)
    if unit_path:
        taps_two, residual, hidden, stat_three, film_rows, kernel_two = call(
            second_conv,
            (taps, plane, low_plane, stats, stats, kernel),
            common + (*second_ones, *second_twos),
            scalars,
            scratch + (pltpu.VMEM((EMB, 2 * C), bf16),),
            flops=2 * 9 * C * C * PIX,
        )
    else:
        kernel_two = second_full
        taps_two, residual, hidden, stat_three, film_rows = call(
            second_conv_plain,
            (taps, plane, low_plane, stats, stats),
            common + (kernel_two, film_full),
            scalars,
            scratch,
        )
    common = (hidden, residual, stat_three, mask, vecs, own_cotangent, other_cotangent)
    padded = pltpu.VMEM((PIX, 512), bf16)
    scratch = (
        pltpu.VMEM((C, 3 * C), f32),
        pltpu.VMEM((C, C), f32),
        pltpu.VMEM((C, 1536), bf16),
        pltpu.VMEM((512, C), bf16),
        *([padded] * 8),
        pltpu.VMEM((PIX, 128), f32),
        pltpu.VMEM((PIX, 128), f32),
        pltpu.VMEM((PIX, C), bf16),
        rows_scratch,
        pltpu.VMEM((C, PIX), f32),
        pltpu.VMEM((PIX, 256), bf16),
    )
    flops = 2 * HEADS * PIX * PIX * 128 * 6
    if unit_path:
        units = shaped((8, 176, 128), bf16)
        output, direct, taps_back, back_two, vec_grad, keep_att, send_att = call(
            attention,
            (half_plane, plane, taps, back_half, vec_rows, units, units),
            common + tuple(second_twos),
            scalars,
            scratch,
            flops=flops,
        )
        units = shaped((8, 336, 128), bf16)
        keep, send = call(
            conv_terms,
            (units, units),
            (taps_two, back_two),
            scalars,
            (pltpu.VMEM((9 * C, 256), f32),),
            flops=2 * 9 * C * 256 * PIX,
        )
        parts_second = reduce_units(
            jnp.concatenate((keep, keep_att), axis=1),
            jnp.concatenate((send, send_att), axis=1),
            scalars,
            wide,
        )
    else:
        output, direct, taps_back, back_two, vec_grad, in_term, out_term = call(
            attention_plain,
            (
                half_plane, plane, taps, back_half, vec_rows,
                shaped((C, 768), f32), shaped((C, 256), f32),
            ),
            common + (in_full, out_full),
            scalars,
            scratch,
        )
        (second_term,) = call(
            conv_terms_plain, (shaped((9 * C, 256), f32),), (taps_two, back_two), scalars
        )
    taps_back_one, back_one, vec_grad = call(
        second_back,
        (taps, back_half, vec_rows),
        (taps_back, kernel_two, out_one, stat_two, film_rows, mask, vecs, vec_grad),
        scalars,
        (pltpu.VMEM((PIX, C), f32), rows_scratch),
        flops=2 * 9 * C * C * PIX,
    )
    if unit_path:
        units = shaped((8, 336, 128), bf16)
        keep, send = call(
            conv_terms,
            (units, units),
            (taps_one, back_one),
            scalars,
            (pltpu.VMEM((9 * C, 256), f32),),
            flops=2 * 9 * C * 256 * PIX,
        )
        parts_first = reduce_units(keep, send, scalars, wide)
    else:
        (first_term,) = call(
            conv_terms_plain, (shaped((9 * C, 256), f32),), (taps_one, back_one), scalars
        )
    soft = jax.nn.silu(embedding.astype(f32)).astype(bf16)
    soft_all = lax.all_gather(soft, "wide", axis=0, tiled=True)
    rows_here = film_weight.shape[0]
    soft_here = lax.dynamic_slice_in_dim(soft_all, wide_at * rows_here, rows_here, axis=1)
    film_term = lax.dynamic_slice_in_dim(vec_grad[11:13], narrow_at * HALF, HALF, axis=1)
    film_all = lax.all_gather(film_term.astype(bf16)[None], "wide", axis=0, tiled=True)
    film_gradient = jnp.einsum("se,stj->etj", soft_here, film_all, preferred_element_type=f32)

    input_gradient, vec_grad = call(
        first_back,
        (half_plane, vec_rows),
        (taps_back_one, kernel_one, turned, stat_one, direct, mask, vecs, vec_grad),
        scalars,
        (pltpu.VMEM((PIX, C), f32), pltpu.VMEM((C, PIX), f32)),
        flops=2 * 9 * C * C * PIX,
    )
    vec_half = lax.dynamic_slice_in_dim(vec_grad, narrow_at * HALF, HALF, axis=1)
    if unit_path:
        vec_sum = sum_vectors(vec_half, wide)[:13]
    else:
        vec_sum = lax.psum(vec_half, "wide")[:13]

    rates = step_rates()
    shard = shaped(conv_first.shape, f32)
    if unit_path:
        second_results = call(
            finish_second,
            (shard,) * 4 + (shaped((3, 24, HALF), f32), shaped((24, HALF), f32)),
            (*parts_second, conv_second, conv_second_moment, conv_second_square),
            scalars,
        )
        in_gradient = jnp.transpose(second_results[4], (1, 0, 2))
        out_gradient = second_results[5]
        second_results = second_results[:4]
        first_results = call(
            finish_first,
            (shard,) * 4,
            (*parts_first, conv_first, conv_first_moment, conv_first_square),
            scalars,
        )
    else:

        def scatter(term):
            return lax.psum_scatter(term, "wide", scatter_dimension=0, tiled=True)

        first_gradient = scatter(first_term[:, :HALF])
        second_gradient = scatter(second_term[:, :HALF])
        in_gradient = scatter(in_term.reshape(C, 3, 256)[:, :, :HALF])
        out_gradient = scatter(out_term[:, :HALF])
        first_results = (first_gradient,) + adam_update(
            conv_first, first_gradient, conv_first_moment, conv_first_square, rates[0]
        )
        second_results = (second_gradient,) + adam_update(
            conv_second, second_gradient, conv_second_moment, conv_second_square, rates[1]
        )

    def finish(weight, gradient, moment, square, rate):
        return (gradient,) + adam_update(weight, gradient, moment, square, rate)

    return (
        output[None],
        input_gradient[None],
        *first_results,
        *second_results,
        *finish(film_weight, film_gradient, film_weight_moment, film_weight_square, rates[2]),
        *finish(attend_in, in_gradient, attend_in_moment, attend_in_square, rates[3]),
        *finish(attend_out, out_gradient, attend_out_moment, attend_out_square, rates[4]),
        *finish(vectors, vec_sum, vectors_moment, vectors_square, rates[5]),
    )


def solution(mesh):
    in_specs = (
        P("wide", "narrow", None),
        P("wide", None),
        P("wide", None),
        P("wide", "narrow", None),
        P("wide", "narrow"),
        P("wide", "narrow"),
        P("wide", "narrow"),
        P("wide", "narrow"),
        P("wide", "narrow"),
        P("wide", "narrow"),
        P("wide", None, "narrow"),
        P("wide", None, "narrow"),
        P("wide", None, "narrow"),
        P("wide", None, "narrow"),
        P("wide", None, "narrow"),
        P("wide", None, "narrow"),
        P("wide", "narrow"),
        P("wide", "narrow"),
        P("wide", "narrow"),
        P(None, "narrow"),
        P(None, "narrow"),
        P(None, "narrow"),
    )
    out_specs = (
        P("wide", "narrow", None),
        P("wide", "narrow", None),
        P("wide", "narrow"),
        P("wide", "narrow"),
        P("wide", "narrow"),
        P("wide", "narrow"),
        P("wide", "narrow"),
        P("wide", "narrow"),
        P("wide", "narrow"),
        P("wide", "narrow"),
        P("wide", None, "narrow"),
        P("wide", None, "narrow"),
        P("wide", None, "narrow"),
        P("wide", None, "narrow"),
        P("wide", None, "narrow"),
        P("wide", None, "narrow"),
        P("wide", None, "narrow"),
        P("wide", None, "narrow"),
        P("wide", "narrow"),
        P("wide", "narrow"),
        P("wide", "narrow"),
        P("wide", "narrow"),
        P(None, "narrow"),
        P(None, "narrow"),
        P(None, "narrow"),
        P(None, "narrow"),
    )
    return jax.shard_map(
        per_device, mesh=mesh, in_specs=in_specs, out_specs=out_specs, check_vma=False
    )
```

```python
import jax
import jax.numpy as jnp
from jax import lax
from jax.experimental import pallas as pl
from jax.experimental.pallas import tpu as pltpu
from jax.sharding import PartitionSpec as P

C = 384
HEADS = 4
GROUPS = 32
EMB = 768
SIDE = 32
STEP = 10
PIX = SIDE * SIDE
HALF = C // 2
PADDED = PIX + 2 * SIDE
HEAD = C // HEADS
ROWS = 216
CHUNK = 64

beta_one = 0.9
beta_two = 0.999
adam_eps = 1e-08
decay_rate = 0.01
norm_eps = 1e-05
masked_score = -1e30
score_scale = HEAD ** (-0.5)
exponent_scale = score_scale * 1.4426950408889634

f32 = jnp.float32
bf16 = jnp.bfloat16
ON_LAST = (((1,), (1,)), ((), ()))
ON_FIRST = (((0,), (0,)), ((), ()))
VMEM_BYTES = 45 * 1024 * 1024


def step_rates():
    return (
        2.0 * (9 * C) ** (-0.5),
        2.0 * (9 * C) ** (-0.5),
        2.0 * EMB ** (-0.5),
        2.0 * C ** (-0.5),
        2.0 * (C // 64) ** (-0.5),
        0.5,
    )


def spec():
    return pl.BlockSpec(memory_space=pltpu.VMEM)


def call(body, outs, ins, scalars, scratch=(), far=(), aliases=None, flops=0):
    far = tuple(pltpu.with_memory_space_constraint(v, pltpu.HBM) for v in far)
    ins = tuple(ins) + far
    limit = VMEM_BYTES if body in (middle_of_block, attention_plain) else VMEM_BYTES // 3
    return pl.pallas_call(
        body,
        out_shape=tuple(outs),
        in_specs=[pl.BlockSpec(memory_space=pltpu.SMEM)]
        + [spec() for _ in ins[: len(ins) - len(far)]]
        + [pl.BlockSpec(memory_space=pltpu.HBM) for _ in far],
        out_specs=tuple(spec() for _ in outs),
        scratch_shapes=list(scratch),
        input_output_aliases=aliases or {},
        compiler_params=pltpu.CompilerParams(vmem_limit_bytes=limit),
        cost_estimate=pl.CostEstimate(flops=flops, bytes_accessed=1024, transcendentals=0),
    )(scalars, *ins)


def shaped(shape, kind):
    return jax.ShapeDtypeStruct(shape, kind)


def aligned(value, by):
    return pl.multiple_of(value, by)


def wide_mask(mask_ref, start, count):
    part = mask_ref[pl.ds(start, count), :]
    return jnp.concatenate((part, part, part), axis=1)


def group_sum(row):
    first = (lax.broadcasted_iota(jnp.int32, (C, C), 0) * 5462) >> 16
    second = (lax.broadcasted_iota(jnp.int32, (C, C), 1) * 5462) >> 16
    member = jnp.where(first == second, 1.0, 0.0).astype(f32)
    spread = jnp.broadcast_to(row, (8, C))
    return jnp.dot(
        spread, member, preferred_element_type=f32, precision=lax.Precision.HIGHEST
    )[0:1]


def fold(block):
    return jnp.sum(block.reshape(block.shape[0] // 8, 8, block.shape[1]), axis=0)


def total(acc):
    return jnp.sum(acc, axis=0, keepdims=True)


def chunks(step, init):
    def body(index, carry):
        return step(aligned(index * CHUNK, CHUNK), carry)

    return lax.fori_loop(0, PIX // CHUNK, body, init, unroll=2)


def norm_stats(source_ref, mask_ref):
    zero = jnp.zeros((8, C), f32)

    def first(start, carry):
        sums, count = carry
        valid = wide_mask(mask_ref, start, CHUNK)
        return (sums + fold(source_ref[pl.ds(start, CHUNK), :] * valid), count + fold(valid))

    sums, count = chunks(first, (zero, zero))
    tally = total(count) * float(C // GROUPS)
    mean = group_sum(total(sums)) / tally

    def second(start, carry):
        valid = wide_mask(mask_ref, start, CHUNK)
        centred = source_ref[pl.ds(start, CHUNK), :] - mean
        return carry + fold(centred * centred * valid)

    variance = group_sum(total(chunks(second, zero))) / tally
    return mean, lax.rsqrt(variance + norm_eps), tally


def keep_stats(stat_ref, mean, inverse, tally):
    stat_ref[0:1, :] = mean
    stat_ref[1:2, :] = inverse
    stat_ref[2:3, :] = tally


def column_index(count):
    return lax.broadcasted_iota(jnp.int32, (count, 1), 0) & (SIDE - 1)


def write_taps(rows_ref, taps_ref):
    blank = jnp.zeros((SIDE, 3 * C), bf16)
    taps_ref[0:SIDE, :] = blank
    taps_ref[SIDE + PIX : PADDED, :] = blank
    column = column_index(CHUNK)
    for index in range(PIX // CHUNK):
        start = index * CHUNK
        here = pl.ds(SIDE + start, CHUNK)
        left = rows_ref[pl.ds(7 + start, CHUNK), :]
        right = rows_ref[pl.ds(9 + start, CHUNK), :]
        taps_ref[here, 0:C] = jnp.where(column == 0, 0.0, left).astype(bf16)
        taps_ref[here, C : 2 * C] = rows_ref[pl.ds(8 + start, CHUNK), :].astype(bf16)
        taps_ref[here, 2 * C : 3 * C] = jnp.where(column == SIDE - 1, 0.0, right).astype(bf16)


def lane(count):
    return lax.broadcasted_iota(jnp.int32, (count, 128), 1)


def own_half(block, narrow):
    one, two, three = block[:, 0:128], block[:, 128:256], block[:, 256:384]
    turned_two, turned_three = pltpu.roll(two, 64, 1), pltpu.roll(three, 64, 1)
    upper = jnp.where(lane(block.shape[0]) < 64, turned_two, turned_three)
    return jnp.concatenate(
        (jnp.where(narrow == 0, one, upper), jnp.where(narrow == 0, two, turned_three)), axis=1
    )


def write_own(rows_ref, own_ref, narrow):
    blank = jnp.zeros((SIDE, 256), bf16)
    own_ref[0:SIDE, :] = blank
    own_ref[SIDE + PIX : PADDED, :] = blank
    for index in range(PIX // CHUNK):
        start = index * CHUNK
        block = rows_ref[pl.ds(8 + start, CHUNK), :]
        own_ref[pl.ds(SIDE + start, CHUNK), :] = own_half(block, narrow).astype(bf16)


def convolve(taps_ref, kernel_ref, done, block=512):
    for index in range(PIX // block):
        start = index * block
        acc = None
        for tap in range(3):
            part = jnp.dot(
                taps_ref[pl.ds(start + SIDE * tap, block), :],
                kernel_ref[tap * 3 * C : (tap + 1) * 3 * C, :],
                preferred_element_type=f32,
            )
            acc = part if acc is None else acc + part
        done(start, block, acc)


def convolve_back(taps_ref, kernel_ref, done, block=512):
    for index in range(PIX // block):
        start = index * block
        acc = None
        for tap in range(9):
            tap_row, tap_col = tap // 3, tap % 3
            flipped = 8 - tap
            part = lax.dot_general(
                taps_ref[pl.ds(start + SIDE * tap_row, block), tap_col * C : (tap_col + 1) * C],
                kernel_ref[flipped * C : (flipped + 1) * C, :],
                ON_LAST,
                preferred_element_type=f32,
            )
            acc = part if acc is None else acc + part
        done(start, block, acc)


def kernel_terms(taps_ref, own_ref, terms_ref):
    for tap_col in range(3):
        for tap_row in range(3):
            tap = 3 * tap_row + tap_col
            first = 2 * SIDE - SIDE * tap_row
            terms_ref[tap * C : (tap + 1) * C, :] = lax.dot_general(
                taps_ref[SIDE : SIDE + PIX, tap_col * C : (tap_col + 1) * C],
                own_ref[first : first + PIX, :],
                ON_FIRST,
                preferred_element_type=f32,
            )


def slope(value):
    logistic = lax.logistic(value)
    return logistic * (1.0 + value * (1.0 - logistic))


def tile_parts(block, narrow):
    rows = block.shape[0]
    one = block[:, 0:128]
    two = jnp.concatenate((block[:, 128:192], jnp.zeros((rows, 64), f32)), axis=1)
    turned = jnp.where(lane(rows) < 64, pltpu.roll(one, 64, 1), pltpu.roll(two, 64, 1))
    return jnp.where(narrow == 0, one, turned), jnp.where(narrow == 0, two, one)


def pair_rows(block, top):
    rows = block.shape[0]
    low = block[top:rows]
    if rows < 2 * top:
        low = jnp.concatenate((low, jnp.zeros((2 * top - rows, 128), f32)), axis=0)
    return jnp.where(lane(top) < 64, block[0:top], pltpu.roll(low, 64, 1))


def pad_rows(block, rows):
    if block.shape[0] == rows:
        return block
    return jnp.concatenate((block, jnp.zeros((rows - block.shape[0], block.shape[1]), f32)), axis=0)


def middle(first, second, top, rows):
    one = jnp.where(lane(top) < 64, first, pltpu.roll(second, 64, 1))
    two = jnp.where(lane(top) < 64, pltpu.roll(first, 64, 1), second)
    return jnp.concatenate((one, two[0 : rows - top]), axis=0)


def pack_exchange(at, features_ref, vec_ref, out_ref):
    out_ref[0:HALF, :] = features_ref[...]
    vec = jnp.concatenate((vec_ref[...], jnp.zeros((3, HALF), f32)), axis=0)
    coarse = vec.astype(bf16)
    out_ref[HALF : HALF + 16, :] = jnp.zeros((16, PIX), bf16)
    out_ref[HALF : HALF + 16, 0:HALF] = coarse
    out_ref[HALF : HALF + 16, 256 : 256 + HALF] = (vec - coarse.astype(f32)).astype(bf16)


def pack_first(at, conv_ref, out_ref):
    part, shared = tile_parts(conv_ref[...].T, at[0])
    out_ref[0:224, :] = pad_rows(part, 224).astype(bf16)
    out_ref[224:336, :] = pair_rows(shared, 112).astype(bf16)


FIRST_ROWS = 336
FILM_AT, FILM_SHARED, EMBED_AT, IN_AT, IN_SHARED, OUT_AT, OUT_SHARED, SECOND_ROWS = 336, 432, 480, 496, 576, 624, 656, 672


def stack(at, *refs):
    for step in range(4):
        refs[-1][step] = refs[step][...]


def pass_on(at, *refs):
    pass


def put_rows(out_ref, start, block):
    rows = -(-block.shape[0] // 16) * 16
    out_ref[start : start + rows, :] = pad_rows(block, rows).astype(bf16)


def pack_second(at, conv_ref, film_ref, embed_ref, in_ref, out_weight_ref, out_ref):
    narrow = at[0]
    embed = embed_ref[...].astype(f32)
    put_rows(
        out_ref,
        EMBED_AT,
        jnp.concatenate([embed[:, 128 * i : 128 * i + 128] for i in range(EMB // 128)], axis=0),
    )
    part, shared = tile_parts(conv_ref[...].T, narrow)
    put_rows(out_ref, 0, part)
    put_rows(out_ref, 224, pair_rows(shared, 112))
    part, shared = tile_parts(
        jnp.concatenate((film_ref[:, 0, :], film_ref[:, 1, :]), axis=0), narrow
    )
    put_rows(out_ref, FILM_AT, part)
    put_rows(out_ref, FILM_SHARED, pair_rows(shared, 48))
    part, shared = tile_parts(jnp.concatenate((in_ref[0], in_ref[1], in_ref[2]), axis=0), narrow)
    put_rows(out_ref, IN_AT, part)
    put_rows(out_ref, IN_SHARED, pair_rows(shared, 40))
    part, shared = tile_parts(out_weight_ref[...], narrow)
    put_rows(out_ref, OUT_AT, part)
    put_rows(out_ref, OUT_SHARED, pair_rows(shared, 16))


class Gathered:
    def __init__(self, at, refs, held_ref, sems):
        self.narrow, self.core, self.side, self.depth = at[0], at[1], at[2], at[3]
        self.held = held_ref
        self.copies = {}
        for differs in (0, 1):
            for index in range(differs, 8, 2):
                copy = pltpu.make_async_copy(refs[index], held_ref.at[index], sems.at[index])
                copy.start()
                self.copies[index] = copy

    def part(self, other, differs, across, step):
        return self.held.at[4 * other + 2 * across + differs, step]

    def wait(self, differs):
        for index in range(differs, 8, 2):
            self.copies[index].wait()

    def chips(self):
        for differs in (0, 1):
            for step in range(4):
                yield differs, step, (self.depth ^ step) * 2 + (self.side ^ differs)

    def cores(self, differs, step, start, rows):
        upto = -(-rows // 16) * 16
        found = []
        for across in (0, 1):
            own = self.part(0, differs, across, step)[start : start + upto, :].astype(f32)[0:rows]
            other = self.part(1, differs, across, step)[start : start + upto, :].astype(f32)[0:rows]
            found.append(
                (jnp.where(self.core == 0, own, other), jnp.where(self.core == 0, other, own))
            )
        here, there = found
        return tuple(
            tuple(
                jnp.where((self.narrow == 0) == (tile == 0), here[core], there[core])
                for core in (0, 1)
            )
            for tile in (0, 1)
        )


def place_conv(units, kernel_ref):
    for differs, step, chip in units.chips():
        if step == 0:
            units.wait(differs)
        rows = pl.ds(aligned(chip * (2 * ROWS), 16), 2 * ROWS)
        low, high = units.cores(differs, step, 0, ROWS)
        kernel_ref[rows, 0:128] = jnp.concatenate(low, axis=0).astype(bf16)
        kernel_ref[rows, 256:384] = jnp.concatenate(high, axis=0).astype(bf16)
        low, high = units.cores(differs, step, 224, 112)
        kernel_ref[rows, 128:256] = jnp.concatenate(
            [middle(low[core], high[core], 112, ROWS) for core in (0, 1)], axis=0
        ).astype(bf16)


def place_film(units, film_ref):
    for differs, step, chip in units.chips():
        rows = pl.ds(aligned(chip * 96, 16), 96)
        low, high = units.cores(differs, step, FILM_AT, 96)
        for index in (0, 1):
            part = slice(48 * index, 48 * index + 48)
            film_ref[rows, index * C : index * C + 128] = jnp.concatenate(
                [low[core][part] for core in (0, 1)], axis=0
            ).astype(bf16)
            film_ref[rows, index * C + 256 : index * C + 384] = jnp.concatenate(
                [high[core][part] for core in (0, 1)], axis=0
            ).astype(bf16)
        low, high = units.cores(differs, step, FILM_SHARED, 48)
        both = [middle(low[core], high[core], 48, 96) for core in (0, 1)]
        for index in (0, 1):
            part = slice(48 * index, 48 * index + 48)
            film_ref[rows, index * C + 128 : index * C + 256] = jnp.concatenate(
                [both[core][part] for core in (0, 1)], axis=0
            ).astype(bf16)


def place_embeddings(shared, soft_ref):
    for differs, step, chip in shared.chips():
        for other in (0, 1):
            row = 4 * step + 2 * differs + other
            part = shared.part(other, differs, 0, step)[EMBED_AT : EMBED_AT + 16, :].astype(f32)
            part = (part * lax.logistic(part)).astype(bf16).astype(f32)
            for index in range(EMB // 128):
                soft_ref[row : row + 1, 128 * index : 128 * index + 128] = part[index : index + 1]


def place_attention(units, in_ref, out_ref):
    for differs, step, chip in units.chips():
        rows = pl.ds(aligned(chip * 48, 16), 48)
        low, high = units.cores(differs, step, IN_AT, 72)
        near, far = units.cores(differs, step, IN_SHARED, 40)
        both = [middle(near[core], far[core], 40, 72) for core in (0, 1)]
        for index in range(3):
            part = slice(24 * index, 24 * index + 24)
            for tile, source in ((0, low), (1, both), (2, high)):
                in_ref[rows, index * C + 128 * tile : index * C + 128 * tile + 128] = (
                    jnp.concatenate([source[core][part] for core in (0, 1)], axis=0)
                )
        low, high = units.cores(differs, step, OUT_AT, 24)
        near, far = units.cores(differs, step, OUT_SHARED, 16)
        both = [middle(near[core], far[core], 16, 24) for core in (0, 1)]
        for tile, source in ((0, low), (1, both), (2, high)):
            out_ref[rows, 128 * tile : 128 * tile + 128] = jnp.concatenate(source, axis=0)


def spread_heads(block):
    one, two, three = block[:, 0:128], block[:, 128:256], block[:, 256:384]
    place = lane(block.shape[0])

    def cut(value):
        return jnp.where(place < HEAD, value, 0.0)

    return jnp.concatenate(
        (
            cut(one),
            cut(jnp.where(place < 32, pltpu.roll(one, 32, 1), pltpu.roll(two, 32, 1))),
            cut(jnp.where(place < 64, pltpu.roll(two, 64, 1), pltpu.roll(three, 64, 1))),
            cut(pltpu.roll(three, 96, 1)),
        ),
        axis=1,
    )


def join_heads(block):
    one, two = block[:, 0:128], pltpu.roll(block[:, 128:256], HEAD, 1)
    return jnp.concatenate((jnp.where(lane(block.shape[0]) < HEAD, one, two), two), axis=1)


def first_norm(at, own_ref, other_ref, mask_ref, vec_own_ref, cot_ref, *refs):
    turned_ref, taps_ref, stat_ref, vec_ref, cot_out_ref, rows_ref, raw_ref = refs[-7:]
    narrow = at[0]
    cot_out_ref[...] = cot_ref[...]
    own = vec_own_ref[...]
    other = (
        other_ref[HALF : HALF + 16, 0:HALF].astype(f32)
        + other_ref[HALF : HALF + 16, 256 : 256 + HALF].astype(f32)
    )[0:13]
    vec_ref[0:13, 0:HALF] = jnp.where(narrow == 0, own, other)
    vec_ref[0:13, HALF:C] = jnp.where(narrow == 0, other, own)
    vec_ref[13:16, :] = jnp.zeros((3, C), f32)
    own = own_ref[...].astype(f32)
    other = other_ref[0:HALF, :].astype(f32)
    low = jnp.where(narrow == 0, own, other)
    high = jnp.where(narrow == 0, other, own)
    for index in range(PIX // 128):
        here = slice(128 * index, 128 * index + 128)
        block = jnp.concatenate((low[:, here], high[:, here]), axis=0).T
        raw_ref[here, :] = block
        turned_ref[here, :] = block.astype(bf16)
    mean, inverse, tally = norm_stats(raw_ref, mask_ref)
    keep_stats(stat_ref, mean, inverse, tally)
    gain, shift = vec_ref[0:1, :], vec_ref[1:2, :]

    def apply(start, carry):
        valid = wide_mask(mask_ref, start, CHUNK)
        normed = (raw_ref[pl.ds(start, CHUNK), :] - mean) * inverse
        value = (normed * gain + shift) * valid
        rows_ref[pl.ds(start + 8, CHUNK), :] = value * lax.logistic(value)
        return carry

    chunks(apply, 0)
    write_taps(rows_ref, taps_ref)


def conv_then_stats(taps_ref, kernel_ref, mask_ref, vec_ref, out_ref, stat_ref):
    bias = vec_ref[2:3, :]

    def done(start, count, acc):
        out_ref[pl.ds(start, count), :] = acc + bias

    convolve(taps_ref, kernel_ref, done)
    keep_stats(stat_ref, *norm_stats(out_ref, mask_ref))


def first_conv(at, taps_ref, mask_ref, vec_ref, *refs):
    out_ref, kernel_ref, stat_ref, held_ref, sems = refs[-5:]
    units = Gathered(at, refs[0:8], held_ref, sems)
    place_conv(units, kernel_ref)
    conv_then_stats(taps_ref, kernel_ref, mask_ref, vec_ref, out_ref, stat_ref)


def first_conv_plain(at, taps_ref, mask_ref, vec_ref, kernel_ref, out_ref, stat_ref):
    conv_then_stats(taps_ref, kernel_ref, mask_ref, vec_ref, out_ref, stat_ref)


def film_to_third_norm(
    one_ref, stat_two_ref, turned_ref, mask_ref, vec_ref, embed_ref, kernel_ref, film_ref,
    taps_ref, residual_ref, hidden_ref, stat_ref, film_rows_ref, soft_ref, rows_ref,
):
    embed = embed_ref[...].astype(f32)
    soft = (embed * lax.logistic(embed)).astype(bf16)
    soft_ref[...] = jnp.broadcast_to(soft.astype(f32), soft_ref.shape)
    rounded = soft_ref[...].astype(bf16)
    scale = 1.0 + (
        jnp.dot(rounded, film_ref[:, 0:C], preferred_element_type=f32)[0:1] + vec_ref[11:12, :]
    )
    shift = jnp.dot(rounded, film_ref[:, C : 2 * C], preferred_element_type=f32)[0:1] + vec_ref[12:13, :]
    film_rows_ref[0:1, :] = scale
    film_rows_ref[1:2, :] = shift
    mean, inverse = stat_two_ref[0:1, :], stat_two_ref[1:2, :]
    gain_two, shift_two = vec_ref[3:4, :], vec_ref[4:5, :]

    def modulate(start, carry):
        valid = wide_mask(mask_ref, start, CHUNK)
        normed = (one_ref[pl.ds(start, CHUNK), :] - mean) * inverse
        value = (normed * gain_two + shift_two) * valid * scale + shift
        rows_ref[pl.ds(start + 8, CHUNK), :] = value * lax.logistic(value) * valid
        return carry

    chunks(modulate, 0)
    write_taps(rows_ref, taps_ref)
    bias = vec_ref[5:6, :]

    def done(start, count, acc):
        here = pl.ds(start, count)
        valid = wide_mask(mask_ref, start, count)
        residual_ref[here, :] = (turned_ref[here, :].astype(f32) + (acc + bias)) * valid

    convolve(taps_ref, kernel_ref, done)
    mean, inverse, tally = norm_stats(residual_ref, mask_ref)
    keep_stats(stat_ref, mean, inverse, tally)
    gain, shift_three = vec_ref[6:7, :], vec_ref[7:8, :]

    def apply(start, carry):
        valid = wide_mask(mask_ref, start, CHUNK)
        normed = (residual_ref[pl.ds(start, CHUNK), :] - mean) * inverse
        hidden_ref[pl.ds(start, CHUNK), :] = ((normed * gain + shift_three) * valid).astype(bf16)
        return carry

    chunks(apply, 0)


def second_conv_plain(
    at, one_ref, stat_two_ref, turned_ref, mask_ref, vec_ref, embed_ref, kernel_ref, film_ref,
    taps_ref, residual_ref, hidden_ref, stat_ref, film_rows_ref, soft_ref, rows_ref,
):
    film_to_third_norm(
        one_ref, stat_two_ref, turned_ref, mask_ref, vec_ref, embed_ref, kernel_ref, film_ref,
        taps_ref, residual_ref, hidden_ref, stat_ref, film_rows_ref, soft_ref, rows_ref,
    )


QUERY = 256


def attention_both(q_ref, k_ref, v_ref, kt_ref, vt_ref, upt_ref, outt_ref, dqt_ref, dk_acc, dv_acc):
    place = lax.broadcasted_iota(jnp.int32, (128, QUERY), 0)
    steps = PIX // QUERY

    def where(item):
        head, step = divmod(item, steps)
        return slice(128 * head, 128 * head + 128), slice(step * QUERY, step * QUERY + QUERY), step

    def raise_scores(item):
        columns, rows, _ = where(item)
        scores = lax.dot_general(
            k_ref[:, columns], q_ref[rows, columns], ON_LAST, preferred_element_type=f32
        )
        highest = jnp.max(scores, axis=0, keepdims=True)
        return jnp.exp2((scores - highest) * exponent_scale)

    def score_slopes(item, raised):
        columns, rows, _ = where(item)
        low = raised.astype(bf16)
        mixture = jnp.dot(vt_ref[columns, :], low, preferred_element_type=f32)
        inverse = 1.0 / mixture[HEAD : HEAD + 1, :]
        mixture = mixture * inverse
        outt_ref[columns, rows] = mixture.astype(bf16)
        up = (upt_ref[columns, rows].astype(f32) * inverse).astype(bf16)
        wide_up = up.astype(f32)
        both = jnp.sum(wide_up * mixture, axis=0, keepdims=True)
        coarse = both.astype(bf16).astype(f32)
        wide_up = jnp.where(place == HEAD, -coarse, wide_up)
        wide_up = jnp.where(place == HEAD + 1, coarse - both, wide_up)
        slopes = jnp.dot(v_ref[:, columns], wide_up.astype(bf16), preferred_element_type=f32)
        return low, up, (raised * slopes).astype(bf16)

    def gradients(item, low, up, slopes):
        columns, rows, step = where(item)
        dqt_ref[columns, rows] = (
            jnp.dot(kt_ref[columns, :], slopes, preferred_element_type=f32) * score_scale
        ).astype(bf16)
        dk = jnp.dot(slopes, q_ref[rows, columns], preferred_element_type=f32)
        dv = lax.dot_general(low, up, ON_LAST, preferred_element_type=f32)
        if step == 0:
            dk_acc[...] = dk
            dv_acc[...] = dv
        elif step < steps - 1:
            dk_acc[...] += dk
            dv_acc[...] += dv
        else:
            k_ref[:, columns] = ((dk_acc[...] + dk) * score_scale).astype(bf16)
            v_ref[:, columns] = (dv_acc[...] + dv).astype(bf16)

    count = HEADS * steps
    raised, waiting = raise_scores(0), None
    for item in range(count):
        following = raise_scores(item + 1) if item + 1 < count else None
        found = score_slopes(item, raised)
        if waiting is not None:
            gradients(*waiting)
        waiting = (item, *found)
        raised = following
    gradients(*waiting)


def attention_body(
    at, hidden_ref, residual_ref, stat_ref, mask_ref, vec_ref, own_ref, other_ref,
    out_ref, direct_ref, taps_ref, back_ref, vec_grad_ref, in_nat, out_nat,
    in_ref, weight_ref, q_ref, k_ref, v_ref, kt_ref, vt_ref, upt_ref, mixt_ref, dqt_ref,
    dk_acc, dv_acc, cot_ref, rows_ref, terms_ref, own_cot,
):
    narrow = at[0]
    for index in range(3):
        in_ref[:, 512 * index : 512 * index + 512] = spread_heads(
            in_nat[:, C * index : C * index + C]
        ).astype(bf16)
    blank = jnp.zeros((32, C), bf16)
    for head in range(HEADS):
        weight_ref[128 * head : 128 * head + HEAD, :] = out_nat[HEAD * head : HEAD * head + HEAD, :].astype(bf16)
        weight_ref[128 * head + HEAD : 128 * head + 128, :] = blank
    own = own_ref[...].astype(f32)
    other = other_ref[...].astype(f32)
    low = jnp.where(narrow == 0, own, other)
    high = jnp.where(narrow == 0, other, own)
    zero = jnp.zeros((8, C), f32)
    bias_out = zero
    for index in range(PIX // 128):
        here = slice(128 * index, 128 * index + 128)
        block = jnp.concatenate((low[:, here], high[:, here]), axis=0).T
        rows_ref[pl.ds(8 + 128 * index, 128), :] = block
        part = block * wide_mask(mask_ref, 128 * index, 128)
        bias_out = bias_out + fold(part)
        cot_ref[here, :] = part.astype(bf16)
        own_cot[here, :] = own_half(part, narrow).astype(bf16)
    bias_q = spread_heads(jnp.broadcast_to(vec_ref[8:9, :], (8, C)))[0:1]
    bias_v = spread_heads(jnp.broadcast_to(vec_ref[9:10, :], (8, C)))[0:1]
    block_rows = 256
    spare = lax.broadcasted_iota(jnp.int32, (block_rows, 512), 1) & 127
    for index in range(PIX // block_rows):
        here = slice(block_rows * index, block_rows * index + block_rows)
        hidden = hidden_ref[here, :]
        value = jnp.dot(hidden, in_ref[:, 0:512], preferred_element_type=f32) + bias_q
        q_ref[here, :] = jnp.where(spare == HEAD, 1.0, value).astype(bf16)
        value = jnp.dot(hidden, in_ref[:, 512:1024], preferred_element_type=f32)
        valid = mask_ref[here, :]
        barred = jnp.where(valid > 0, 0.0, masked_score)
        barred = jnp.concatenate((barred, barred, barred, barred), axis=1)
        value = jnp.where(spare == HEAD, barred, value).astype(bf16)
        k_ref[here, :] = value
        kt_ref[:, here] = value.T
        value = jnp.dot(hidden, in_ref[:, 1024:1536], preferred_element_type=f32) + bias_v
        value = jnp.where((spare == HEAD) | (spare == HEAD + 1), 1.0, value).astype(bf16)
        v_ref[here, :] = value
        vt_ref[:, here] = value.T
        upt_ref[:, here] = lax.dot_general(
            weight_ref[...], cot_ref[here, :], ON_LAST, preferred_element_type=f32
        ).astype(bf16)
    attention_both(q_ref, k_ref, v_ref, kt_ref, vt_ref, upt_ref, mixt_ref, dqt_ref, dk_acc, dv_acc)
    dk_ref, dv_ref = k_ref, v_ref
    bias = vec_ref[10:11, :]
    for index in range(PIX // 128):
        here = slice(128 * index, 128 * index + 128)
        value = jnp.dot(mixt_ref[:, here].T, weight_ref[...], preferred_element_type=f32) + bias
        valid = wide_mask(mask_ref, 128 * index, 128)
        quarter, side = divmod(index, 2)
        terms_ref[quarter * C : quarter * C + C, 128 * side : 128 * side + 128] = (
            residual_ref[here, :] + value * valid
        ).T
    for quarter in range(4):
        out_ref[:, 256 * quarter : 256 * quarter + 256] = terms_ref[
            pl.ds(aligned(quarter * C + narrow * HALF, 16), HALF), :
        ].astype(bf16)
    heads_here = pl.ds(aligned(narrow * 256, 128), 256)
    terms = jnp.dot(mixt_ref[...], own_cot[...], preferred_element_type=f32)
    for head in range(HEADS):
        out_nat[HEAD * head : HEAD * head + HEAD, 0:256] = terms[128 * head : 128 * head + HEAD]
    terms = jnp.dot(
        dqt_ref[pl.ds(aligned(narrow * 256, 128), 256), :],
        hidden_ref[...],
        preferred_element_type=f32,
    )
    in_nat[:, 0:256] = join_heads(terms.T)
    for index, source in ((1, dk_ref), (2, dv_ref)):
        terms = lax.dot_general(
            hidden_ref[...], source[:, heads_here], ON_FIRST, preferred_element_type=f32
        )
        in_nat[:, 256 * index : 256 * index + 256] = join_heads(terms)
    ones = jnp.ones((8, PIX), bf16)
    sums = (
        lax.dot_general(ones, dqt_ref[...], ON_LAST, preferred_element_type=f32),
        jnp.dot(ones, dv_ref[...], preferred_element_type=f32),
    )
    mean, inverse, tally = stat_ref[0:1, :], stat_ref[1:2, :], stat_ref[2:3, :]
    gain = vec_ref[6:7, :]
    acc_shift, acc_gain = zero, zero
    for index in range(PIX // 256):
        here = slice(256 * index, 256 * index + 256)
        value = None
        for part, source in enumerate((dqt_ref[:, here].T, dk_ref[here, :], dv_ref[here, :])):
            term = lax.dot_general(
                source, in_ref[:, 512 * part : 512 * part + 512], ON_LAST,
                preferred_element_type=f32,
            )
            value = term if value is None else value + term
        value = value * wide_mask(mask_ref, 256 * index, 256)
        normed = (residual_ref[here, :] - mean) * inverse
        acc_shift = acc_shift + fold(value)
        acc_gain = acc_gain + fold(value * normed)
        direct_ref[here, :] = value
    shift_grad, gain_grad = total(acc_shift), total(acc_gain)
    first_mean = group_sum(gain * shift_grad) / tally
    second_mean = group_sum(gain * gain_grad) / tally

    def back(start, carry):
        valid = wide_mask(mask_ref, start, CHUNK)
        here = pl.ds(start, CHUNK)
        normed = (residual_ref[here, :] - mean) * inverse
        extra = (direct_ref[here, :] * gain - first_mean - normed * second_mean) * inverse
        value = (rows_ref[pl.ds(start + 8, CHUNK), :] + extra) * valid
        direct_ref[here, :] = value
        low = value.astype(bf16).astype(f32)
        rows_ref[pl.ds(start + 8, CHUNK), :] = low
        return carry + fold(low)

    bias_two = chunks(back, zero)
    write_taps(rows_ref, taps_ref)
    write_own(rows_ref, back_ref, narrow)
    vec_grad_ref[...] = jnp.zeros_like(vec_grad_ref)
    vec_grad_ref[5:6, :] = total(bias_two)
    vec_grad_ref[6:7, :] = gain_grad
    vec_grad_ref[7:8, :] = shift_grad
    for row, acc in ((8, sums[0]), (9, sums[1])):
        pair_one, pair_two = join_heads(acc[:, 0:256]), join_heads(acc[:, 256:512])
        turned = pltpu.roll(pair_two[:, 0:128], 64, 1)
        natural = jnp.concatenate(
            (
                pair_one[:, 0:128],
                jnp.where(lane(8) < 64, pair_one[:, 128:256], turned),
                jnp.where(lane(8) < 64, turned, pltpu.roll(pair_two[:, 128:256], 64, 1)),
            ),
            axis=1,
        )
        vec_grad_ref[row : row + 1, :] = natural[0:1]
    vec_grad_ref[10:11, :] = total(bias_out)


def unit_rows(grad, chip, core):
    return pl.ds(aligned(chip * 2 * grad + core * grad, 8), grad)


def middle_of_block(
    at, one_ref, stat_two_ref, turned_ref, mask_ref, vec_ref, embed_ref, own_ref, other_ref, *refs
):
    (
        out_ref, direct_ref, back_taps_ref, vec_grad_ref, film_rows_ref, kernel_ref, soft_all_ref,
        keep_ref, send_ref,
    ) = refs[8:17]
    (
        taps_ref, residual_ref, hidden_ref, stat_ref, soft_ref, film_ref, held_ref, sems, back_ref,
    ) = refs[17:26]
    attention_refs = refs[26:]
    in_nat, out_nat = attention_refs[0:2]
    rows_ref, terms_ref = attention_refs[-3:-1]
    units = Gathered(at, refs[0:8], held_ref, sems)
    place_conv(units, kernel_ref)
    place_film(units, film_ref)
    place_embeddings(units, soft_all_ref)
    film_to_third_norm(
        one_ref, stat_two_ref, turned_ref, mask_ref, vec_ref, embed_ref, kernel_ref, film_ref,
        taps_ref, residual_ref, hidden_ref, stat_ref, film_rows_ref, soft_ref, rows_ref,
    )
    place_attention(units, in_nat, out_nat)
    attention_body(
        at, hidden_ref, residual_ref, stat_ref, mask_ref, vec_ref, own_ref, other_ref,
        out_ref, direct_ref, back_taps_ref, back_ref, vec_grad_ref, *attention_refs,
    )
    for chip in range(8):
        for target, core in ((keep_ref, at[1]), (send_ref, 1 - at[1])):
            rows = unit_rows(24, chip, core)
            block = jnp.concatenate(
                [in_nat[rows, 256 * index : 256 * index + 256] for index in range(3)], axis=0
            )
            target[chip, 336:416, :] = pad_rows(block[:, 0:128], 80).astype(bf16)
            target[chip, 416:464, :] = pad_rows(pair_rows(block[:, 128:256], 40), 48).astype(bf16)
            block = out_nat[rows, 0:256]
            target[chip, 464:496, :] = pad_rows(block[:, 0:128], 32).astype(bf16)
            target[chip, 496:512, :] = pair_rows(block[:, 128:256], 16).astype(bf16)
    kernel_terms(taps_ref, back_ref, terms_ref)
    pack_units(terms_ref, at, keep_ref, send_ref)


def attention_plain(
    at, hidden_ref, residual_ref, stat_ref, mask_ref, vec_ref, own_ref, other_ref,
    in_given, out_given, out_ref, direct_ref, taps_ref, back_ref, vec_grad_ref,
    in_term_ref, out_term_ref, *refs,
):
    in_nat, out_nat = refs[0:2]
    in_nat[...] = in_given[...].astype(f32)
    out_nat[...] = out_given[...].astype(f32)
    attention_body(
        at, hidden_ref, residual_ref, stat_ref, mask_ref, vec_ref, own_ref, other_ref,
        out_ref, direct_ref, taps_ref, back_ref, vec_grad_ref, *refs,
    )
    in_term_ref[...] = in_nat[:, 0:768]
    out_term_ref[...] = out_nat[:, 0:256]


def pack_units(terms_ref, at, keep_ref, send_ref):
    for chip in range(8):
        for target, core in ((keep_ref, at[1]), (send_ref, 1 - at[1])):
            rows = unit_rows(ROWS, chip, core)
            target[chip, 0:224, :] = pad_rows(terms_ref[rows, 0:128], 224).astype(bf16)
            target[chip, 224:336, :] = pair_rows(terms_ref[rows, 128:256], 112).astype(bf16)


def conv_terms_plain(at, taps_ref, own_ref, terms_ref):
    kernel_terms(taps_ref, own_ref, terms_ref)


def second_back(at, *refs):
    taps_one_ref, back_taps_ref, vec_grad_ref, keep_ref, send_ref = refs[8:9] + refs[-8:-4]
    grad_ref, rows_ref, back_ref, terms_ref = refs[-4:]
    second_back_body(at, *refs[:8], back_taps_ref, back_ref, vec_grad_ref, grad_ref, rows_ref)
    kernel_terms(taps_one_ref, back_ref, terms_ref)
    pack_units(terms_ref, at, keep_ref, send_ref)


def second_back_plain(at, *refs):
    second_back_body(at, *refs)


def second_back_body(
    at, taps_ref, kernel_ref, one_ref, stat_ref, film_rows_ref, mask_ref, vec_ref, vec_in_ref,
    back_taps_ref, back_ref, vec_grad_ref, grad_ref, rows_ref,
):
    def done(start, count, acc):
        grad_ref[pl.ds(start, count), :] = acc

    convolve_back(taps_ref, kernel_ref, done)
    mean, inverse, tally = stat_ref[0:1, :], stat_ref[1:2, :], stat_ref[2:3, :]
    gain, shift = vec_ref[3:4, :], vec_ref[4:5, :]
    scale, offset = film_rows_ref[0:1, :], film_rows_ref[1:2, :]
    zero = jnp.zeros((8, C), f32)

    def gather(start, carry):
        plain, with_normed = carry
        valid = wide_mask(mask_ref, start, CHUNK)
        here = pl.ds(start, CHUNK)
        normed = (one_ref[here, :] - mean) * inverse
        value = grad_ref[here, :] * valid * slope((normed * gain + shift) * valid * scale + offset)
        grad_ref[here, :] = value
        return (plain + fold(value), with_normed + fold(value * normed))

    plain, with_normed = chunks(gather, (zero, zero))
    plain, with_normed = total(plain), total(with_normed)
    gain_grad, shift_grad = scale * with_normed, scale * plain
    first_mean = group_sum(gain * shift_grad) / tally
    second_mean = group_sum(gain * gain_grad) / tally
    joint = scale * gain

    def back(start, carry):
        valid = wide_mask(mask_ref, start, CHUNK)
        here = pl.ds(start, CHUNK)
        normed = (one_ref[here, :] - mean) * inverse
        value = (grad_ref[here, :] * joint - first_mean - normed * second_mean) * inverse * valid
        low = value.astype(bf16).astype(f32)
        rows_ref[pl.ds(start + 8, CHUNK), :] = low
        return carry + fold(low)

    bias = chunks(back, zero)
    write_taps(rows_ref, back_taps_ref)
    write_own(rows_ref, back_ref, at[0])
    vec_grad_ref[...] = vec_in_ref[...]
    vec_grad_ref[2:3, :] = total(bias)
    vec_grad_ref[3:4, :] = gain_grad
    vec_grad_ref[4:5, :] = shift_grad
    vec_grad_ref[11:12, :] = (gain * with_normed + shift * plain).astype(bf16).astype(f32)
    vec_grad_ref[12:13, :] = plain.astype(bf16).astype(f32)


def first_back(
    at, taps_ref, kernel_ref, turned_ref, stat_ref, direct_ref, mask_ref, vec_ref, vec_in_ref, *refs,
):
    out_ref, vec_grad_ref, grad_ref, turn_ref = refs[-4:]

    def done(start, count, acc):
        grad_ref[pl.ds(start, count), :] = acc

    convolve_back(taps_ref, kernel_ref, done)
    mean, inverse, tally = stat_ref[0:1, :], stat_ref[1:2, :], stat_ref[2:3, :]
    gain, shift = vec_ref[0:1, :], vec_ref[1:2, :]
    zero = jnp.zeros((8, C), f32)

    def gather(start, carry):
        plain, with_normed = carry
        valid = wide_mask(mask_ref, start, CHUNK)
        here = pl.ds(start, CHUNK)
        normed = (turned_ref[here, :].astype(f32) - mean) * inverse
        value = grad_ref[here, :] * slope((normed * gain + shift) * valid) * valid
        grad_ref[here, :] = value
        return (plain + fold(value), with_normed + fold(value * normed))

    plain, with_normed = chunks(gather, (zero, zero))
    shift_grad, gain_grad = total(plain), total(with_normed)
    first_mean = group_sum(gain * shift_grad) / tally
    second_mean = group_sum(gain * gain_grad) / tally
    for index in range(PIX // 128):
        here = slice(128 * index, 128 * index + 128)
        valid = wide_mask(mask_ref, 128 * index, 128)
        normed = (turned_ref[here, :].astype(f32) - mean) * inverse
        value = (grad_ref[here, :] * gain - first_mean - normed * second_mean) * inverse * valid
        turn_ref[:, here] = (value + direct_ref[here, :]).T
    out_ref[...] = turn_ref[pl.ds(aligned(at[0] * HALF, 16), HALF), :].astype(bf16)
    place = lax.broadcasted_iota(jnp.int32, (16, 1), 0)
    rows = jnp.where(place == 0, gain_grad, jnp.where(place == 1, shift_grad, vec_in_ref[...]))
    vec_grad_ref[...] = own_half(rows, at[0])


def add_cores(at, keep_ref, back_ref, own_ref, across_ref):
    for depth in range(4):
        for target, side in ((own_ref, at[2]), (across_ref, 1 - at[2])):
            chip = depth * 2 + side
            target[depth] = (keep_ref[chip].astype(f32) + back_ref[chip].astype(f32)).astype(bf16)


def add_sides(at, own_ref, back_ref, mine_ref, *across):
    for step, target in enumerate((mine_ref,) + across):
        depth = at[3] ^ step
        target[...] = (own_ref[depth].astype(f32) + back_ref[depth].astype(f32)).astype(bf16)


def adam_update(weight, gradient, moment, square, step_rate):
    moment_new = beta_one * moment + (1.0 - beta_one) * gradient
    square_new = beta_two * square + (1.0 - beta_two) * gradient * gradient
    ratio = (
        moment_new
        / (1.0 - beta_one**STEP)
        / (jnp.sqrt(square_new / (1.0 - beta_two**STEP)) + adam_eps)
    )
    return (weight - step_rate * (ratio + decay_rate * weight), moment_new, square_new)


def unpair_rows(block, rows):
    top = block.shape[0]
    return jnp.concatenate((block, pltpu.roll(block, 64, 1)[0 : rows - top]), axis=0)


def adam_into(gradient, given, outs, rate, where):
    weight, moment, square = (ref[where] for ref in given)
    results = adam_update(weight, gradient, moment, square, rate)
    for out, value in zip(outs, (gradient,) + results):
        out[where] = value


def conv_adam(parts, weight_ref, moment_ref, square_ref, outs, rate):
    def summed(start, stop):
        return sum(part[start:stop, :].astype(f32) for part in parts[1:]) + parts[0][
            start:stop, :
        ].astype(f32)

    low = summed(0, 224)[0:ROWS]
    high = unpair_rows(summed(224, 336), ROWS)
    gradient = jnp.concatenate((low, high[:, 0:64]), axis=1).T
    results = adam_update(weight_ref[...], gradient, moment_ref[...], square_ref[...], rate)
    for out, value in zip(outs, (gradient,) + results):
        out[...] = value
    return summed


def finish_first(at, *refs):
    conv_adam(refs[0:4], *refs[4:7], refs[7:11], step_rates()[0])


def finish_second(at, *refs):
    given, results = refs[4:13], refs[13:]
    summed = conv_adam(refs[0:4], *given[0:3], results[0:4], step_rates()[1])
    gradient = jnp.concatenate(
        (summed(336, 416)[0:72], unpair_rows(summed(416, 464)[0:40], 72)[:, 0:64]), axis=1
    )
    for index in range(3):
        adam_into(
            gradient[24 * index : 24 * index + 24], given[3:6], results[4:8], step_rates()[3], index
        )
    gradient = jnp.concatenate(
        (summed(464, 496)[0:24], unpair_rows(summed(496, 512), 24)[:, 0:64]), axis=1
    )
    adam_into(gradient, given[6:9], results[8:12], step_rates()[4], Ellipsis)


def finish_small(at, own_ref, one_ref, two_ref, three_ref, soft_ref, *refs):
    wide = (at[3] * 2 + at[2]) * 2 + at[1]
    given, results, grad_ref = refs[0:6], refs[6:14], refs[14]
    sums, films = None, []
    for far, ref in enumerate((own_ref, one_ref, two_ref, three_ref)):
        for near in range(4):
            rows = ref[near]
            sums = rows if sums is None else sums + rows
            films.append(jnp.concatenate((rows[11:12], rows[12:13]), axis=1))
    adam_into(sums[0:13, 0:HALF], given[0:3], results[0:4], step_rates()[5], Ellipsis)
    grad_ref[...] = lax.dot_general(
        soft_ref[...].astype(bf16), jnp.concatenate(films, axis=0).astype(bf16), ON_FIRST,
        preferred_element_type=f32,
    )
    here = pl.ds(aligned(wide * 48, 8), 48)
    for index in (0, 1):
        gradient = grad_ref[here, 256 * index : 256 * index + HALF]
        adam_into(
            gradient, given[3:6], results[4:8], step_rates()[2], (slice(None), index, slice(None))
        )


def along_depth(unit, wide):
    return [unit] + [
        lax.ppermute(unit, "wide", [(i, i ^ (4 * step)) for i in range(wide)])
        for step in (1, 2, 3)
    ]


def gather_rest(depth, after, scalars, wide):
    (whole,) = call(stack, (shaped((4, *depth[0].shape), bf16),), depth, scalars, far=after)
    both = ("wide", "narrow")
    diagonal = [(2 * i + x, 2 * (i ^ 2) + 1 - x) for i in range(wide) for x in (0, 1)]
    return [
        whole,
        lax.ppermute(whole, "wide", [(i, i ^ 2) for i in range(wide)]),
        lax.ppermute(whole, "narrow", [(0, 1), (1, 0)]),
        lax.ppermute(whole, both, diagonal),
    ]


def both_cores(parts, wide):
    return list(parts) + [
        lax.ppermute(v, "wide", [(i, i ^ 1) for i in range(wide)]) for v in parts
    ]


def tie(values, after, scalars):
    ins = [pltpu.with_memory_space_constraint(v, pltpu.HBM) for v in (*values, *after)]
    return pl.pallas_call(
        pass_on,
        out_shape=tuple(shaped(v.shape, v.dtype) for v in values),
        in_specs=[pl.BlockSpec(memory_space=pltpu.SMEM)]
        + [pl.BlockSpec(memory_space=pltpu.HBM) for _ in ins],
        out_specs=tuple(pl.BlockSpec(memory_space=pltpu.HBM) for _ in values),
        input_output_aliases={index + 1: index for index in range(len(values))},
    )(scalars, *ins)


def add_core_units(keep, send, scalars, wide):
    back = lax.ppermute(send, "wide", [(i, i ^ 1) for i in range(wide)])
    four = shaped((4, keep.shape[1], 128), bf16)
    return call(add_cores, (four, four), (keep, back), scalars)


def add_far_units(own, across, scalars, wide):
    back = lax.ppermute(across, "wide", [(i, i ^ 2) for i in range(wide)])
    one = shaped((own.shape[1], 128), bf16)
    parts = call(add_sides, (one,) * 4, (own, back), scalars)
    return [parts[0]] + [
        lax.ppermute(parts[step], "wide", [(i, i ^ (4 * step)) for i in range(wide)])
        for step in (1, 2, 3)
    ]


def gather_vectors(rows, wide):
    rows = jnp.stack((rows, lax.ppermute(rows, "wide", [(i, i ^ 1) for i in range(wide)])))
    rows = jnp.concatenate((rows, lax.ppermute(rows, "wide", [(i, i ^ 2) for i in range(wide)])))
    return along_depth(rows, wide)


def per_device(
    features,
    embedding,
    valid_mask,
    cotangent,
    conv_first,
    conv_first_moment,
    conv_first_square,
    conv_second,
    conv_second_moment,
    conv_second_square,
    film_weight,
    film_weight_moment,
    film_weight_square,
    attend_in,
    attend_in_moment,
    attend_in_square,
    attend_out,
    attend_out_moment,
    attend_out_square,
    vectors,
    vectors_moment,
    vectors_square,
):
    wide = lax.axis_size("wide")
    unit_path = wide == 16
    narrow_at = lax.axis_index("narrow").astype(jnp.int32)
    wide_at = lax.axis_index("wide").astype(jnp.int32)
    scalars = jnp.stack((narrow_at, wide_at & 1, (wide_at >> 1) & 1, wide_at >> 2))
    flip = [(0, 1), (1, 0)]
    plane = shaped((PIX, C), f32)
    low_plane = shaped((PIX, C), bf16)
    taps = shaped((PADDED, 3 * C), bf16)
    back_half = shaped((PADDED, 256), bf16)
    kernel = shaped((9 * C, C), bf16)
    stats = shaped((8, C), f32)
    vec_rows = shaped((16, C), f32)
    half_plane = shaped((HALF, PIX), bf16)
    rows_scratch = pltpu.VMEM((PIX + 16, C), f32)

    mask = jnp.broadcast_to(valid_mask[0].astype(f32)[:, None], (PIX, 128))
    own_features = features[0]
    own_cotangent = cotangent[0]
    (exchange,) = call(
        pack_exchange, (shaped((HALF + 16, PIX), bf16),), (own_features, vectors), scalars
    )
    other_features = lax.ppermute(exchange, "narrow", flip)

    if unit_path:
        (unit_first,) = call(
            pack_first,
            (shaped((FIRST_ROWS, 128), bf16),),
            (jnp.transpose(conv_first),),
            scalars,
        )
        depth_first = along_depth(unit_first, wide)
        (unit_second,) = call(
            pack_second,
            (shaped((SECOND_ROWS, 128), bf16),),
            (
                jnp.transpose(conv_second),
                film_weight,
                embedding,
                jnp.transpose(attend_in, (1, 0, 2)),
                attend_out,
            ),
            scalars,
        )
        first_units = both_cores(gather_rest(depth_first, (unit_second,), scalars, wide), wide)
    else:

        def whole(array, axis):
            array = lax.all_gather(array.astype(bf16), "wide", axis=0, tiled=True)
            return lax.all_gather(array, "narrow", axis=axis, tiled=True)

        first_full, second_full = whole(conv_first, 1), whole(conv_second, 1)
        film_full = whole(film_weight, 2).reshape(EMB, 2 * C)
        in_full = whole(attend_in, 2).reshape(C, 3 * C)
        out_full = whole(attend_out, 1)

    turned, taps_one, stat_one, vecs, cotangent_copy = call(
        first_norm,
        (low_plane, taps, stats, vec_rows, half_plane),
        (own_features, other_features, mask, vectors, own_cotangent),
        scalars,
        (rows_scratch, pltpu.VMEM((PIX, C), f32)),
        far=(first_units[0],) if unit_path else (),
        flops=4 * 10**9,
    )
    other_cotangent = lax.ppermute(cotangent_copy, "narrow", flip)
    if unit_path:
        (unit_second,) = tie((unit_second,), (first_units[0],), scalars)
        depth_second = along_depth(unit_second, wide)
        second_parts = gather_rest(
            depth_second, (*first_units[1:4], other_cotangent), scalars, wide
        )
        out_one, kernel_one, stat_two = call(
            first_conv,
            (plane, kernel, stats),
            (taps_one, mask, vecs),
            scalars,
            (
                pltpu.VMEM((8, 4, FIRST_ROWS, 128), bf16),
                pltpu.SemaphoreType.DMA((8,)),
            ),
            far=(*first_units, second_parts[0]),
            flops=10**10,
        )
        second_units = both_cores(
            [second_parts[0], *tie(second_parts[1:4], (stat_two,), scalars)], wide
        )
    else:
        kernel_one = first_full
        out_one, stat_two = call(
            first_conv_plain, (plane, stats), (taps_one, mask, vecs, kernel_one), scalars
        )
    common = (out_one, stat_two, turned, mask, vecs, embedding)
    attention_scratch = (
        pltpu.VMEM((C, 3 * C), f32),
        pltpu.VMEM((C, C), f32),
        pltpu.VMEM((C, 1536), bf16),
        pltpu.VMEM((512, C), bf16),
        *([pltpu.VMEM((PIX, 512), bf16)] * 3),
        *([pltpu.VMEM((512, PIX), bf16)] * 5),
        pltpu.VMEM((PIX, 128), f32),
        pltpu.VMEM((PIX, 128), f32),
        pltpu.VMEM((PIX, C), bf16),
        rows_scratch,
        pltpu.VMEM((9 * C, 256), f32),
        pltpu.VMEM((PIX, 256), bf16),
    )
    back_scratch = (pltpu.VMEM((PIX, C), f32), rows_scratch)
    terms_scratch = (pltpu.VMEM((PADDED, 256), bf16), pltpu.VMEM((9 * C, 256), f32))
    if unit_path:
        units = shaped((8, 512, 128), bf16)
        (
            output, direct, taps_back, vec_grad, film_rows, kernel_two, soft_all, keep, send,
        ) = call(
            middle_of_block,
            (
                half_plane, plane, taps, vec_rows, stats, kernel, shaped((16, EMB), f32),
                units, units,
            ),
            common + (own_cotangent, other_cotangent),
            scalars,
            (
                pltpu.VMEM((PADDED, 3 * C), bf16),
                pltpu.VMEM((PIX, C), f32),
                pltpu.VMEM((PIX, C), bf16),
                pltpu.VMEM((8, C), f32),
                pltpu.VMEM((16, EMB), f32),
                pltpu.VMEM((EMB, 2 * C), bf16),
                pltpu.VMEM((8, 4, SECOND_ROWS, 128), bf16),
                pltpu.SemaphoreType.DMA((8,)),
                pltpu.VMEM((PADDED, 256), bf16),
                *attention_scratch,
            ),
            far=second_units,
            flops=4 * 10**10,
        )
        own_second, across_second = add_core_units(keep, send, scalars, wide)
        units = shaped((8, 336, 128), bf16)
        taps_back_one, vec_grad, keep, send = call(
            second_back,
            (taps, vec_rows, units, units),
            (
                taps_back, kernel_two, out_one, stat_two, film_rows, mask, vecs, vec_grad,
                taps_one,
            ),
            scalars,
            back_scratch + terms_scratch,
            far=(across_second,),
            flops=10**10,
        )
        own_first, across_first = add_core_units(keep, send, scalars, wide)
        parts_second = add_far_units(own_second, across_second, scalars, wide)
        parts_first = add_far_units(own_first, across_first, scalars, wide)
        started = (across_first,)
    else:
        kernel_two = second_full
        taps_two, residual, hidden, stat_three, film_rows = call(
            second_conv_plain,
            (taps, plane, low_plane, stats, stats),
            common + (kernel_two, film_full),
            scalars,
            (pltpu.VMEM((16, EMB), f32), rows_scratch),
        )
        output, direct, taps_back, back_two, vec_grad, in_term, out_term = call(
            attention_plain,
            (
                half_plane, plane, taps, back_half, vec_rows,
                shaped((C, 768), f32), shaped((C, 256), f32),
            ),
            (
                hidden, residual, stat_three, mask, vecs, own_cotangent, other_cotangent,
                in_full, out_full,
            ),
            scalars,
            attention_scratch,
        )
        (second_term,) = call(
            conv_terms_plain, (shaped((9 * C, 256), f32),), (taps_two, back_two), scalars
        )
        taps_back_one, back_one, vec_grad = call(
            second_back_plain,
            (taps, back_half, vec_rows),
            (taps_back, kernel_two, out_one, stat_two, film_rows, mask, vecs, vec_grad),
            scalars,
            back_scratch,
        )
        (first_term,) = call(
            conv_terms_plain, (shaped((9 * C, 256), f32),), (taps_one, back_one), scalars
        )
        started = ()
    input_gradient, vec_half = call(
        first_back,
        (half_plane, shaped((16, 256), f32)),
        (taps_back_one, kernel_one, turned, stat_one, direct, mask, vecs, vec_grad),
        scalars,
        (pltpu.VMEM((PIX, C), f32), pltpu.VMEM((C, PIX), f32)),
        far=started,
        flops=10**10,
    )
    if unit_path:
        vec_shape, film_shape = shaped((13, HALF), f32), shaped(film_weight.shape, f32)
        small = call(
            finish_small,
            (vec_shape,) * 4 + (film_shape,) * 4,
            (
                *gather_vectors(vec_half, wide),
                soft_all,
                vectors,
                vectors_moment,
                vectors_square,
                film_weight,
                film_weight_moment,
                film_weight_square,
            ),
            scalars,
            (pltpu.VMEM((EMB, 512), f32),),
        )
        vec_results, film_results = small[:4], small[4:]
    else:
        vec_half = vec_half[:13, :HALF]
        vec_sum = lax.psum(vec_half, "wide")
        soft = jax.nn.silu(embedding.astype(f32)).astype(bf16)
        soft_all = lax.all_gather(soft, "wide", axis=0, tiled=True)
        rows_here = film_weight.shape[0]
        soft_here = lax.dynamic_slice_in_dim(soft_all, wide_at * rows_here, rows_here, axis=1)
        film_all = lax.all_gather(vec_half[11:13].astype(bf16)[None], "wide", axis=0, tiled=True)
        film_gradient = jnp.einsum("se,stj->etj", soft_here, film_all, preferred_element_type=f32)

    rates = step_rates()
    shard = shaped((HALF, ROWS), f32)

    def turned_shards(*shards):
        return tuple(jnp.transpose(v) for v in shards)

    if unit_path:
        in_shape, out_shape = shaped((3, 24, HALF), f32), shaped((24, HALF), f32)
        in_given = tuple(
            jnp.transpose(v, (1, 0, 2)) for v in (attend_in, attend_in_moment, attend_in_square)
        )
        second_results = call(
            finish_second,
            (shard,) * 4 + (in_shape,) * 4 + (out_shape,) * 4,
            (
                *parts_second,
                *turned_shards(conv_second, conv_second_moment, conv_second_square),
                *in_given,
                attend_out,
                attend_out_moment,
                attend_out_square,
            ),
            scalars,
        )
        in_results = tuple(jnp.transpose(v, (1, 0, 2)) for v in second_results[4:8])
        out_results = second_results[8:12]
        second_results = turned_shards(*second_results[:4])
        first_results = call(
            finish_first,
            (shard,) * 4,
            (*parts_first, *turned_shards(conv_first, conv_first_moment, conv_first_square)),
            scalars,
        )
        first_results = turned_shards(*first_results)
    else:

        def scatter(term):
            return lax.psum_scatter(term, "wide", scatter_dimension=0, tiled=True)

        first_gradient = scatter(first_term[:, :HALF])
        second_gradient = scatter(second_term[:, :HALF])
        in_gradient = scatter(in_term.reshape(C, 3, 256)[:, :, :HALF])
        out_gradient = scatter(out_term[:, :HALF])

        def finish(weight, gradient, moment, square, rate):
            return (gradient,) + adam_update(weight, gradient, moment, square, rate)

        first_results = finish(
            conv_first, first_gradient, conv_first_moment, conv_first_square, rates[0]
        )
        second_results = finish(
            conv_second, second_gradient, conv_second_moment, conv_second_square, rates[1]
        )
        film_results = finish(
            film_weight, film_gradient, film_weight_moment, film_weight_square, rates[2]
        )
        in_results = finish(
            attend_in, in_gradient, attend_in_moment, attend_in_square, rates[3]
        )
        out_results = finish(
            attend_out, out_gradient, attend_out_moment, attend_out_square, rates[4]
        )
        vec_results = finish(vectors, vec_sum, vectors_moment, vectors_square, rates[5])

    return (
        output[None],
        input_gradient[None],
        *first_results,
        *second_results,
        *film_results,
        *in_results,
        *out_results,
        *vec_results,
    )


def solution(mesh):
    in_specs = (
        P("wide", "narrow", None),
        P("wide", None),
        P("wide", None),
        P("wide", "narrow", None),
        P("wide", "narrow"),
        P("wide", "narrow"),
        P("wide", "narrow"),
        P("wide", "narrow"),
        P("wide", "narrow"),
        P("wide", "narrow"),
        P("wide", None, "narrow"),
        P("wide", None, "narrow"),
        P("wide", None, "narrow"),
        P("wide", None, "narrow"),
        P("wide", None, "narrow"),
        P("wide", None, "narrow"),
        P("wide", "narrow"),
        P("wide", "narrow"),
        P("wide", "narrow"),
        P(None, "narrow"),
        P(None, "narrow"),
        P(None, "narrow"),
    )
    out_specs = (
        P("wide", "narrow", None),
        P("wide", "narrow", None),
        P("wide", "narrow"),
        P("wide", "narrow"),
        P("wide", "narrow"),
        P("wide", "narrow"),
        P("wide", "narrow"),
        P("wide", "narrow"),
        P("wide", "narrow"),
        P("wide", "narrow"),
        P("wide", None, "narrow"),
        P("wide", None, "narrow"),
        P("wide", None, "narrow"),
        P("wide", None, "narrow"),
        P("wide", None, "narrow"),
        P("wide", None, "narrow"),
        P("wide", None, "narrow"),
        P("wide", None, "narrow"),
        P("wide", "narrow"),
        P("wide", "narrow"),
        P("wide", "narrow"),
        P("wide", "narrow"),
        P(None, "narrow"),
        P(None, "narrow"),
        P(None, "narrow"),
        P(None, "narrow"),
    )
    return jax.shard_map(
        per_device, mesh=mesh, in_specs=in_specs, out_specs=out_specs, check_vma=False
    )
```

```python
import jax
import jax.numpy as jnp
from jax import lax
from jax.experimental import pallas as pl
from jax.experimental.pallas import tpu as pltpu
from jax.sharding import PartitionSpec as P

C = 384
HEADS = 4
GROUPS = 32
EMB = 768
SIDE = 32
STEP = 10
PIX = SIDE * SIDE
HALF = C // 2
PADDED = PIX + 2 * SIDE
HEAD = C // HEADS
ROWS = 216
CHUNK = 64

beta_one = 0.9
beta_two = 0.999
adam_eps = 1e-08
decay_rate = 0.01
norm_eps = 1e-05
masked_score = -1e30
score_scale = HEAD ** (-0.5)
exponent_scale = score_scale * 1.4426950408889634

f32 = jnp.float32
bf16 = jnp.bfloat16
ON_LAST = (((1,), (1,)), ((), ()))
ON_FIRST = (((0,), (0,)), ((), ()))
VMEM_BYTES = 45 * 1024 * 1024


def step_rates():
    return (
        2.0 * (9 * C) ** (-0.5),
        2.0 * (9 * C) ** (-0.5),
        2.0 * EMB ** (-0.5),
        2.0 * C ** (-0.5),
        2.0 * (C // 64) ** (-0.5),
        0.5,
    )


def spec():
    return pl.BlockSpec(memory_space=pltpu.VMEM)


def call(body, outs, ins, scalars, scratch=(), far=(), aliases=None, flops=0):
    far = tuple(pltpu.with_memory_space_constraint(v, pltpu.HBM) for v in far)
    ins = tuple(ins) + far
    limit = VMEM_BYTES if body in (middle_of_block, attention_plain) else VMEM_BYTES // 3
    return pl.pallas_call(
        body,
        out_shape=tuple(outs),
        in_specs=[pl.BlockSpec(memory_space=pltpu.SMEM)]
        + [spec() for _ in ins[: len(ins) - len(far)]]
        + [pl.BlockSpec(memory_space=pltpu.HBM) for _ in far],
        out_specs=tuple(spec() for _ in outs),
        scratch_shapes=list(scratch),
        input_output_aliases=aliases or {},
        compiler_params=pltpu.CompilerParams(vmem_limit_bytes=limit),
        cost_estimate=pl.CostEstimate(flops=flops, bytes_accessed=1024, transcendentals=0),
    )(scalars, *ins)


def shaped(shape, kind):
    return jax.ShapeDtypeStruct(shape, kind)


def aligned(value, by):
    return pl.multiple_of(value, by)


def wide_mask(mask_ref, start, count):
    part = mask_ref[pl.ds(start, count), :]
    return jnp.concatenate((part, part, part), axis=1)


def group_sum(row):
    first = (lax.broadcasted_iota(jnp.int32, (C, C), 0) * 5462) >> 16
    second = (lax.broadcasted_iota(jnp.int32, (C, C), 1) * 5462) >> 16
    member = jnp.where(first == second, 1.0, 0.0).astype(f32)
    spread = jnp.broadcast_to(row, (8, C))
    return jnp.dot(
        spread, member, preferred_element_type=f32, precision=lax.Precision.HIGHEST
    )[0:1]


def fold(block):
    return jnp.sum(block.reshape(block.shape[0] // 8, 8, block.shape[1]), axis=0)


def total(acc):
    return jnp.sum(acc, axis=0, keepdims=True)


def chunks(step, init):
    def body(index, carry):
        return step(aligned(index * CHUNK, CHUNK), carry)

    return lax.fori_loop(0, PIX // CHUNK, body, init, unroll=2)


def norm_stats(source_ref, mask_ref):
    zero = jnp.zeros((8, C), f32)

    def first(start, carry):
        sums, count = carry
        valid = wide_mask(mask_ref, start, CHUNK)
        return (sums + fold(source_ref[pl.ds(start, CHUNK), :] * valid), count + fold(valid))

    sums, count = chunks(first, (zero, zero))
    tally = total(count) * float(C // GROUPS)
    mean = group_sum(total(sums)) / tally

    def second(start, carry):
        valid = wide_mask(mask_ref, start, CHUNK)
        centred = source_ref[pl.ds(start, CHUNK), :] - mean
        return carry + fold(centred * centred * valid)

    variance = group_sum(total(chunks(second, zero))) / tally
    return mean, lax.rsqrt(variance + norm_eps), tally


def keep_stats(stat_ref, mean, inverse, tally):
    stat_ref[0:1, :] = mean
    stat_ref[1:2, :] = inverse
    stat_ref[2:3, :] = tally


def column_index(count):
    return lax.broadcasted_iota(jnp.int32, (count, 1), 0) & (SIDE - 1)


def write_taps(rows_ref, taps_ref):
    blank = jnp.zeros((SIDE, 3 * C), bf16)
    taps_ref[0:SIDE, :] = blank
    taps_ref[SIDE + PIX : PADDED, :] = blank
    column = column_index(CHUNK)
    for index in range(PIX // CHUNK):
        start = index * CHUNK
        here = pl.ds(SIDE + start, CHUNK)
        left = rows_ref[pl.ds(7 + start, CHUNK), :]
        right = rows_ref[pl.ds(9 + start, CHUNK), :]
        taps_ref[here, 0:C] = jnp.where(column == 0, 0.0, left).astype(bf16)
        taps_ref[here, C : 2 * C] = rows_ref[pl.ds(8 + start, CHUNK), :].astype(bf16)
        taps_ref[here, 2 * C : 3 * C] = jnp.where(column == SIDE - 1, 0.0, right).astype(bf16)


def lane(count):
    return lax.broadcasted_iota(jnp.int32, (count, 128), 1)


def own_half(block, narrow):
    one, two, three = block[:, 0:128], block[:, 128:256], block[:, 256:384]
    turned_two, turned_three = pltpu.roll(two, 64, 1), pltpu.roll(three, 64, 1)
    upper = jnp.where(lane(block.shape[0]) < 64, turned_two, turned_three)
    return jnp.concatenate(
        (jnp.where(narrow == 0, one, upper), jnp.where(narrow == 0, two, turned_three)), axis=1
    )


def write_own(rows_ref, own_ref, narrow):
    blank = jnp.zeros((SIDE, 256), bf16)
    own_ref[0:SIDE, :] = blank
    own_ref[SIDE + PIX : PADDED, :] = blank
    for index in range(PIX // CHUNK):
        start = index * CHUNK
        block = rows_ref[pl.ds(8 + start, CHUNK), :]
        own_ref[pl.ds(SIDE + start, CHUNK), :] = own_half(block, narrow).astype(bf16)


def convolve(taps_ref, kernel_ref, done, block=512):
    for index in range(PIX // block):
        start = index * block
        acc = None
        for tap in range(3):
            part = jnp.dot(
                taps_ref[pl.ds(start + SIDE * tap, block), :],
                kernel_ref[tap * 3 * C : (tap + 1) * 3 * C, :],
                preferred_element_type=f32,
            )
            acc = part if acc is None else acc + part
        done(start, block, acc)


def convolve_back(taps_ref, kernel_ref, done, block=512):
    for index in range(PIX // block):
        start = index * block
        acc = None
        for tap in range(9):
            tap_row, tap_col = tap // 3, tap % 3
            flipped = 8 - tap
            part = lax.dot_general(
                taps_ref[pl.ds(start + SIDE * tap_row, block), tap_col * C : (tap_col + 1) * C],
                kernel_ref[flipped * C : (flipped + 1) * C, :],
                ON_LAST,
                preferred_element_type=f32,
            )
            acc = part if acc is None else acc + part
        done(start, block, acc)


def kernel_terms(taps_ref, own_ref, terms_ref):
    for tap_col in range(3):
        for tap_row in range(3):
            tap = 3 * tap_row + tap_col
            first = 2 * SIDE - SIDE * tap_row
            terms_ref[tap * C : (tap + 1) * C, :] = lax.dot_general(
                taps_ref[SIDE : SIDE + PIX, tap_col * C : (tap_col + 1) * C],
                own_ref[first : first + PIX, :],
                ON_FIRST,
                preferred_element_type=f32,
            )


def slope(value):
    logistic = lax.logistic(value)
    return logistic * (1.0 + value * (1.0 - logistic))


def tile_parts(block, narrow):
    rows = block.shape[0]
    one = block[:, 0:128]
    two = jnp.concatenate((block[:, 128:192], jnp.zeros((rows, 64), f32)), axis=1)
    turned = jnp.where(lane(rows) < 64, pltpu.roll(one, 64, 1), pltpu.roll(two, 64, 1))
    return jnp.where(narrow == 0, one, turned), jnp.where(narrow == 0, two, one)


def pair_rows(block, top):
    rows = block.shape[0]
    low = block[top:rows]
    if rows < 2 * top:
        low = jnp.concatenate((low, jnp.zeros((2 * top - rows, 128), f32)), axis=0)
    return jnp.where(lane(top) < 64, block[0:top], pltpu.roll(low, 64, 1))


def pad_rows(block, rows):
    if block.shape[0] == rows:
        return block
    return jnp.concatenate((block, jnp.zeros((rows - block.shape[0], block.shape[1]), f32)), axis=0)


def middle(first, second, top, rows):
    one = jnp.where(lane(top) < 64, first, pltpu.roll(second, 64, 1))
    two = jnp.where(lane(top) < 64, pltpu.roll(first, 64, 1), second)
    return jnp.concatenate((one, two[0 : rows - top]), axis=0)


def pack_exchange(at, features_ref, vec_ref, cot_ref, out_ref):
    out_ref[HALF + 16 : 2 * HALF + 16, :] = cot_ref[...]
    out_ref[0:HALF, :] = features_ref[...]
    vec = jnp.concatenate((vec_ref[...], jnp.zeros((3, HALF), f32)), axis=0)
    coarse = vec.astype(bf16)
    out_ref[HALF : HALF + 16, :] = jnp.zeros((16, PIX), bf16)
    out_ref[HALF : HALF + 16, 0:HALF] = coarse
    out_ref[HALF : HALF + 16, 256 : 256 + HALF] = (vec - coarse.astype(f32)).astype(bf16)


FIRST_ROWS = 336
FILM_AT, FILM_SHARED, EMBED_AT, IN_AT, IN_SHARED, OUT_AT, OUT_SHARED, SECOND_ROWS = 336, 432, 480, 496, 576, 624, 656, 672


def stack_all(at, *refs):
    first_ref, second_ref = refs[4:6]
    for step in range(4):
        first_ref[step] = refs[step][0:FIRST_ROWS, :]
        second_ref[step] = refs[step][FIRST_ROWS : FIRST_ROWS + SECOND_ROWS, :]


def pass_on(at, *refs):
    pass


def put_rows(out_ref, start, block):
    rows = -(-block.shape[0] // 16) * 16
    out_ref[start : start + rows, :] = pad_rows(block, rows).astype(bf16)


def pack_weights(at, embed_ref, *refs):
    unit_ref, first_ref, second_ref, film_ref, in_ref, out_ref, sems = refs[5:]
    narrow = at[0]
    copies = [
        pltpu.make_async_copy(source, target, sems.at[index])
        for index, (source, target) in enumerate(
            zip(refs[0:5], (first_ref, second_ref, film_ref, in_ref, out_ref))
        )
    ]
    for copy in copies:
        copy.start()
    embed = embed_ref[...].astype(f32)
    put_rows(
        unit_ref,
        FIRST_ROWS + EMBED_AT,
        jnp.concatenate([embed[:, 128 * i : 128 * i + 128] for i in range(EMB // 128)], axis=0),
    )
    copies[0].wait()
    part, shared = tile_parts(first_ref[...].T, narrow)
    put_rows(unit_ref, 0, part)
    put_rows(unit_ref, 224, pair_rows(shared, 112))
    for copy in copies[1:]:
        copy.wait()
    for block, start, shared_start, top in (
        (second_ref[...].T, 0, 224, 112),
        (
            jnp.concatenate((film_ref[:, 0, :], film_ref[:, 1, :]), axis=0),
            FILM_AT, FILM_SHARED, 48,
        ),
        (jnp.concatenate((in_ref[0], in_ref[1], in_ref[2]), axis=0), IN_AT, IN_SHARED, 40),
        (out_ref[...], OUT_AT, OUT_SHARED, 16),
    ):
        part, shared = tile_parts(block, narrow)
        put_rows(unit_ref, FIRST_ROWS + start, part)
        put_rows(unit_ref, FIRST_ROWS + shared_start, pair_rows(shared, top))


class Gathered:
    def __init__(self, at, refs, held_ref, sems):
        self.narrow, self.core, self.side, self.depth = at[0], at[1], at[2], at[3]
        self.held = held_ref
        self.copies = {}
        for differs in (0, 1):
            for index in range(differs, 8, 2):
                copy = pltpu.make_async_copy(refs[index], held_ref.at[index], sems.at[index])
                copy.start()
                self.copies[index] = copy

    def part(self, other, differs, across, step):
        return self.held.at[4 * other + 2 * across + differs, step]

    def wait(self, differs):
        for index in range(differs, 8, 2):
            self.copies[index].wait()

    def chips(self):
        for differs in (0, 1):
            for step in range(4):
                yield differs, step, (self.depth ^ step) * 2 + (self.side ^ differs)

    def cores(self, differs, step, start, rows):
        upto = -(-rows // 16) * 16
        found = []
        for across in (0, 1):
            own = self.part(0, differs, across, step)[start : start + upto, :].astype(f32)[0:rows]
            other = self.part(1, differs, across, step)[start : start + upto, :].astype(f32)[0:rows]
            found.append(
                (jnp.where(self.core == 0, own, other), jnp.where(self.core == 0, other, own))
            )
        here, there = found
        return tuple(
            tuple(
                jnp.where((self.narrow == 0) == (tile == 0), here[core], there[core])
                for core in (0, 1)
            )
            for tile in (0, 1)
        )


def place_conv(units, kernel_ref):
    for differs, step, chip in units.chips():
        if step == 0:
            units.wait(differs)
        rows = pl.ds(aligned(chip * (2 * ROWS), 16), 2 * ROWS)
        low, high = units.cores(differs, step, 0, ROWS)
        kernel_ref[rows, 0:128] = jnp.concatenate(low, axis=0).astype(bf16)
        kernel_ref[rows, 256:384] = jnp.concatenate(high, axis=0).astype(bf16)
        low, high = units.cores(differs, step, 224, 112)
        kernel_ref[rows, 128:256] = jnp.concatenate(
            [middle(low[core], high[core], 112, ROWS) for core in (0, 1)], axis=0
        ).astype(bf16)


def place_film(units, film_ref):
    for differs, step, chip in units.chips():
        rows = pl.ds(aligned(chip * 96, 16), 96)
        low, high = units.cores(differs, step, FILM_AT, 96)
        for index in (0, 1):
            part = slice(48 * index, 48 * index + 48)
            film_ref[rows, index * C : index * C + 128] = jnp.concatenate(
                [low[core][part] for core in (0, 1)], axis=0
            ).astype(bf16)
            film_ref[rows, index * C + 256 : index * C + 384] = jnp.concatenate(
                [high[core][part] for core in (0, 1)], axis=0
            ).astype(bf16)
        low, high = units.cores(differs, step, FILM_SHARED, 48)
        both = [middle(low[core], high[core], 48, 96) for core in (0, 1)]
        for index in (0, 1):
            part = slice(48 * index, 48 * index + 48)
            film_ref[rows, index * C + 128 : index * C + 256] = jnp.concatenate(
                [both[core][part] for core in (0, 1)], axis=0
            ).astype(bf16)


def place_embeddings(shared, soft_ref):
    for differs, step, chip in shared.chips():
        for other in (0, 1):
            row = 4 * step + 2 * differs + other
            part = shared.part(other, differs, 0, step)[EMBED_AT : EMBED_AT + 16, :].astype(f32)
            part = (part * lax.logistic(part)).astype(bf16).astype(f32)
            for index in range(EMB // 128):
                soft_ref[row : row + 1, 128 * index : 128 * index + 128] = part[index : index + 1]


def place_attention(units, in_ref, out_ref):
    for differs, step, chip in units.chips():
        rows = pl.ds(aligned(chip * 48, 16), 48)
        low, high = units.cores(differs, step, IN_AT, 72)
        near, far = units.cores(differs, step, IN_SHARED, 40)
        both = [middle(near[core], far[core], 40, 72) for core in (0, 1)]
        for index in range(3):
            part = slice(24 * index, 24 * index + 24)
            for tile, source in ((0, low), (1, both), (2, high)):
                in_ref[rows, index * C + 128 * tile : index * C + 128 * tile + 128] = (
                    jnp.concatenate([source[core][part] for core in (0, 1)], axis=0)
                )
        low, high = units.cores(differs, step, OUT_AT, 24)
        near, far = units.cores(differs, step, OUT_SHARED, 16)
        both = [middle(near[core], far[core], 16, 24) for core in (0, 1)]
        for tile, source in ((0, low), (1, both), (2, high)):
            out_ref[rows, 128 * tile : 128 * tile + 128] = jnp.concatenate(source, axis=0)


def spread_heads(block):
    one, two, three = block[:, 0:128], block[:, 128:256], block[:, 256:384]
    place = lane(block.shape[0])

    def cut(value):
        return jnp.where(place < HEAD, value, 0.0)

    return jnp.concatenate(
        (
            cut(one),
            cut(jnp.where(place < 32, pltpu.roll(one, 32, 1), pltpu.roll(two, 32, 1))),
            cut(jnp.where(place < 64, pltpu.roll(two, 64, 1), pltpu.roll(three, 64, 1))),
            cut(pltpu.roll(three, 96, 1)),
        ),
        axis=1,
    )


def join_heads(block):
    one, two = block[:, 0:128], pltpu.roll(block[:, 128:256], HEAD, 1)
    return jnp.concatenate((jnp.where(lane(block.shape[0]) < HEAD, one, two), two), axis=1)


def first_norm(at, own_ref, other_ref, mask_ref, vec_own_ref, *refs):
    turned_ref, taps_ref, stat_ref, vec_ref, rows_ref, raw_ref = refs[-6:]
    narrow = at[0]
    own = vec_own_ref[...]
    other = (
        other_ref[HALF : HALF + 16, 0:HALF].astype(f32)
        + other_ref[HALF : HALF + 16, 256 : 256 + HALF].astype(f32)
    )[0:13]
    vec_ref[0:13, 0:HALF] = jnp.where(narrow == 0, own, other)
    vec_ref[0:13, HALF:C] = jnp.where(narrow == 0, other, own)
    vec_ref[13:16, :] = jnp.zeros((3, C), f32)
    own = own_ref[...].astype(f32)
    other = other_ref[0:HALF, :].astype(f32)
    low = jnp.where(narrow == 0, own, other)
    high = jnp.where(narrow == 0, other, own)
    for index in range(PIX // 128):
        here = slice(128 * index, 128 * index + 128)
        block = jnp.concatenate((low[:, here], high[:, here]), axis=0).T
        raw_ref[here, :] = block
        turned_ref[here, :] = block.astype(bf16)
    mean, inverse, tally = norm_stats(raw_ref, mask_ref)
    keep_stats(stat_ref, mean, inverse, tally)
    gain, shift = vec_ref[0:1, :], vec_ref[1:2, :]

    def apply(start, carry):
        valid = wide_mask(mask_ref, start, CHUNK)
        normed = (raw_ref[pl.ds(start, CHUNK), :] - mean) * inverse
        value = (normed * gain + shift) * valid
        rows_ref[pl.ds(start + 8, CHUNK), :] = value * lax.logistic(value)
        return carry

    chunks(apply, 0)
    write_taps(rows_ref, taps_ref)


def conv_then_stats(taps_ref, kernel_ref, mask_ref, vec_ref, out_ref, stat_ref):
    bias = vec_ref[2:3, :]

    def done(start, count, acc):
        out_ref[pl.ds(start, count), :] = acc + bias

    convolve(taps_ref, kernel_ref, done)
    keep_stats(stat_ref, *norm_stats(out_ref, mask_ref))


def first_conv(at, taps_ref, mask_ref, vec_ref, *refs):
    out_ref, kernel_ref, stat_ref, held_ref, sems = refs[-5:]
    units = Gathered(at, refs[0:8], held_ref, sems)
    place_conv(units, kernel_ref)
    conv_then_stats(taps_ref, kernel_ref, mask_ref, vec_ref, out_ref, stat_ref)


def first_conv_plain(at, taps_ref, mask_ref, vec_ref, kernel_ref, out_ref, stat_ref):
    conv_then_stats(taps_ref, kernel_ref, mask_ref, vec_ref, out_ref, stat_ref)


def film_to_third_norm(
    one_ref, stat_two_ref, turned_ref, mask_ref, vec_ref, embed_ref, kernel_ref, film_ref,
    taps_ref, residual_ref, hidden_ref, stat_ref, film_rows_ref, soft_ref, rows_ref,
):
    embed = embed_ref[...].astype(f32)
    soft = (embed * lax.logistic(embed)).astype(bf16)
    soft_ref[...] = jnp.broadcast_to(soft.astype(f32), soft_ref.shape)
    rounded = soft_ref[...].astype(bf16)
    scale = 1.0 + (
        jnp.dot(rounded, film_ref[:, 0:C], preferred_element_type=f32)[0:1] + vec_ref[11:12, :]
    )
    shift = jnp.dot(rounded, film_ref[:, C : 2 * C], preferred_element_type=f32)[0:1] + vec_ref[12:13, :]
    film_rows_ref[0:1, :] = scale
    film_rows_ref[1:2, :] = shift
    mean, inverse = stat_two_ref[0:1, :], stat_two_ref[1:2, :]
    gain_two, shift_two = vec_ref[3:4, :], vec_ref[4:5, :]

    def modulate(start, carry):
        valid = wide_mask(mask_ref, start, CHUNK)
        normed = (one_ref[pl.ds(start, CHUNK), :] - mean) * inverse
        value = (normed * gain_two + shift_two) * valid * scale + shift
        rows_ref[pl.ds(start + 8, CHUNK), :] = value * lax.logistic(value) * valid
        return carry

    chunks(modulate, 0)
    write_taps(rows_ref, taps_ref)
    bias = vec_ref[5:6, :]

    def done(start, count, acc):
        here = pl.ds(start, count)
        valid = wide_mask(mask_ref, start, count)
        residual_ref[here, :] = (turned_ref[here, :].astype(f32) + (acc + bias)) * valid

    convolve(taps_ref, kernel_ref, done)
    mean, inverse, tally = norm_stats(residual_ref, mask_ref)
    keep_stats(stat_ref, mean, inverse, tally)
    gain, shift_three = vec_ref[6:7, :], vec_ref[7:8, :]

    def apply(start, carry):
        valid = wide_mask(mask_ref, start, CHUNK)
        normed = (residual_ref[pl.ds(start, CHUNK), :] - mean) * inverse
        hidden_ref[pl.ds(start, CHUNK), :] = ((normed * gain + shift_three) * valid).astype(bf16)
        return carry

    chunks(apply, 0)


def second_conv_plain(
    at, one_ref, stat_two_ref, turned_ref, mask_ref, vec_ref, embed_ref, kernel_ref, film_ref,
    taps_ref, residual_ref, hidden_ref, stat_ref, film_rows_ref, soft_ref, rows_ref,
):
    film_to_third_norm(
        one_ref, stat_two_ref, turned_ref, mask_ref, vec_ref, embed_ref, kernel_ref, film_ref,
        taps_ref, residual_ref, hidden_ref, stat_ref, film_rows_ref, soft_ref, rows_ref,
    )


QUERY = 256


def attention_both(q_ref, k_ref, v_ref, kt_ref, vt_ref, upt_ref, outt_ref, dqt_ref, dk_acc, dv_acc):
    place = lax.broadcasted_iota(jnp.int32, (128, QUERY), 0)
    steps = PIX // QUERY

    def where(item):
        head, step = divmod(item, steps)
        return slice(128 * head, 128 * head + 128), slice(step * QUERY, step * QUERY + QUERY), step

    def raise_scores(item):
        columns, rows, _ = where(item)
        scores = lax.dot_general(
            k_ref[:, columns], q_ref[rows, columns], ON_LAST, preferred_element_type=f32
        )
        highest = jnp.max(scores, axis=0, keepdims=True)
        return jnp.exp2((scores - highest) * exponent_scale)

    def score_slopes(item, raised):
        columns, rows, _ = where(item)
        low = raised.astype(bf16)
        mixture = jnp.dot(vt_ref[columns, :], low, preferred_element_type=f32)
        inverse = 1.0 / mixture[HEAD : HEAD + 1, :]
        mixture = mixture * inverse
        outt_ref[columns, rows] = mixture.astype(bf16)
        up = (upt_ref[columns, rows].astype(f32) * inverse).astype(bf16)
        wide_up = up.astype(f32)
        both = jnp.sum(wide_up * mixture, axis=0, keepdims=True)
        coarse = both.astype(bf16).astype(f32)
        wide_up = jnp.where(place == HEAD, -coarse, wide_up)
        wide_up = jnp.where(place == HEAD + 1, coarse - both, wide_up)
        slopes = jnp.dot(v_ref[:, columns], wide_up.astype(bf16), preferred_element_type=f32)
        return low, up, (raised * slopes).astype(bf16)

    def gradients(item, low, up, slopes):
        columns, rows, step = where(item)
        dqt_ref[columns, rows] = (
            jnp.dot(kt_ref[columns, :], slopes, preferred_element_type=f32) * score_scale
        ).astype(bf16)
        dk = jnp.dot(slopes, q_ref[rows, columns], preferred_element_type=f32)
        dv = lax.dot_general(low, up, ON_LAST, preferred_element_type=f32)
        if step == 0:
            dk_acc[...] = dk
            dv_acc[...] = dv
        elif step < steps - 1:
            dk_acc[...] += dk
            dv_acc[...] += dv
        else:
            k_ref[:, columns] = ((dk_acc[...] + dk) * score_scale).astype(bf16)
            v_ref[:, columns] = (dv_acc[...] + dv).astype(bf16)

    count = HEADS * steps
    raised, waiting = raise_scores(0), None
    for item in range(count):
        following = raise_scores(item + 1) if item + 1 < count else None
        found = score_slopes(item, raised)
        if waiting is not None:
            gradients(*waiting)
        waiting = (item, *found)
        raised = following
    gradients(*waiting)


def attention_body(
    at, hidden_ref, residual_ref, stat_ref, mask_ref, vec_ref, own_ref, other_ref,
    out_ref, direct_ref, taps_ref, back_ref, vec_grad_ref, in_nat, out_nat,
    in_ref, weight_ref, q_ref, k_ref, v_ref, kt_ref, vt_ref, upt_ref, mixt_ref, dqt_ref,
    dk_acc, dv_acc, cot_ref, rows_ref, terms_ref, own_cot,
):
    narrow = at[0]
    for index in range(3):
        in_ref[:, 512 * index : 512 * index + 512] = spread_heads(
            in_nat[:, C * index : C * index + C]
        ).astype(bf16)
    blank = jnp.zeros((32, C), bf16)
    for head in range(HEADS):
        weight_ref[128 * head : 128 * head + HEAD, :] = out_nat[HEAD * head : HEAD * head + HEAD, :].astype(bf16)
        weight_ref[128 * head + HEAD : 128 * head + 128, :] = blank
    own = own_ref[...].astype(f32)
    other = other_ref[HALF + 16 : 2 * HALF + 16, :].astype(f32)
    low = jnp.where(narrow == 0, own, other)
    high = jnp.where(narrow == 0, other, own)
    zero = jnp.zeros((8, C), f32)
    bias_out = zero
    for index in range(PIX // 128):
        here = slice(128 * index, 128 * index + 128)
        block = jnp.concatenate((low[:, here], high[:, here]), axis=0).T
        rows_ref[pl.ds(8 + 128 * index, 128), :] = block
        part = block * wide_mask(mask_ref, 128 * index, 128)
        bias_out = bias_out + fold(part)
        cot_ref[here, :] = part.astype(bf16)
        own_cot[here, :] = own_half(part, narrow).astype(bf16)
    bias_q = spread_heads(jnp.broadcast_to(vec_ref[8:9, :], (8, C)))[0:1]
    bias_v = spread_heads(jnp.broadcast_to(vec_ref[9:10, :], (8, C)))[0:1]
    block_rows = 256
    spare = lax.broadcasted_iota(jnp.int32, (block_rows, 512), 1) & 127
    for index in range(PIX // block_rows):
        here = slice(block_rows * index, block_rows * index + block_rows)
        hidden = hidden_ref[here, :]
        value = jnp.dot(hidden, in_ref[:, 0:512], preferred_element_type=f32) + bias_q
        q_ref[here, :] = jnp.where(spare == HEAD, 1.0, value).astype(bf16)
        value = jnp.dot(hidden, in_ref[:, 512:1024], preferred_element_type=f32)
        valid = mask_ref[here, :]
        barred = jnp.where(valid > 0, 0.0, masked_score)
        barred = jnp.concatenate((barred, barred, barred, barred), axis=1)
        value = jnp.where(spare == HEAD, barred, value).astype(bf16)
        k_ref[here, :] = value
        kt_ref[:, here] = value.T
        value = jnp.dot(hidden, in_ref[:, 1024:1536], preferred_element_type=f32) + bias_v
        value = jnp.where((spare == HEAD) | (spare == HEAD + 1), 1.0, value).astype(bf16)
        v_ref[here, :] = value
        vt_ref[:, here] = value.T
        upt_ref[:, here] = lax.dot_general(
            weight_ref[...], cot_ref[here, :], ON_LAST, preferred_element_type=f32
        ).astype(bf16)
    attention_both(q_ref, k_ref, v_ref, kt_ref, vt_ref, upt_ref, mixt_ref, dqt_ref, dk_acc, dv_acc)
    dk_ref, dv_ref = k_ref, v_ref
    bias = vec_ref[10:11, :]
    for index in range(PIX // 128):
        here = slice(128 * index, 128 * index + 128)
        value = jnp.dot(mixt_ref[:, here].T, weight_ref[...], preferred_element_type=f32) + bias
        valid = wide_mask(mask_ref, 128 * index, 128)
        quarter, side = divmod(index, 2)
        terms_ref[quarter * C : quarter * C + C, 128 * side : 128 * side + 128] = (
            residual_ref[here, :] + value * valid
        ).T
    for quarter in range(4):
        out_ref[:, 256 * quarter : 256 * quarter + 256] = terms_ref[
            pl.ds(aligned(quarter * C + narrow * HALF, 16), HALF), :
        ].astype(bf16)
    heads_here = pl.ds(aligned(narrow * 256, 128), 256)
    terms = jnp.dot(mixt_ref[...], own_cot[...], preferred_element_type=f32)
    for head in range(HEADS):
        out_nat[HEAD * head : HEAD * head + HEAD, 0:256] = terms[128 * head : 128 * head + HEAD]
    terms = jnp.dot(
        dqt_ref[pl.ds(aligned(narrow * 256, 128), 256), :],
        hidden_ref[...],
        preferred_element_type=f32,
    )
    in_nat[:, 0:256] = join_heads(terms.T)
    for index, source in ((1, dk_ref), (2, dv_ref)):
        terms = lax.dot_general(
            hidden_ref[...], source[:, heads_here], ON_FIRST, preferred_element_type=f32
        )
        in_nat[:, 256 * index : 256 * index + 256] = join_heads(terms)
    ones = jnp.ones((8, PIX), bf16)
    sums = (
        lax.dot_general(ones, dqt_ref[...], ON_LAST, preferred_element_type=f32),
        jnp.dot(ones, dv_ref[...], preferred_element_type=f32),
    )
    mean, inverse, tally = stat_ref[0:1, :], stat_ref[1:2, :], stat_ref[2:3, :]
    gain = vec_ref[6:7, :]
    acc_shift, acc_gain = zero, zero
    for index in range(PIX // 256):
        here = slice(256 * index, 256 * index + 256)
        value = None
        for part, source in enumerate((dqt_ref[:, here].T, dk_ref[here, :], dv_ref[here, :])):
            term = lax.dot_general(
                source, in_ref[:, 512 * part : 512 * part + 512], ON_LAST,
                preferred_element_type=f32,
            )
            value = term if value is None else value + term
        value = value * wide_mask(mask_ref, 256 * index, 256)
        normed = (residual_ref[here, :] - mean) * inverse
        acc_shift = acc_shift + fold(value)
        acc_gain = acc_gain + fold(value * normed)
        direct_ref[here, :] = value
    shift_grad, gain_grad = total(acc_shift), total(acc_gain)
    first_mean = group_sum(gain * shift_grad) / tally
    second_mean = group_sum(gain * gain_grad) / tally

    def back(start, carry):
        valid = wide_mask(mask_ref, start, CHUNK)
        here = pl.ds(start, CHUNK)
        normed = (residual_ref[here, :] - mean) * inverse
        extra = (direct_ref[here, :] * gain - first_mean - normed * second_mean) * inverse
        value = (rows_ref[pl.ds(start + 8, CHUNK), :] + extra) * valid
        direct_ref[here, :] = value
        low = value.astype(bf16).astype(f32)
        rows_ref[pl.ds(start + 8, CHUNK), :] = low
        return carry + fold(low)

    bias_two = chunks(back, zero)
    write_taps(rows_ref, taps_ref)
    write_own(rows_ref, back_ref, narrow)
    vec_grad_ref[...] = jnp.zeros_like(vec_grad_ref)
    vec_grad_ref[5:6, :] = total(bias_two)
    vec_grad_ref[6:7, :] = gain_grad
    vec_grad_ref[7:8, :] = shift_grad
    for row, acc in ((8, sums[0]), (9, sums[1])):
        pair_one, pair_two = join_heads(acc[:, 0:256]), join_heads(acc[:, 256:512])
        turned = pltpu.roll(pair_two[:, 0:128], 64, 1)
        natural = jnp.concatenate(
            (
                pair_one[:, 0:128],
                jnp.where(lane(8) < 64, pair_one[:, 128:256], turned),
                jnp.where(lane(8) < 64, turned, pltpu.roll(pair_two[:, 128:256], 64, 1)),
            ),
            axis=1,
        )
        vec_grad_ref[row : row + 1, :] = natural[0:1]
    vec_grad_ref[10:11, :] = total(bias_out)


def unit_rows(grad, chip, core):
    return pl.ds(aligned(chip * 2 * grad + core * grad, 8), grad)


def middle_of_block(
    at, one_ref, stat_two_ref, turned_ref, mask_ref, vec_ref, embed_ref, own_ref, other_ref, *refs
):
    (
        out_ref, direct_ref, back_taps_ref, vec_grad_ref, film_rows_ref, kernel_ref, soft_all_ref,
        keep_ref, send_ref,
    ) = refs[8:17]
    (
        taps_ref, residual_ref, hidden_ref, stat_ref, soft_ref, film_ref, held_ref, sems, back_ref,
    ) = refs[17:26]
    attention_refs = refs[26:]
    in_nat, out_nat = attention_refs[0:2]
    rows_ref, terms_ref = attention_refs[-3:-1]
    units = Gathered(at, refs[0:8], held_ref, sems)
    place_conv(units, kernel_ref)
    place_film(units, film_ref)
    place_embeddings(units, soft_all_ref)
    film_to_third_norm(
        one_ref, stat_two_ref, turned_ref, mask_ref, vec_ref, embed_ref, kernel_ref, film_ref,
        taps_ref, residual_ref, hidden_ref, stat_ref, film_rows_ref, soft_ref, rows_ref,
    )
    place_attention(units, in_nat, out_nat)
    attention_body(
        at, hidden_ref, residual_ref, stat_ref, mask_ref, vec_ref, own_ref, other_ref,
        out_ref, direct_ref, back_taps_ref, back_ref, vec_grad_ref, *attention_refs,
    )
    for chip in range(8):
        for target, core in ((keep_ref, at[1]), (send_ref, 1 - at[1])):
            rows = unit_rows(24, chip, core)
            block = jnp.concatenate(
                [in_nat[rows, 256 * index : 256 * index + 256] for index in range(3)], axis=0
            )
            target[chip, 336:416, :] = pad_rows(block[:, 0:128], 80).astype(bf16)
            target[chip, 416:464, :] = pad_rows(pair_rows(block[:, 128:256], 40), 48).astype(bf16)
            block = out_nat[rows, 0:256]
            target[chip, 464:496, :] = pad_rows(block[:, 0:128], 32).astype(bf16)
            target[chip, 496:512, :] = pair_rows(block[:, 128:256], 16).astype(bf16)
    kernel_terms(taps_ref, back_ref, terms_ref)
    pack_units(terms_ref, at, keep_ref, send_ref)


def attention_plain(
    at, hidden_ref, residual_ref, stat_ref, mask_ref, vec_ref, own_ref, other_ref,
    in_given, out_given, out_ref, direct_ref, taps_ref, back_ref, vec_grad_ref,
    in_term_ref, out_term_ref, *refs,
):
    in_nat, out_nat = refs[0:2]
    in_nat[...] = in_given[...].astype(f32)
    out_nat[...] = out_given[...].astype(f32)
    attention_body(
        at, hidden_ref, residual_ref, stat_ref, mask_ref, vec_ref, own_ref, other_ref,
        out_ref, direct_ref, taps_ref, back_ref, vec_grad_ref, *refs,
    )
    in_term_ref[...] = in_nat[:, 0:768]
    out_term_ref[...] = out_nat[:, 0:256]


def pack_units(terms_ref, at, keep_ref, send_ref):
    for chip in range(8):
        for target, core in ((keep_ref, at[1]), (send_ref, 1 - at[1])):
            rows = unit_rows(ROWS, chip, core)
            target[chip, 0:224, :] = pad_rows(terms_ref[rows, 0:128], 224).astype(bf16)
            target[chip, 224:336, :] = pair_rows(terms_ref[rows, 128:256], 112).astype(bf16)


def conv_terms_plain(at, taps_ref, own_ref, terms_ref):
    kernel_terms(taps_ref, own_ref, terms_ref)


def second_back(at, *refs):
    taps_one_ref = refs[8]
    back_taps_ref, vec_grad_ref, keep_ref, send_ref = refs[-8:-4]
    grad_ref, rows_ref, back_ref, terms_ref = refs[-4:]
    second_back_body(at, *refs[:8], back_taps_ref, back_ref, vec_grad_ref, grad_ref, rows_ref)
    kernel_terms(taps_one_ref, back_ref, terms_ref)
    pack_units(terms_ref, at, keep_ref, send_ref)


def second_back_plain(at, *refs):
    second_back_body(at, *refs)


def second_back_body(
    at, taps_ref, kernel_ref, one_ref, stat_ref, film_rows_ref, mask_ref, vec_ref, vec_in_ref,
    back_taps_ref, back_ref, vec_grad_ref, grad_ref, rows_ref,
):
    def done(start, count, acc):
        grad_ref[pl.ds(start, count), :] = acc

    convolve_back(taps_ref, kernel_ref, done)
    mean, inverse, tally = stat_ref[0:1, :], stat_ref[1:2, :], stat_ref[2:3, :]
    gain, shift = vec_ref[3:4, :], vec_ref[4:5, :]
    scale, offset = film_rows_ref[0:1, :], film_rows_ref[1:2, :]
    zero = jnp.zeros((8, C), f32)

    def gather(start, carry):
        plain, with_normed = carry
        valid = wide_mask(mask_ref, start, CHUNK)
        here = pl.ds(start, CHUNK)
        normed = (one_ref[here, :] - mean) * inverse
        value = grad_ref[here, :] * valid * slope((normed * gain + shift) * valid * scale + offset)
        grad_ref[here, :] = value
        return (plain + fold(value), with_normed + fold(value * normed))

    plain, with_normed = chunks(gather, (zero, zero))
    plain, with_normed = total(plain), total(with_normed)
    gain_grad, shift_grad = scale * with_normed, scale * plain
    first_mean = group_sum(gain * shift_grad) / tally
    second_mean = group_sum(gain * gain_grad) / tally
    joint = scale * gain

    def back(start, carry):
        valid = wide_mask(mask_ref, start, CHUNK)
        here = pl.ds(start, CHUNK)
        normed = (one_ref[here, :] - mean) * inverse
        value = (grad_ref[here, :] * joint - first_mean - normed * second_mean) * inverse * valid
        low = value.astype(bf16).astype(f32)
        rows_ref[pl.ds(start + 8, CHUNK), :] = low
        return carry + fold(low)

    bias = chunks(back, zero)
    write_taps(rows_ref, back_taps_ref)
    write_own(rows_ref, back_ref, at[0])
    vec_grad_ref[...] = vec_in_ref[...]
    vec_grad_ref[2:3, :] = total(bias)
    vec_grad_ref[3:4, :] = gain_grad
    vec_grad_ref[4:5, :] = shift_grad
    vec_grad_ref[11:12, :] = (gain * with_normed + shift * plain).astype(bf16).astype(f32)
    vec_grad_ref[12:13, :] = plain.astype(bf16).astype(f32)


def first_back(
    at, taps_ref, kernel_ref, turned_ref, stat_ref, direct_ref, mask_ref, vec_ref, vec_in_ref, *refs,
):
    out_ref, vec_grad_ref, grad_ref, turn_ref = refs[-4:]

    def done(start, count, acc):
        grad_ref[pl.ds(start, count), :] = acc

    convolve_back(taps_ref, kernel_ref, done)
    mean, inverse, tally = stat_ref[0:1, :], stat_ref[1:2, :], stat_ref[2:3, :]
    gain, shift = vec_ref[0:1, :], vec_ref[1:2, :]
    zero = jnp.zeros((8, C), f32)

    def gather(start, carry):
        plain, with_normed = carry
        valid = wide_mask(mask_ref, start, CHUNK)
        here = pl.ds(start, CHUNK)
        normed = (turned_ref[here, :].astype(f32) - mean) * inverse
        value = grad_ref[here, :] * slope((normed * gain + shift) * valid) * valid
        grad_ref[here, :] = value
        return (plain + fold(value), with_normed + fold(value * normed))

    plain, with_normed = chunks(gather, (zero, zero))
    shift_grad, gain_grad = total(plain), total(with_normed)
    first_mean = group_sum(gain * shift_grad) / tally
    second_mean = group_sum(gain * gain_grad) / tally
    for index in range(PIX // 128):
        here = slice(128 * index, 128 * index + 128)
        valid = wide_mask(mask_ref, 128 * index, 128)
        normed = (turned_ref[here, :].astype(f32) - mean) * inverse
        value = (grad_ref[here, :] * gain - first_mean - normed * second_mean) * inverse * valid
        turn_ref[:, here] = (value + direct_ref[here, :]).T
    out_ref[...] = turn_ref[pl.ds(aligned(at[0] * HALF, 16), HALF), :].astype(bf16)
    place = lax.broadcasted_iota(jnp.int32, (16, 1), 0)
    rows = jnp.where(place == 0, gain_grad, jnp.where(place == 1, shift_grad, vec_in_ref[...]))
    vec_grad_ref[...] = own_half(rows, at[0])


def add_cores(at, keep_ref, back_ref, own_ref, across_ref):
    for depth in range(4):
        for target, side in ((own_ref, at[2]), (across_ref, 1 - at[2])):
            chip = depth * 2 + side
            target[depth] = (keep_ref[chip].astype(f32) + back_ref[chip].astype(f32)).astype(bf16)


def add_sides(at, own_ref, back_ref, mine_ref, *across):
    for step, target in enumerate((mine_ref,) + across):
        depth = at[3] ^ step
        target[...] = (own_ref[depth].astype(f32) + back_ref[depth].astype(f32)).astype(bf16)


def adam_update(weight, gradient, moment, square, step_rate):
    moment_new = beta_one * moment + (1.0 - beta_one) * gradient
    square_new = beta_two * square + (1.0 - beta_two) * gradient * gradient
    ratio = (
        moment_new
        / (1.0 - beta_one**STEP)
        / (jnp.sqrt(square_new / (1.0 - beta_two**STEP)) + adam_eps)
    )
    return (weight - step_rate * (ratio + decay_rate * weight), moment_new, square_new)


def unpair_rows(block, rows):
    top = block.shape[0]
    return jnp.concatenate((block, pltpu.roll(block, 64, 1)[0 : rows - top]), axis=0)


def adam_into(gradient, given, outs, rate, where):
    weight, moment, square = (ref[where] for ref in given)
    results = adam_update(weight, gradient, moment, square, rate)
    for out, value in zip(outs, (gradient,) + results):
        out[where] = value


def conv_adam(parts, weight_ref, moment_ref, square_ref, outs, rate):
    def summed(start, stop):
        return sum(part[start:stop, :].astype(f32) for part in parts[1:]) + parts[0][
            start:stop, :
        ].astype(f32)

    low = summed(0, 224)[0:ROWS]
    high = unpair_rows(summed(224, 336), ROWS)
    gradient = jnp.concatenate((low, high[:, 0:64]), axis=1).T
    results = adam_update(weight_ref[...], gradient, moment_ref[...], square_ref[...], rate)
    for out, value in zip(outs, (gradient,) + results):
        out[...] = value
    return summed


def finish_first(at, *refs):
    conv_adam(refs[0:4], *refs[4:7], refs[7:11], step_rates()[0])


def finish_second(at, *refs):
    given, results = refs[4:13], refs[13:]
    summed = conv_adam(refs[0:4], *given[0:3], results[0:4], step_rates()[1])
    gradient = jnp.concatenate(
        (summed(336, 416)[0:72], unpair_rows(summed(416, 464)[0:40], 72)[:, 0:64]), axis=1
    )
    for index in range(3):
        adam_into(
            gradient[24 * index : 24 * index + 24], given[3:6], results[4:8], step_rates()[3], index
        )
    gradient = jnp.concatenate(
        (summed(464, 496)[0:24], unpair_rows(summed(496, 512), 24)[:, 0:64]), axis=1
    )
    adam_into(gradient, given[6:9], results[8:12], step_rates()[4], Ellipsis)


def finish_small(at, own_ref, one_ref, two_ref, three_ref, soft_ref, *refs):
    wide = (at[3] * 2 + at[2]) * 2 + at[1]
    given, results, grad_ref = refs[0:6], refs[6:14], refs[14]
    sums, films = None, []
    for far, ref in enumerate((own_ref, one_ref, two_ref, three_ref)):
        for near in range(4):
            rows = ref[near]
            sums = rows if sums is None else sums + rows
            films.append(jnp.concatenate((rows[11:12], rows[12:13]), axis=1))
    adam_into(sums[0:13, 0:HALF], given[0:3], results[0:4], step_rates()[5], Ellipsis)
    grad_ref[...] = lax.dot_general(
        soft_ref[...].astype(bf16), jnp.concatenate(films, axis=0).astype(bf16), ON_FIRST,
        preferred_element_type=f32,
    )
    here = pl.ds(aligned(wide * 48, 8), 48)
    for index in (0, 1):
        gradient = grad_ref[here, 256 * index : 256 * index + HALF]
        adam_into(
            gradient, given[3:6], results[4:8], step_rates()[2], (slice(None), index, slice(None))
        )


def along_depth(unit, wide):
    return [unit] + [
        lax.ppermute(unit, "wide", [(i, i ^ (4 * step)) for i in range(wide)])
        for step in (1, 2, 3)
    ]


def along_plane(stack, wide):
    diagonal = [(2 * i + x, 2 * (i ^ 2) + 1 - x) for i in range(wide) for x in (0, 1)]
    return [
        stack,
        lax.ppermute(stack, "wide", [(i, i ^ 2) for i in range(wide)]),
        lax.ppermute(stack, "narrow", [(0, 1), (1, 0)]),
        lax.ppermute(stack, ("wide", "narrow"), diagonal),
    ]


def both_cores(parts, wide):
    return list(parts) + [
        lax.ppermute(v, "wide", [(i, i ^ 1) for i in range(wide)]) for v in parts
    ]


def tie(values, after, scalars):
    ins = [pltpu.with_memory_space_constraint(v, pltpu.HBM) for v in (*values, *after)]
    return pl.pallas_call(
        pass_on,
        out_shape=tuple(shaped(v.shape, v.dtype) for v in values),
        in_specs=[pl.BlockSpec(memory_space=pltpu.SMEM)]
        + [pl.BlockSpec(memory_space=pltpu.HBM) for _ in ins],
        out_specs=tuple(pl.BlockSpec(memory_space=pltpu.HBM) for _ in values),
        input_output_aliases={index + 1: index for index in range(len(values))},
    )(scalars, *ins)


def add_core_units(keep, send, scalars, wide):
    back = lax.ppermute(send, "wide", [(i, i ^ 1) for i in range(wide)])
    four = shaped((4, keep.shape[1], 128), bf16)
    return call(add_cores, (four, four), (keep, back), scalars)


def add_far_units(own, across, scalars, wide):
    back = lax.ppermute(across, "wide", [(i, i ^ 2) for i in range(wide)])
    one = shaped((own.shape[1], 128), bf16)
    parts = call(add_sides, (one,) * 4, (own, back), scalars)
    return [parts[0]] + [
        lax.ppermute(parts[step], "wide", [(i, i ^ (4 * step)) for i in range(wide)])
        for step in (1, 2, 3)
    ]


def gather_vectors(rows, wide):
    rows = jnp.stack((rows, lax.ppermute(rows, "wide", [(i, i ^ 1) for i in range(wide)])))
    rows = jnp.concatenate((rows, lax.ppermute(rows, "wide", [(i, i ^ 2) for i in range(wide)])))
    return along_depth(rows, wide)


def per_device(
    features,
    embedding,
    valid_mask,
    cotangent,
    conv_first,
    conv_first_moment,
    conv_first_square,
    conv_second,
    conv_second_moment,
    conv_second_square,
    film_weight,
    film_weight_moment,
    film_weight_square,
    attend_in,
    attend_in_moment,
    attend_in_square,
    attend_out,
    attend_out_moment,
    attend_out_square,
    vectors,
    vectors_moment,
    vectors_square,
):
    wide = lax.axis_size("wide")
    unit_path = wide == 16
    narrow_at = lax.axis_index("narrow").astype(jnp.int32)
    wide_at = lax.axis_index("wide").astype(jnp.int32)
    scalars = jnp.stack((narrow_at, wide_at & 1, (wide_at >> 1) & 1, wide_at >> 2))
    flip = [(0, 1), (1, 0)]
    plane = shaped((PIX, C), f32)
    low_plane = shaped((PIX, C), bf16)
    taps = shaped((PADDED, 3 * C), bf16)
    back_half = shaped((PADDED, 256), bf16)
    kernel = shaped((9 * C, C), bf16)
    stats = shaped((8, C), f32)
    vec_rows = shaped((16, C), f32)
    half_plane = shaped((HALF, PIX), bf16)
    rows_scratch = pltpu.VMEM((PIX + 16, C), f32)

    mask = jnp.broadcast_to(valid_mask[0].astype(f32)[:, None], (PIX, 128))
    own_features = features[0]
    own_cotangent = cotangent[0]
    (exchange,) = call(
        pack_exchange,
        (shaped((2 * HALF + 16, PIX), bf16),),
        (own_features, vectors, own_cotangent),
        scalars,
    )
    exchanged = lax.ppermute(exchange, "narrow", flip)

    if unit_path:
        weights = (
            jnp.transpose(conv_first),
            jnp.transpose(conv_second),
            film_weight,
            jnp.transpose(attend_in, (1, 0, 2)),
            attend_out,
        )
        (unit,) = call(
            pack_weights,
            (shaped((FIRST_ROWS + SECOND_ROWS, 128), bf16),),
            (embedding,),
            scalars,
            tuple(pltpu.VMEM(v.shape, f32) for v in weights) + (pltpu.SemaphoreType.DMA((5,)),),
            far=weights,
        )
        first_stack, second_stack = call(
            stack_all,
            tuple(shaped((4, rows, 128), bf16) for rows in (FIRST_ROWS, SECOND_ROWS)),
            along_depth(unit, wide),
            scalars,
        )
        first_units = both_cores(along_plane(first_stack, wide), wide)
    else:

        def whole(array, axis):
            array = lax.all_gather(array.astype(bf16), "wide", axis=0, tiled=True)
            return lax.all_gather(array, "narrow", axis=axis, tiled=True)

        first_full, second_full = whole(conv_first, 1), whole(conv_second, 1)
        film_full = whole(film_weight, 2).reshape(EMB, 2 * C)
        in_full = whole(attend_in, 2).reshape(C, 3 * C)
        out_full = whole(attend_out, 1)

    turned, taps_one, stat_one, vecs = call(
        first_norm,
        (low_plane, taps, stats, vec_rows),
        (own_features, exchanged, mask, vectors),
        scalars,
        (rows_scratch, pltpu.VMEM((PIX, C), f32)),
        far=(first_stack,) if unit_path else (),
    )
    if unit_path:
        second_parts = along_plane(second_stack, wide)
        out_one, kernel_one, stat_two = call(
            first_conv,
            (plane, kernel, stats),
            (taps_one, mask, vecs),
            scalars,
            (
                pltpu.VMEM((8, 4, FIRST_ROWS, 128), bf16),
                pltpu.SemaphoreType.DMA((8,)),
            ),
            far=(*first_units, second_stack),
        )
        arrived = [tie((part,), (stat_two,), scalars)[0] for part in second_parts[1:4]]
        second_units = both_cores([second_parts[0], *arrived], wide)
    else:
        kernel_one = first_full
        out_one, stat_two = call(
            first_conv_plain, (plane, stats), (taps_one, mask, vecs, kernel_one), scalars
        )
    common = (out_one, stat_two, turned, mask, vecs, embedding)
    attention_scratch = (
        pltpu.VMEM((C, 3 * C), f32),
        pltpu.VMEM((C, C), f32),
        pltpu.VMEM((C, 1536), bf16),
        pltpu.VMEM((512, C), bf16),
        *([pltpu.VMEM((PIX, 512), bf16)] * 3),
        *([pltpu.VMEM((512, PIX), bf16)] * 5),
        pltpu.VMEM((PIX, 128), f32),
        pltpu.VMEM((PIX, 128), f32),
        pltpu.VMEM((PIX, C), bf16),
        rows_scratch,
        pltpu.VMEM((9 * C, 256), f32),
        pltpu.VMEM((PIX, 256), bf16),
    )
    back_scratch = (pltpu.VMEM((PIX, C), f32), rows_scratch)
    terms_scratch = (pltpu.VMEM((PADDED, 256), bf16), pltpu.VMEM((9 * C, 256), f32))
    if unit_path:
        units = shaped((8, 512, 128), bf16)
        (
            output, direct, taps_back, vec_grad, film_rows, kernel_two, soft_all, keep, send,
        ) = call(
            middle_of_block,
            (
                half_plane, plane, taps, vec_rows, stats, kernel, shaped((16, EMB), f32),
                units, units,
            ),
            common + (own_cotangent, exchanged),
            scalars,
            (
                pltpu.VMEM((PADDED, 3 * C), bf16),
                pltpu.VMEM((PIX, C), f32),
                pltpu.VMEM((PIX, C), bf16),
                pltpu.VMEM((8, C), f32),
                pltpu.VMEM((16, EMB), f32),
                pltpu.VMEM((EMB, 2 * C), bf16),
                pltpu.VMEM((8, 4, SECOND_ROWS, 128), bf16),
                pltpu.SemaphoreType.DMA((8,)),
                pltpu.VMEM((PADDED, 256), bf16),
                *attention_scratch,
            ),
            far=second_units,
            flops=4 * 10**10,
        )
        own_second, across_second = add_core_units(keep, send, scalars, wide)
        units = shaped((8, 336, 128), bf16)
        taps_back_one, vec_grad, keep, send = call(
            second_back,
            (taps, vec_rows, units, units),
            (
                taps_back, kernel_two, out_one, stat_two, film_rows, mask, vecs, vec_grad,
                taps_one,
            ),
            scalars,
            back_scratch + terms_scratch,
            far=(across_second,),
        )
        parts_second = add_far_units(own_second, across_second, scalars, wide)
        own_first, across_first = add_core_units(keep, send, scalars, wide)
        parts_first = add_far_units(own_first, across_first, scalars, wide)
        started = (across_first,)
    else:
        kernel_two = second_full
        taps_two, residual, hidden, stat_three, film_rows = call(
            second_conv_plain,
            (taps, plane, low_plane, stats, stats),
            common + (kernel_two, film_full),
            scalars,
            (pltpu.VMEM((16, EMB), f32), rows_scratch),
        )
        output, direct, taps_back, back_two, vec_grad, in_term, out_term = call(
            attention_plain,
            (
                half_plane, plane, taps, back_half, vec_rows,
                shaped((C, 768), f32), shaped((C, 256), f32),
            ),
            (
                hidden, residual, stat_three, mask, vecs, own_cotangent, exchanged,
                in_full, out_full,
            ),
            scalars,
            attention_scratch,
        )
        (second_term,) = call(
            conv_terms_plain, (shaped((9 * C, 256), f32),), (taps_two, back_two), scalars
        )
        taps_back_one, back_one, vec_grad = call(
            second_back_plain,
            (taps, back_half, vec_rows),
            (taps_back, kernel_two, out_one, stat_two, film_rows, mask, vecs, vec_grad),
            scalars,
            back_scratch,
        )
        (first_term,) = call(
            conv_terms_plain, (shaped((9 * C, 256), f32),), (taps_one, back_one), scalars
        )
        started = ()
    input_gradient, vec_half = call(
        first_back,
        (half_plane, shaped((16, 256), f32)),
        (taps_back_one, kernel_one, turned, stat_one, direct, mask, vecs, vec_grad),
        scalars,
        (pltpu.VMEM((PIX, C), f32), pltpu.VMEM((C, PIX), f32)),
        far=started,
    )
    if unit_path:
        vec_shape, film_shape = shaped((13, HALF), f32), shaped(film_weight.shape, f32)
        small = call(
            finish_small,
            (vec_shape,) * 4 + (film_shape,) * 4,
            (
                *gather_vectors(vec_half, wide),
                soft_all,
                vectors,
                vectors_moment,
                vectors_square,
                film_weight,
                film_weight_moment,
                film_weight_square,
            ),
            scalars,
            (pltpu.VMEM((EMB, 512), f32),),
        )
        vec_results, film_results = small[:4], small[4:]
    else:
        vec_half = vec_half[:13, :HALF]
        vec_sum = lax.psum(vec_half, "wide")
        soft = jax.nn.silu(embedding.astype(f32)).astype(bf16)
        soft_all = lax.all_gather(soft, "wide", axis=0, tiled=True)
        rows_here = film_weight.shape[0]
        soft_here = lax.dynamic_slice_in_dim(soft_all, wide_at * rows_here, rows_here, axis=1)
        film_all = lax.all_gather(vec_half[11:13].astype(bf16)[None], "wide", axis=0, tiled=True)
        film_gradient = jnp.einsum("se,stj->etj", soft_here, film_all, preferred_element_type=f32)

    rates = step_rates()
    shard = shaped((HALF, ROWS), f32)

    def turned_shards(*shards):
        return tuple(jnp.transpose(v) for v in shards)

    if unit_path:
        in_shape, out_shape = shaped((3, 24, HALF), f32), shaped((24, HALF), f32)
        in_given = tuple(
            jnp.transpose(v, (1, 0, 2)) for v in (attend_in, attend_in_moment, attend_in_square)
        )
        second_results = call(
            finish_second,
            (shard,) * 4 + (in_shape,) * 4 + (out_shape,) * 4,
            (
                *parts_second,
                *turned_shards(conv_second, conv_second_moment, conv_second_square),
                *in_given,
                attend_out,
                attend_out_moment,
                attend_out_square,
            ),
            scalars,
        )
        in_results = tuple(jnp.transpose(v, (1, 0, 2)) for v in second_results[4:8])
        out_results = second_results[8:12]
        second_results = turned_shards(*second_results[:4])
        first_results = call(
            finish_first,
            (shard,) * 4,
            (*parts_first, *turned_shards(conv_first, conv_first_moment, conv_first_square)),
            scalars,
        )
        first_results = turned_shards(*first_results)
    else:

        def scatter(term):
            return lax.psum_scatter(term, "wide", scatter_dimension=0, tiled=True)

        first_gradient = scatter(first_term[:, :HALF])
        second_gradient = scatter(second_term[:, :HALF])
        in_gradient = scatter(in_term.reshape(C, 3, 256)[:, :, :HALF])
        out_gradient = scatter(out_term[:, :HALF])

        def finish(weight, gradient, moment, square, rate):
            return (gradient,) + adam_update(weight, gradient, moment, square, rate)

        first_results = finish(
            conv_first, first_gradient, conv_first_moment, conv_first_square, rates[0]
        )
        second_results = finish(
            conv_second, second_gradient, conv_second_moment, conv_second_square, rates[1]
        )
        film_results = finish(
            film_weight, film_gradient, film_weight_moment, film_weight_square, rates[2]
        )
        in_results = finish(
            attend_in, in_gradient, attend_in_moment, attend_in_square, rates[3]
        )
        out_results = finish(
            attend_out, out_gradient, attend_out_moment, attend_out_square, rates[4]
        )
        vec_results = finish(vectors, vec_sum, vectors_moment, vectors_square, rates[5])

    return (
        output[None],
        input_gradient[None],
        *first_results,
        *second_results,
        *film_results,
        *in_results,
        *out_results,
        *vec_results,
    )


def solution(mesh):
    in_specs = (
        P("wide", "narrow", None),
        P("wide", None),
        P("wide", None),
        P("wide", "narrow", None),
        P("wide", "narrow"),
        P("wide", "narrow"),
        P("wide", "narrow"),
        P("wide", "narrow"),
        P("wide", "narrow"),
        P("wide", "narrow"),
        P("wide", None, "narrow"),
        P("wide", None, "narrow"),
        P("wide", None, "narrow"),
        P("wide", None, "narrow"),
        P("wide", None, "narrow"),
        P("wide", None, "narrow"),
        P("wide", "narrow"),
        P("wide", "narrow"),
        P("wide", "narrow"),
        P(None, "narrow"),
        P(None, "narrow"),
        P(None, "narrow"),
    )
    out_specs = (
        P("wide", "narrow", None),
        P("wide", "narrow", None),
        P("wide", "narrow"),
        P("wide", "narrow"),
        P("wide", "narrow"),
        P("wide", "narrow"),
        P("wide", "narrow"),
        P("wide", "narrow"),
        P("wide", "narrow"),
        P("wide", "narrow"),
        P("wide", None, "narrow"),
        P("wide", None, "narrow"),
        P("wide", None, "narrow"),
        P("wide", None, "narrow"),
        P("wide", None, "narrow"),
        P("wide", None, "narrow"),
        P("wide", None, "narrow"),
        P("wide", None, "narrow"),
        P("wide", "narrow"),
        P("wide", "narrow"),
        P("wide", "narrow"),
        P("wide", "narrow"),
        P(None, "narrow"),
        P(None, "narrow"),
        P(None, "narrow"),
        P(None, "narrow"),
    )
    return jax.shard_map(
        per_device, mesh=mesh, in_specs=in_specs, out_specs=out_specs, check_vma=False
    )
```

```python
import jax
import jax.numpy as jnp
from jax import lax
from jax.experimental import pallas as pl
from jax.experimental.pallas import tpu as pltpu
from jax.sharding import PartitionSpec as P

C = 384
HEADS = 4
GROUPS = 32
EMB = 768
SIDE = 32
STEP = 10
PIX = SIDE * SIDE
HALF = C // 2
PADDED = PIX + 2 * SIDE
HEAD = C // HEADS
ROWS = 216
CHUNK = 64

beta_one = 0.9
beta_two = 0.999
adam_eps = 1e-08
decay_rate = 0.01
norm_eps = 1e-05
masked_score = -1e30
score_scale = HEAD ** (-0.5)
exponent_scale = score_scale * 1.4426950408889634

f32 = jnp.float32
bf16 = jnp.bfloat16
ON_LAST = (((1,), (1,)), ((), ()))
ON_FIRST = (((0,), (0,)), ((), ()))
VMEM_BYTES = 45 * 1024 * 1024


def step_rates():
    return (
        2.0 * (9 * C) ** (-0.5),
        2.0 * (9 * C) ** (-0.5),
        2.0 * EMB ** (-0.5),
        2.0 * C ** (-0.5),
        2.0 * (C // 64) ** (-0.5),
        0.5,
    )


def spec():
    return pl.BlockSpec(memory_space=pltpu.VMEM)


def call(body, outs, ins, scalars, scratch=(), far=(), aliases=None, flops=0):
    far = tuple(pltpu.with_memory_space_constraint(v, pltpu.HBM) for v in far)
    ins = tuple(ins) + far
    limit = VMEM_BYTES if body in (middle_of_block, attention_plain) else VMEM_BYTES // 3
    return pl.pallas_call(
        body,
        out_shape=tuple(outs),
        in_specs=[pl.BlockSpec(memory_space=pltpu.SMEM)]
        + [spec() for _ in ins[: len(ins) - len(far)]]
        + [pl.BlockSpec(memory_space=pltpu.HBM) for _ in far],
        out_specs=tuple(spec() for _ in outs),
        scratch_shapes=list(scratch),
        input_output_aliases=aliases or {},
        compiler_params=pltpu.CompilerParams(vmem_limit_bytes=limit),
        cost_estimate=pl.CostEstimate(flops=flops, bytes_accessed=1024, transcendentals=0),
    )(scalars, *ins)


def shaped(shape, kind):
    return jax.ShapeDtypeStruct(shape, kind)


def aligned(value, by):
    return pl.multiple_of(value, by)


def wide_mask(mask_ref, start, count):
    part = mask_ref[pl.ds(start, count), :]
    return jnp.concatenate((part, part, part), axis=1)


def group_sum(row):
    first = (lax.broadcasted_iota(jnp.int32, (C, C), 0) * 5462) >> 16
    second = (lax.broadcasted_iota(jnp.int32, (C, C), 1) * 5462) >> 16
    member = jnp.where(first == second, 1.0, 0.0).astype(f32)
    spread = jnp.broadcast_to(row, (8, C))
    return jnp.dot(
        spread, member, preferred_element_type=f32, precision=lax.Precision.HIGHEST
    )[0:1]


def fold(block):
    return jnp.sum(block.reshape(block.shape[0] // 8, 8, block.shape[1]), axis=0)


def total(acc):
    return jnp.sum(acc, axis=0, keepdims=True)


def chunks(step, init):
    def body(index, carry):
        return step(aligned(index * CHUNK, CHUNK), carry)

    return lax.fori_loop(0, PIX // CHUNK, body, init, unroll=2)


def norm_stats(source_ref, mask_ref):
    zero = jnp.zeros((8, C), f32)

    def first(start, carry):
        sums, count = carry
        valid = wide_mask(mask_ref, start, CHUNK)
        return (sums + fold(source_ref[pl.ds(start, CHUNK), :] * valid), count + fold(valid))

    sums, count = chunks(first, (zero, zero))
    tally = total(count) * float(C // GROUPS)
    mean = group_sum(total(sums)) / tally

    def second(start, carry):
        valid = wide_mask(mask_ref, start, CHUNK)
        centred = source_ref[pl.ds(start, CHUNK), :] - mean
        return carry + fold(centred * centred * valid)

    variance = group_sum(total(chunks(second, zero))) / tally
    return mean, lax.rsqrt(variance + norm_eps), tally


def keep_stats(stat_ref, mean, inverse, tally):
    stat_ref[0:1, :] = mean
    stat_ref[1:2, :] = inverse
    stat_ref[2:3, :] = tally


def column_index(count):
    return lax.broadcasted_iota(jnp.int32, (count, 1), 0) & (SIDE - 1)


def write_taps(rows_ref, taps_ref):
    blank = jnp.zeros((SIDE, 3 * C), bf16)
    taps_ref[0:SIDE, :] = blank
    taps_ref[SIDE + PIX : PADDED, :] = blank
    column = column_index(CHUNK)
    for index in range(PIX // CHUNK):
        start = index * CHUNK
        here = pl.ds(SIDE + start, CHUNK)
        left = rows_ref[pl.ds(7 + start, CHUNK), :]
        right = rows_ref[pl.ds(9 + start, CHUNK), :]
        taps_ref[here, 0:C] = jnp.where(column == 0, 0.0, left).astype(bf16)
        taps_ref[here, C : 2 * C] = rows_ref[pl.ds(8 + start, CHUNK), :].astype(bf16)
        taps_ref[here, 2 * C : 3 * C] = jnp.where(column == SIDE - 1, 0.0, right).astype(bf16)


def lane(count):
    return lax.broadcasted_iota(jnp.int32, (count, 128), 1)


def own_half(block, narrow):
    one, two, three = block[:, 0:128], block[:, 128:256], block[:, 256:384]
    turned_two, turned_three = pltpu.roll(two, 64, 1), pltpu.roll(three, 64, 1)
    upper = jnp.where(lane(block.shape[0]) < 64, turned_two, turned_three)
    return jnp.concatenate(
        (jnp.where(narrow == 0, one, upper), jnp.where(narrow == 0, two, turned_three)), axis=1
    )


def write_own(rows_ref, own_ref, narrow):
    blank = jnp.zeros((SIDE, 256), bf16)
    own_ref[0:SIDE, :] = blank
    own_ref[SIDE + PIX : PADDED, :] = blank
    for index in range(PIX // CHUNK):
        start = index * CHUNK
        block = rows_ref[pl.ds(8 + start, CHUNK), :]
        own_ref[pl.ds(SIDE + start, CHUNK), :] = own_half(block, narrow).astype(bf16)


def convolve(taps_ref, kernel_ref, done, block=512):
    for index in range(PIX // block):
        start = index * block
        acc = None
        for tap in range(3):
            part = jnp.dot(
                taps_ref[pl.ds(start + SIDE * tap, block), :],
                kernel_ref[tap * 3 * C : (tap + 1) * 3 * C, :],
                preferred_element_type=f32,
            )
            acc = part if acc is None else acc + part
        done(start, block, acc)


def convolve_back(taps_ref, kernel_ref, done, block=512):
    for index in range(PIX // block):
        start = index * block
        acc = None
        for tap in range(9):
            tap_row, tap_col = tap // 3, tap % 3
            flipped = 8 - tap
            part = lax.dot_general(
                taps_ref[pl.ds(start + SIDE * tap_row, block), tap_col * C : (tap_col + 1) * C],
                kernel_ref[flipped * C : (flipped + 1) * C, :],
                ON_LAST,
                preferred_element_type=f32,
            )
            acc = part if acc is None else acc + part
        done(start, block, acc)


def kernel_terms(taps_ref, own_ref, terms_ref):
    for tap_col in range(3):
        for tap_row in range(3):
            tap = 3 * tap_row + tap_col
            first = 2 * SIDE - SIDE * tap_row
            terms_ref[tap * C : (tap + 1) * C, :] = lax.dot_general(
                taps_ref[SIDE : SIDE + PIX, tap_col * C : (tap_col + 1) * C],
                own_ref[first : first + PIX, :],
                ON_FIRST,
                preferred_element_type=f32,
            )


def slope(value):
    logistic = lax.logistic(value)
    return logistic * (1.0 + value * (1.0 - logistic))


def tile_parts(block, narrow):
    rows = block.shape[0]
    one = block[:, 0:128]
    two = jnp.concatenate((block[:, 128:192], jnp.zeros((rows, 64), f32)), axis=1)
    turned = jnp.where(lane(rows) < 64, pltpu.roll(one, 64, 1), pltpu.roll(two, 64, 1))
    return jnp.where(narrow == 0, one, turned), jnp.where(narrow == 0, two, one)


def pair_rows(block, top):
    rows = block.shape[0]
    low = block[top:rows]
    if rows < 2 * top:
        low = jnp.concatenate((low, jnp.zeros((2 * top - rows, 128), f32)), axis=0)
    return jnp.where(lane(top) < 64, block[0:top], pltpu.roll(low, 64, 1))


def pad_rows(block, rows):
    if block.shape[0] == rows:
        return block
    return jnp.concatenate((block, jnp.zeros((rows - block.shape[0], block.shape[1]), f32)), axis=0)


def middle(first, second, top, rows):
    one = jnp.where(lane(top) < 64, first, pltpu.roll(second, 64, 1))
    two = jnp.where(lane(top) < 64, pltpu.roll(first, 64, 1), second)
    return jnp.concatenate((one, two[0 : rows - top]), axis=0)


def pack_exchange(at, features_ref, vec_ref, cot_ref, out_ref):
    out_ref[HALF + 16 : 2 * HALF + 16, :] = cot_ref[...]
    out_ref[0:HALF, :] = features_ref[...]
    vec = jnp.concatenate((vec_ref[...], jnp.zeros((3, HALF), f32)), axis=0)
    coarse = vec.astype(bf16)
    out_ref[HALF : HALF + 16, :] = jnp.zeros((16, PIX), bf16)
    out_ref[HALF : HALF + 16, 0:HALF] = coarse
    out_ref[HALF : HALF + 16, 256 : 256 + HALF] = (vec - coarse.astype(f32)).astype(bf16)


FIRST_ROWS = 336
FILM_AT, FILM_SHARED, EMBED_AT, IN_AT, IN_SHARED, OUT_AT, OUT_SHARED, SECOND_ROWS = 336, 432, 480, 496, 576, 624, 656, 672


def stack_all(at, *refs):
    first_ref, second_ref = refs[4:6]
    for step in range(4):
        first_ref[step] = refs[step][0:FIRST_ROWS, :]
        second_ref[step] = refs[step][FIRST_ROWS : FIRST_ROWS + SECOND_ROWS, :]


def pass_on(at, *refs):
    pass


def put_rows(out_ref, start, block):
    rows = -(-block.shape[0] // 16) * 16
    out_ref[start : start + rows, :] = pad_rows(block, rows).astype(bf16)


def pack_weights(at, embed_ref, *refs):
    unit_ref, first_ref, second_ref, film_ref, in_ref, out_ref, sems = refs[5:]
    narrow = at[0]
    copies = [
        pltpu.make_async_copy(source, target, sems.at[index])
        for index, (source, target) in enumerate(
            zip(refs[0:5], (first_ref, second_ref, film_ref, in_ref, out_ref))
        )
    ]
    for copy in copies:
        copy.start()
    embed = embed_ref[...].astype(f32)
    put_rows(
        unit_ref,
        FIRST_ROWS + EMBED_AT,
        jnp.concatenate([embed[:, 128 * i : 128 * i + 128] for i in range(EMB // 128)], axis=0),
    )
    copies[0].wait()
    part, shared = tile_parts(first_ref[...].T, narrow)
    put_rows(unit_ref, 0, part)
    put_rows(unit_ref, 224, pair_rows(shared, 112))
    for copy in copies[1:]:
        copy.wait()
    for block, start, shared_start, top in (
        (second_ref[...].T, 0, 224, 112),
        (
            jnp.concatenate((film_ref[:, 0, :], film_ref[:, 1, :]), axis=0),
            FILM_AT, FILM_SHARED, 48,
        ),
        (jnp.concatenate((in_ref[0], in_ref[1], in_ref[2]), axis=0), IN_AT, IN_SHARED, 40),
        (out_ref[...], OUT_AT, OUT_SHARED, 16),
    ):
        part, shared = tile_parts(block, narrow)
        put_rows(unit_ref, FIRST_ROWS + start, part)
        put_rows(unit_ref, FIRST_ROWS + shared_start, pair_rows(shared, top))


class Gathered:
    def __init__(self, at, refs, held_ref, sems):
        self.narrow, self.core, self.side, self.depth = at[0], at[1], at[2], at[3]
        self.held = held_ref
        self.copies = {}
        for differs in (0, 1):
            for index in range(differs, 8, 2):
                copy = pltpu.make_async_copy(refs[index], held_ref.at[index], sems.at[index])
                copy.start()
                self.copies[index] = copy

    def part(self, other, differs, across, step):
        return self.held.at[4 * other + 2 * across + differs, step]

    def wait(self, differs):
        for index in range(differs, 8, 2):
            self.copies[index].wait()

    def chips(self):
        for differs in (0, 1):
            for step in range(4):
                yield differs, step, (self.depth ^ step) * 2 + (self.side ^ differs)

    def cores(self, differs, step, start, rows):
        upto = -(-rows // 16) * 16
        found = []
        for across in (0, 1):
            own = self.part(0, differs, across, step)[start : start + upto, :].astype(f32)[0:rows]
            other = self.part(1, differs, across, step)[start : start + upto, :].astype(f32)[0:rows]
            found.append(
                (jnp.where(self.core == 0, own, other), jnp.where(self.core == 0, other, own))
            )
        here, there = found
        return tuple(
            tuple(
                jnp.where((self.narrow == 0) == (tile == 0), here[core], there[core])
                for core in (0, 1)
            )
            for tile in (0, 1)
        )


def place_conv(units, kernel_ref):
    for differs, step, chip in units.chips():
        if step == 0:
            units.wait(differs)
        rows = pl.ds(aligned(chip * (2 * ROWS), 16), 2 * ROWS)
        low, high = units.cores(differs, step, 0, ROWS)
        kernel_ref[rows, 0:128] = jnp.concatenate(low, axis=0).astype(bf16)
        kernel_ref[rows, 256:384] = jnp.concatenate(high, axis=0).astype(bf16)
        low, high = units.cores(differs, step, 224, 112)
        kernel_ref[rows, 128:256] = jnp.concatenate(
            [middle(low[core], high[core], 112, ROWS) for core in (0, 1)], axis=0
        ).astype(bf16)


def place_film(units, film_ref):
    for differs, step, chip in units.chips():
        rows = pl.ds(aligned(chip * 96, 16), 96)
        low, high = units.cores(differs, step, FILM_AT, 96)
        for index in (0, 1):
            part = slice(48 * index, 48 * index + 48)
            film_ref[rows, index * C : index * C + 128] = jnp.concatenate(
                [low[core][part] for core in (0, 1)], axis=0
            ).astype(bf16)
            film_ref[rows, index * C + 256 : index * C + 384] = jnp.concatenate(
                [high[core][part] for core in (0, 1)], axis=0
            ).astype(bf16)
        low, high = units.cores(differs, step, FILM_SHARED, 48)
        both = [middle(low[core], high[core], 48, 96) for core in (0, 1)]
        for index in (0, 1):
            part = slice(48 * index, 48 * index + 48)
            film_ref[rows, index * C + 128 : index * C + 256] = jnp.concatenate(
                [both[core][part] for core in (0, 1)], axis=0
            ).astype(bf16)


def place_embeddings(shared, soft_ref):
    for differs, step, chip in shared.chips():
        for other in (0, 1):
            row = 4 * step + 2 * differs + other
            part = shared.part(other, differs, 0, step)[EMBED_AT : EMBED_AT + 16, :].astype(f32)
            part = (part * lax.logistic(part)).astype(bf16).astype(f32)
            for index in range(EMB // 128):
                soft_ref[row : row + 1, 128 * index : 128 * index + 128] = part[index : index + 1]


def place_attention(units, in_ref, out_ref):
    for differs, step, chip in units.chips():
        rows = pl.ds(aligned(chip * 48, 16), 48)
        low, high = units.cores(differs, step, IN_AT, 72)
        near, far = units.cores(differs, step, IN_SHARED, 40)
        both = [middle(near[core], far[core], 40, 72) for core in (0, 1)]
        for index in range(3):
            part = slice(24 * index, 24 * index + 24)
            for tile, source in ((0, low), (1, both), (2, high)):
                in_ref[rows, index * C + 128 * tile : index * C + 128 * tile + 128] = (
                    jnp.concatenate([source[core][part] for core in (0, 1)], axis=0)
                )
        low, high = units.cores(differs, step, OUT_AT, 24)
        near, far = units.cores(differs, step, OUT_SHARED, 16)
        both = [middle(near[core], far[core], 16, 24) for core in (0, 1)]
        for tile, source in ((0, low), (1, both), (2, high)):
            out_ref[rows, 128 * tile : 128 * tile + 128] = jnp.concatenate(source, axis=0)


def spread_heads(block):
    one, two, three = block[:, 0:128], block[:, 128:256], block[:, 256:384]
    place = lane(block.shape[0])

    def cut(value):
        return jnp.where(place < HEAD, value, 0.0)

    return jnp.concatenate(
        (
            cut(one),
            cut(jnp.where(place < 32, pltpu.roll(one, 32, 1), pltpu.roll(two, 32, 1))),
            cut(jnp.where(place < 64, pltpu.roll(two, 64, 1), pltpu.roll(three, 64, 1))),
            cut(pltpu.roll(three, 96, 1)),
        ),
        axis=1,
    )


def join_heads(block):
    one, two = block[:, 0:128], pltpu.roll(block[:, 128:256], HEAD, 1)
    return jnp.concatenate((jnp.where(lane(block.shape[0]) < HEAD, one, two), two), axis=1)


def first_norm(at, own_ref, other_ref, mask_ref, vec_own_ref, *refs):
    turned_ref, taps_ref, stat_ref, vec_ref, rows_ref, raw_ref = refs[-6:]
    narrow = at[0]
    own = vec_own_ref[...]
    other = (
        other_ref[HALF : HALF + 16, 0:HALF].astype(f32)
        + other_ref[HALF : HALF + 16, 256 : 256 + HALF].astype(f32)
    )[0:13]
    vec_ref[0:13, 0:HALF] = jnp.where(narrow == 0, own, other)
    vec_ref[0:13, HALF:C] = jnp.where(narrow == 0, other, own)
    vec_ref[13:16, :] = jnp.zeros((3, C), f32)
    own = own_ref[...].astype(f32)
    other = other_ref[0:HALF, :].astype(f32)
    low = jnp.where(narrow == 0, own, other)
    high = jnp.where(narrow == 0, other, own)
    for index in range(PIX // 128):
        here = slice(128 * index, 128 * index + 128)
        block = jnp.concatenate((low[:, here], high[:, here]), axis=0).T
        raw_ref[here, :] = block
        turned_ref[here, :] = block.astype(bf16)
    mean, inverse, tally = norm_stats(raw_ref, mask_ref)
    keep_stats(stat_ref, mean, inverse, tally)
    gain, shift = vec_ref[0:1, :], vec_ref[1:2, :]

    def apply(start, carry):
        valid = wide_mask(mask_ref, start, CHUNK)
        normed = (raw_ref[pl.ds(start, CHUNK), :] - mean) * inverse
        value = (normed * gain + shift) * valid
        rows_ref[pl.ds(start + 8, CHUNK), :] = value * lax.logistic(value)
        return carry

    chunks(apply, 0)
    write_taps(rows_ref, taps_ref)


def conv_then_stats(taps_ref, kernel_ref, mask_ref, vec_ref, out_ref, stat_ref):
    bias = vec_ref[2:3, :]

    def done(start, count, acc):
        out_ref[pl.ds(start, count), :] = acc + bias

    convolve(taps_ref, kernel_ref, done)
    keep_stats(stat_ref, *norm_stats(out_ref, mask_ref))


def first_conv(at, taps_ref, mask_ref, vec_ref, *refs):
    out_ref, kernel_ref, stat_ref, held_ref, sems = refs[-5:]
    units = Gathered(at, refs[0:8], held_ref, sems)
    place_conv(units, kernel_ref)
    conv_then_stats(taps_ref, kernel_ref, mask_ref, vec_ref, out_ref, stat_ref)


def first_conv_plain(at, taps_ref, mask_ref, vec_ref, kernel_ref, out_ref, stat_ref):
    conv_then_stats(taps_ref, kernel_ref, mask_ref, vec_ref, out_ref, stat_ref)


def film_to_third_norm(
    one_ref, stat_two_ref, turned_ref, mask_ref, vec_ref, embed_ref, kernel_ref, film_ref,
    taps_ref, residual_ref, hidden_ref, stat_ref, film_rows_ref, soft_ref, rows_ref,
):
    embed = embed_ref[...].astype(f32)
    soft = (embed * lax.logistic(embed)).astype(bf16)
    soft_ref[...] = jnp.broadcast_to(soft.astype(f32), soft_ref.shape)
    rounded = soft_ref[...].astype(bf16)
    scale = 1.0 + (
        jnp.dot(rounded, film_ref[:, 0:C], preferred_element_type=f32)[0:1] + vec_ref[11:12, :]
    )
    shift = jnp.dot(rounded, film_ref[:, C : 2 * C], preferred_element_type=f32)[0:1] + vec_ref[12:13, :]
    film_rows_ref[0:1, :] = scale
    film_rows_ref[1:2, :] = shift
    mean, inverse = stat_two_ref[0:1, :], stat_two_ref[1:2, :]
    gain_two, shift_two = vec_ref[3:4, :], vec_ref[4:5, :]

    def modulate(start, carry):
        valid = wide_mask(mask_ref, start, CHUNK)
        normed = (one_ref[pl.ds(start, CHUNK), :] - mean) * inverse
        value = (normed * gain_two + shift_two) * valid * scale + shift
        rows_ref[pl.ds(start + 8, CHUNK), :] = value * lax.logistic(value) * valid
        return carry

    chunks(modulate, 0)
    write_taps(rows_ref, taps_ref)
    bias = vec_ref[5:6, :]

    def done(start, count, acc):
        here = pl.ds(start, count)
        valid = wide_mask(mask_ref, start, count)
        residual_ref[here, :] = (turned_ref[here, :].astype(f32) + (acc + bias)) * valid

    convolve(taps_ref, kernel_ref, done)
    mean, inverse, tally = norm_stats(residual_ref, mask_ref)
    keep_stats(stat_ref, mean, inverse, tally)
    gain, shift_three = vec_ref[6:7, :], vec_ref[7:8, :]

    def apply(start, carry):
        valid = wide_mask(mask_ref, start, CHUNK)
        normed = (residual_ref[pl.ds(start, CHUNK), :] - mean) * inverse
        hidden_ref[pl.ds(start, CHUNK), :] = ((normed * gain + shift_three) * valid).astype(bf16)
        return carry

    chunks(apply, 0)


def second_conv_plain(
    at, one_ref, stat_two_ref, turned_ref, mask_ref, vec_ref, embed_ref, kernel_ref, film_ref,
    taps_ref, residual_ref, hidden_ref, stat_ref, film_rows_ref, soft_ref, rows_ref,
):
    film_to_third_norm(
        one_ref, stat_two_ref, turned_ref, mask_ref, vec_ref, embed_ref, kernel_ref, film_ref,
        taps_ref, residual_ref, hidden_ref, stat_ref, film_rows_ref, soft_ref, rows_ref,
    )


QUERY = 256


def attention_both(q_ref, k_ref, v_ref, kt_ref, vt_ref, upt_ref, outt_ref, dqt_ref, dk_acc, dv_acc):
    place = lax.broadcasted_iota(jnp.int32, (128, QUERY), 0)
    steps = PIX // QUERY

    def where(item):
        head, step = divmod(item, steps)
        return slice(128 * head, 128 * head + 128), slice(step * QUERY, step * QUERY + QUERY), step

    def raise_scores(item):
        columns, rows, _ = where(item)
        scores = lax.dot_general(
            k_ref[:, columns], q_ref[rows, columns], ON_LAST, preferred_element_type=f32
        )
        highest = jnp.max(scores, axis=0, keepdims=True)
        return jnp.exp2((scores - highest) * exponent_scale)

    def score_slopes(item, raised):
        columns, rows, _ = where(item)
        low = raised.astype(bf16)
        mixture = jnp.dot(vt_ref[columns, :], low, preferred_element_type=f32)
        inverse = 1.0 / mixture[HEAD : HEAD + 1, :]
        mixture = mixture * inverse
        outt_ref[columns, rows] = mixture.astype(bf16)
        up = (upt_ref[columns, rows].astype(f32) * inverse).astype(bf16)
        wide_up = up.astype(f32)
        both = jnp.sum(wide_up * mixture, axis=0, keepdims=True)
        coarse = both.astype(bf16).astype(f32)
        wide_up = jnp.where(place == HEAD, -coarse, wide_up)
        wide_up = jnp.where(place == HEAD + 1, coarse - both, wide_up)
        slopes = jnp.dot(v_ref[:, columns], wide_up.astype(bf16), preferred_element_type=f32)
        return low, up, (raised * slopes).astype(bf16)

    def gradients(item, low, up, slopes):
        columns, rows, step = where(item)
        dqt_ref[columns, rows] = (
            jnp.dot(kt_ref[columns, :], slopes, preferred_element_type=f32) * score_scale
        ).astype(bf16)
        dk = jnp.dot(slopes, q_ref[rows, columns], preferred_element_type=f32)
        dv = lax.dot_general(low, up, ON_LAST, preferred_element_type=f32)
        if step == 0:
            dk_acc[...] = dk
            dv_acc[...] = dv
        elif step < steps - 1:
            dk_acc[...] += dk
            dv_acc[...] += dv
        else:
            k_ref[:, columns] = ((dk_acc[...] + dk) * score_scale).astype(bf16)
            v_ref[:, columns] = (dv_acc[...] + dv).astype(bf16)

    count = HEADS * steps
    raised, waiting = raise_scores(0), None
    for item in range(count):
        following = raise_scores(item + 1) if item + 1 < count else None
        found = score_slopes(item, raised)
        if waiting is not None:
            gradients(*waiting)
        waiting = (item, *found)
        raised = following
    gradients(*waiting)


def attention_body(
    at, hidden_ref, residual_ref, stat_ref, mask_ref, vec_ref, own_ref, other_ref,
    out_ref, direct_ref, taps_ref, back_ref, vec_grad_ref, in_nat, out_nat,
    in_ref, weight_ref, q_ref, k_ref, v_ref, kt_ref, vt_ref, upt_ref, mixt_ref, dqt_ref,
    dk_acc, dv_acc, cot_ref, rows_ref, terms_ref, own_cot,
):
    narrow = at[0]
    for index in range(3):
        in_ref[:, 512 * index : 512 * index + 512] = spread_heads(
            in_nat[:, C * index : C * index + C]
        ).astype(bf16)
    blank = jnp.zeros((32, C), bf16)
    for head in range(HEADS):
        weight_ref[128 * head : 128 * head + HEAD, :] = out_nat[HEAD * head : HEAD * head + HEAD, :].astype(bf16)
        weight_ref[128 * head + HEAD : 128 * head + 128, :] = blank
    own = own_ref[...].astype(f32)
    other = other_ref[HALF + 16 : 2 * HALF + 16, :].astype(f32)
    low = jnp.where(narrow == 0, own, other)
    high = jnp.where(narrow == 0, other, own)
    zero = jnp.zeros((8, C), f32)
    bias_out = zero
    for index in range(PIX // 128):
        here = slice(128 * index, 128 * index + 128)
        block = jnp.concatenate((low[:, here], high[:, here]), axis=0).T
        rows_ref[pl.ds(8 + 128 * index, 128), :] = block
        part = block * wide_mask(mask_ref, 128 * index, 128)
        bias_out = bias_out + fold(part)
        cot_ref[here, :] = part.astype(bf16)
        own_cot[here, :] = own_half(part, narrow).astype(bf16)
    bias_q = spread_heads(jnp.broadcast_to(vec_ref[8:9, :], (8, C)))[0:1]
    bias_v = spread_heads(jnp.broadcast_to(vec_ref[9:10, :], (8, C)))[0:1]
    block_rows = 256
    spare = lax.broadcasted_iota(jnp.int32, (block_rows, 512), 1) & 127
    for index in range(PIX // block_rows):
        here = slice(block_rows * index, block_rows * index + block_rows)
        hidden = hidden_ref[here, :]
        value = jnp.dot(hidden, in_ref[:, 0:512], preferred_element_type=f32) + bias_q
        q_ref[here, :] = jnp.where(spare == HEAD, 1.0, value).astype(bf16)
        value = jnp.dot(hidden, in_ref[:, 512:1024], preferred_element_type=f32)
        valid = mask_ref[here, :]
        barred = jnp.where(valid > 0, 0.0, masked_score)
        barred = jnp.concatenate((barred, barred, barred, barred), axis=1)
        value = jnp.where(spare == HEAD, barred, value).astype(bf16)
        k_ref[here, :] = value
        kt_ref[:, here] = value.T
        value = jnp.dot(hidden, in_ref[:, 1024:1536], preferred_element_type=f32) + bias_v
        value = jnp.where((spare == HEAD) | (spare == HEAD + 1), 1.0, value).astype(bf16)
        v_ref[here, :] = value
        vt_ref[:, here] = value.T
        upt_ref[:, here] = lax.dot_general(
            weight_ref[...], cot_ref[here, :], ON_LAST, preferred_element_type=f32
        ).astype(bf16)
    attention_both(q_ref, k_ref, v_ref, kt_ref, vt_ref, upt_ref, mixt_ref, dqt_ref, dk_acc, dv_acc)
    dk_ref, dv_ref = k_ref, v_ref
    bias = vec_ref[10:11, :]
    for index in range(PIX // 128):
        here = slice(128 * index, 128 * index + 128)
        value = jnp.dot(mixt_ref[:, here].T, weight_ref[...], preferred_element_type=f32) + bias
        valid = wide_mask(mask_ref, 128 * index, 128)
        quarter, side = divmod(index, 2)
        terms_ref[quarter * C : quarter * C + C, 128 * side : 128 * side + 128] = (
            residual_ref[here, :] + value * valid
        ).T
    for quarter in range(4):
        out_ref[:, 256 * quarter : 256 * quarter + 256] = terms_ref[
            pl.ds(aligned(quarter * C + narrow * HALF, 16), HALF), :
        ].astype(bf16)
    heads_here = pl.ds(aligned(narrow * 256, 128), 256)
    terms = jnp.dot(mixt_ref[...], own_cot[...], preferred_element_type=f32)
    for head in range(HEADS):
        out_nat[HEAD * head : HEAD * head + HEAD, 0:256] = terms[128 * head : 128 * head + HEAD]
    terms = jnp.dot(
        dqt_ref[pl.ds(aligned(narrow * 256, 128), 256), :],
        hidden_ref[...],
        preferred_element_type=f32,
    )
    in_nat[:, 0:256] = join_heads(terms.T)
    for index, source in ((1, dk_ref), (2, dv_ref)):
        terms = lax.dot_general(
            hidden_ref[...], source[:, heads_here], ON_FIRST, preferred_element_type=f32
        )
        in_nat[:, 256 * index : 256 * index + 256] = join_heads(terms)
    ones = jnp.ones((8, PIX), bf16)
    sums = (
        lax.dot_general(ones, dqt_ref[...], ON_LAST, preferred_element_type=f32),
        jnp.dot(ones, dv_ref[...], preferred_element_type=f32),
    )
    mean, inverse, tally = stat_ref[0:1, :], stat_ref[1:2, :], stat_ref[2:3, :]
    gain = vec_ref[6:7, :]
    acc_shift, acc_gain = zero, zero
    for index in range(PIX // 256):
        here = slice(256 * index, 256 * index + 256)
        value = None
        for part, source in enumerate((dqt_ref[:, here].T, dk_ref[here, :], dv_ref[here, :])):
            term = lax.dot_general(
                source, in_ref[:, 512 * part : 512 * part + 512], ON_LAST,
                preferred_element_type=f32,
            )
            value = term if value is None else value + term
        value = value * wide_mask(mask_ref, 256 * index, 256)
        normed = (residual_ref[here, :] - mean) * inverse
        acc_shift = acc_shift + fold(value)
        acc_gain = acc_gain + fold(value * normed)
        direct_ref[here, :] = value
    shift_grad, gain_grad = total(acc_shift), total(acc_gain)
    first_mean = group_sum(gain * shift_grad) / tally
    second_mean = group_sum(gain * gain_grad) / tally

    def back(start, carry):
        valid = wide_mask(mask_ref, start, CHUNK)
        here = pl.ds(start, CHUNK)
        normed = (residual_ref[here, :] - mean) * inverse
        extra = (direct_ref[here, :] * gain - first_mean - normed * second_mean) * inverse
        value = (rows_ref[pl.ds(start + 8, CHUNK), :] + extra) * valid
        direct_ref[here, :] = value
        low = value.astype(bf16).astype(f32)
        rows_ref[pl.ds(start + 8, CHUNK), :] = low
        return carry + fold(low)

    bias_two = chunks(back, zero)
    write_taps(rows_ref, taps_ref)
    write_own(rows_ref, back_ref, narrow)
    vec_grad_ref[...] = jnp.zeros_like(vec_grad_ref)
    vec_grad_ref[5:6, :] = total(bias_two)
    vec_grad_ref[6:7, :] = gain_grad
    vec_grad_ref[7:8, :] = shift_grad
    for row, acc in ((8, sums[0]), (9, sums[1])):
        pair_one, pair_two = join_heads(acc[:, 0:256]), join_heads(acc[:, 256:512])
        turned = pltpu.roll(pair_two[:, 0:128], 64, 1)
        natural = jnp.concatenate(
            (
                pair_one[:, 0:128],
                jnp.where(lane(8) < 64, pair_one[:, 128:256], turned),
                jnp.where(lane(8) < 64, turned, pltpu.roll(pair_two[:, 128:256], 64, 1)),
            ),
            axis=1,
        )
        vec_grad_ref[row : row + 1, :] = natural[0:1]
    vec_grad_ref[10:11, :] = total(bias_out)


def unit_rows(grad, chip, core):
    return pl.ds(aligned(chip * 2 * grad + core * grad, 8), grad)


def middle_of_block(
    at, one_ref, stat_two_ref, turned_ref, mask_ref, vec_ref, embed_ref, own_ref, other_ref, *refs
):
    (
        out_ref, direct_ref, back_taps_ref, vec_grad_ref, film_rows_ref, kernel_ref, soft_all_ref,
        keep_ref, send_ref,
    ) = refs[8:17]
    (
        taps_ref, residual_ref, hidden_ref, stat_ref, soft_ref, film_ref, held_ref, sems, back_ref,
    ) = refs[17:26]
    attention_refs = refs[26:]
    in_nat, out_nat = attention_refs[0:2]
    rows_ref, terms_ref = attention_refs[-3:-1]
    units = Gathered(at, refs[0:8], held_ref, sems)
    place_conv(units, kernel_ref)
    place_film(units, film_ref)
    place_embeddings(units, soft_all_ref)
    film_to_third_norm(
        one_ref, stat_two_ref, turned_ref, mask_ref, vec_ref, embed_ref, kernel_ref, film_ref,
        taps_ref, residual_ref, hidden_ref, stat_ref, film_rows_ref, soft_ref, rows_ref,
    )
    place_attention(units, in_nat, out_nat)
    attention_body(
        at, hidden_ref, residual_ref, stat_ref, mask_ref, vec_ref, own_ref, other_ref,
        out_ref, direct_ref, back_taps_ref, back_ref, vec_grad_ref, *attention_refs,
    )
    for chip in range(8):
        for target, core in ((keep_ref, at[1]), (send_ref, 1 - at[1])):
            rows = unit_rows(24, chip, core)
            block = jnp.concatenate(
                [in_nat[rows, 256 * index : 256 * index + 256] for index in range(3)], axis=0
            )
            target[chip, 336:416, :] = pad_rows(block[:, 0:128], 80).astype(bf16)
            target[chip, 416:464, :] = pad_rows(pair_rows(block[:, 128:256], 40), 48).astype(bf16)
            block = out_nat[rows, 0:256]
            target[chip, 464:496, :] = pad_rows(block[:, 0:128], 32).astype(bf16)
            target[chip, 496:512, :] = pair_rows(block[:, 128:256], 16).astype(bf16)
    kernel_terms(taps_ref, back_ref, terms_ref)
    pack_units(terms_ref, at, keep_ref, send_ref)


def attention_plain(
    at, hidden_ref, residual_ref, stat_ref, mask_ref, vec_ref, own_ref, other_ref,
    in_given, out_given, out_ref, direct_ref, taps_ref, back_ref, vec_grad_ref,
    in_term_ref, out_term_ref, *refs,
):
    in_nat, out_nat = refs[0:2]
    in_nat[...] = in_given[...].astype(f32)
    out_nat[...] = out_given[...].astype(f32)
    attention_body(
        at, hidden_ref, residual_ref, stat_ref, mask_ref, vec_ref, own_ref, other_ref,
        out_ref, direct_ref, taps_ref, back_ref, vec_grad_ref, *refs,
    )
    in_term_ref[...] = in_nat[:, 0:768]
    out_term_ref[...] = out_nat[:, 0:256]


def pack_units(terms_ref, at, keep_ref, send_ref):
    for chip in range(8):
        for target, core in ((keep_ref, at[1]), (send_ref, 1 - at[1])):
            rows = unit_rows(ROWS, chip, core)
            target[chip, 0:224, :] = pad_rows(terms_ref[rows, 0:128], 224).astype(bf16)
            target[chip, 224:336, :] = pair_rows(terms_ref[rows, 128:256], 112).astype(bf16)


def conv_terms_plain(at, taps_ref, own_ref, terms_ref):
    kernel_terms(taps_ref, own_ref, terms_ref)


def second_back(at, *refs):
    taps_one_ref = refs[8]
    back_taps_ref, vec_grad_ref, keep_ref, send_ref = refs[-8:-4]
    grad_ref, rows_ref, back_ref, terms_ref = refs[-4:]
    second_back_body(at, *refs[:8], back_taps_ref, back_ref, vec_grad_ref, grad_ref, rows_ref)
    kernel_terms(taps_one_ref, back_ref, terms_ref)
    pack_units(terms_ref, at, keep_ref, send_ref)


def second_back_plain(at, *refs):
    second_back_body(at, *refs)


def second_back_body(
    at, taps_ref, kernel_ref, one_ref, stat_ref, film_rows_ref, mask_ref, vec_ref, vec_in_ref,
    back_taps_ref, back_ref, vec_grad_ref, grad_ref, rows_ref,
):
    def done(start, count, acc):
        grad_ref[pl.ds(start, count), :] = acc

    convolve_back(taps_ref, kernel_ref, done)
    mean, inverse, tally = stat_ref[0:1, :], stat_ref[1:2, :], stat_ref[2:3, :]
    gain, shift = vec_ref[3:4, :], vec_ref[4:5, :]
    scale, offset = film_rows_ref[0:1, :], film_rows_ref[1:2, :]
    zero = jnp.zeros((8, C), f32)

    def gather(start, carry):
        plain, with_normed = carry
        valid = wide_mask(mask_ref, start, CHUNK)
        here = pl.ds(start, CHUNK)
        normed = (one_ref[here, :] - mean) * inverse
        value = grad_ref[here, :] * valid * slope((normed * gain + shift) * valid * scale + offset)
        grad_ref[here, :] = value
        return (plain + fold(value), with_normed + fold(value * normed))

    plain, with_normed = chunks(gather, (zero, zero))
    plain, with_normed = total(plain), total(with_normed)
    gain_grad, shift_grad = scale * with_normed, scale * plain
    first_mean = group_sum(gain * shift_grad) / tally
    second_mean = group_sum(gain * gain_grad) / tally
    joint = scale * gain

    def back(start, carry):
        valid = wide_mask(mask_ref, start, CHUNK)
        here = pl.ds(start, CHUNK)
        normed = (one_ref[here, :] - mean) * inverse
        value = (grad_ref[here, :] * joint - first_mean - normed * second_mean) * inverse * valid
        low = value.astype(bf16).astype(f32)
        rows_ref[pl.ds(start + 8, CHUNK), :] = low
        return carry + fold(low)

    bias = chunks(back, zero)
    write_taps(rows_ref, back_taps_ref)
    write_own(rows_ref, back_ref, at[0])
    vec_grad_ref[...] = vec_in_ref[...]
    vec_grad_ref[2:3, :] = total(bias)
    vec_grad_ref[3:4, :] = gain_grad
    vec_grad_ref[4:5, :] = shift_grad
    vec_grad_ref[11:12, :] = (gain * with_normed + shift * plain).astype(bf16).astype(f32)
    vec_grad_ref[12:13, :] = plain.astype(bf16).astype(f32)


def first_back(
    at, taps_ref, kernel_ref, turned_ref, stat_ref, direct_ref, mask_ref, vec_ref, vec_in_ref, *refs,
):
    out_ref, vec_grad_ref, grad_ref, turn_ref = refs[-4:]

    def done(start, count, acc):
        grad_ref[pl.ds(start, count), :] = acc

    convolve_back(taps_ref, kernel_ref, done)
    mean, inverse, tally = stat_ref[0:1, :], stat_ref[1:2, :], stat_ref[2:3, :]
    gain, shift = vec_ref[0:1, :], vec_ref[1:2, :]
    zero = jnp.zeros((8, C), f32)

    def gather(start, carry):
        plain, with_normed = carry
        valid = wide_mask(mask_ref, start, CHUNK)
        here = pl.ds(start, CHUNK)
        normed = (turned_ref[here, :].astype(f32) - mean) * inverse
        value = grad_ref[here, :] * slope((normed * gain + shift) * valid) * valid
        grad_ref[here, :] = value
        return (plain + fold(value), with_normed + fold(value * normed))

    plain, with_normed = chunks(gather, (zero, zero))
    shift_grad, gain_grad = total(plain), total(with_normed)
    first_mean = group_sum(gain * shift_grad) / tally
    second_mean = group_sum(gain * gain_grad) / tally
    for index in range(PIX // 128):
        here = slice(128 * index, 128 * index + 128)
        valid = wide_mask(mask_ref, 128 * index, 128)
        normed = (turned_ref[here, :].astype(f32) - mean) * inverse
        value = (grad_ref[here, :] * gain - first_mean - normed * second_mean) * inverse * valid
        turn_ref[:, here] = (value + direct_ref[here, :]).T
    out_ref[...] = turn_ref[pl.ds(aligned(at[0] * HALF, 16), HALF), :].astype(bf16)
    place = lax.broadcasted_iota(jnp.int32, (16, 1), 0)
    rows = jnp.where(place == 0, gain_grad, jnp.where(place == 1, shift_grad, vec_in_ref[...]))
    vec_grad_ref[...] = own_half(rows, at[0])


def add_cores(at, keep_ref, back_ref, own_ref, across_ref):
    for depth in range(4):
        for target, side in ((own_ref, at[2]), (across_ref, 1 - at[2])):
            chip = depth * 2 + side
            target[depth] = (keep_ref[chip].astype(f32) + back_ref[chip].astype(f32)).astype(bf16)


def add_sides(at, own_ref, back_ref, mine_ref, *across):
    for step, target in enumerate((mine_ref,) + across):
        depth = at[3] ^ step
        target[...] = (own_ref[depth].astype(f32) + back_ref[depth].astype(f32)).astype(bf16)


def add_cores_depth(at, keep_ref, back_ref, *targets):
    for step, target in enumerate(targets):
        for side in (0, 1):
            chip = (at[3] ^ step) * 2 + side
            target[side] = (keep_ref[chip].astype(f32) + back_ref[chip].astype(f32)).astype(bf16)


def add_depths(at, *refs):
    mine_ref, across_ref = refs[4:6]
    for target, side in ((mine_ref, at[2]), (across_ref, 1 - at[2])):
        terms = [ref[side].astype(f32) for ref in refs[0:4]]
        target[...] = (terms[0] + terms[1] + terms[2] + terms[3]).astype(bf16)


def adam_update(weight, gradient, moment, square, step_rate):
    moment_new = beta_one * moment + (1.0 - beta_one) * gradient
    square_new = beta_two * square + (1.0 - beta_two) * gradient * gradient
    ratio = (
        moment_new
        / (1.0 - beta_one**STEP)
        / (jnp.sqrt(square_new / (1.0 - beta_two**STEP)) + adam_eps)
    )
    return (weight - step_rate * (ratio + decay_rate * weight), moment_new, square_new)


def unpair_rows(block, rows):
    top = block.shape[0]
    return jnp.concatenate((block, pltpu.roll(block, 64, 1)[0 : rows - top]), axis=0)


def adam_into(gradient, given, outs, rate, where):
    weight, moment, square = (ref[where] for ref in given)
    results = adam_update(weight, gradient, moment, square, rate)
    for out, value in zip(outs, (gradient,) + results):
        out[where] = value


def conv_adam(parts, weight_ref, moment_ref, square_ref, outs, rate):
    def summed(start, stop):
        return sum(part[start:stop, :].astype(f32) for part in parts[1:]) + parts[0][
            start:stop, :
        ].astype(f32)

    low = summed(0, 224)[0:ROWS]
    high = unpair_rows(summed(224, 336), ROWS)
    gradient = jnp.concatenate((low, high[:, 0:64]), axis=1).T
    results = adam_update(weight_ref[...], gradient, moment_ref[...], square_ref[...], rate)
    for out, value in zip(outs, (gradient,) + results):
        out[...] = value
    return summed


def finish_first(at, *refs):
    conv_adam(refs[0:2], *refs[2:5], refs[5:9], step_rates()[0])


def finish_second(at, *refs):
    given, results = refs[4:13], refs[13:]
    summed = conv_adam(refs[0:4], *given[0:3], results[0:4], step_rates()[1])
    gradient = jnp.concatenate(
        (summed(336, 416)[0:72], unpair_rows(summed(416, 464)[0:40], 72)[:, 0:64]), axis=1
    )
    for index in range(3):
        adam_into(
            gradient[24 * index : 24 * index + 24], given[3:6], results[4:8], step_rates()[3], index
        )
    gradient = jnp.concatenate(
        (summed(464, 496)[0:24], unpair_rows(summed(496, 512), 24)[:, 0:64]), axis=1
    )
    adam_into(gradient, given[6:9], results[8:12], step_rates()[4], Ellipsis)


def finish_small(at, own_ref, one_ref, two_ref, three_ref, soft_ref, *refs):
    wide = (at[3] * 2 + at[2]) * 2 + at[1]
    given, results, grad_ref = refs[0:6], refs[6:14], refs[14]
    sums, films = None, []
    for ref in (own_ref, one_ref, two_ref, three_ref):
        rows = ref[...]
        sums = rows[0:16] if sums is None else sums + rows[0:16]
        for start in range(16, 24, 2):
            films.append(
                jnp.concatenate((rows[start : start + 1], rows[start + 1 : start + 2]), axis=1)
            )
    adam_into(sums[0:13, 0:HALF], given[0:3], results[0:4], step_rates()[5], Ellipsis)
    grad_ref[...] = lax.dot_general(
        soft_ref[...].astype(bf16), jnp.concatenate(films, axis=0).astype(bf16), ON_FIRST,
        preferred_element_type=f32,
    )
    here = pl.ds(aligned(wide * 48, 8), 48)
    for index in (0, 1):
        gradient = grad_ref[here, 256 * index : 256 * index + HALF]
        adam_into(
            gradient, given[3:6], results[4:8], step_rates()[2], (slice(None), index, slice(None))
        )


def along_depth(unit, wide):
    return [unit] + [
        lax.ppermute(unit, "wide", [(i, i ^ (4 * step)) for i in range(wide)])
        for step in (1, 2, 3)
    ]


def along_plane(stack, wide):
    diagonal = [(2 * i + x, 2 * (i ^ 2) + 1 - x) for i in range(wide) for x in (0, 1)]
    return [
        stack,
        lax.ppermute(stack, "wide", [(i, i ^ 2) for i in range(wide)]),
        lax.ppermute(stack, "narrow", [(0, 1), (1, 0)]),
        lax.ppermute(stack, ("wide", "narrow"), diagonal),
    ]


def both_cores(parts, wide):
    return list(parts) + [
        lax.ppermute(v, "wide", [(i, i ^ 1) for i in range(wide)]) for v in parts
    ]


def tie(values, after, scalars):
    ins = [pltpu.with_memory_space_constraint(v, pltpu.HBM) for v in (*values, *after)]
    return pl.pallas_call(
        pass_on,
        out_shape=tuple(shaped(v.shape, v.dtype) for v in values),
        in_specs=[pl.BlockSpec(memory_space=pltpu.SMEM)]
        + [pl.BlockSpec(memory_space=pltpu.HBM) for _ in ins],
        out_specs=tuple(pl.BlockSpec(memory_space=pltpu.HBM) for _ in values),
        input_output_aliases={index + 1: index for index in range(len(values))},
    )(scalars, *ins)


def add_core_units(keep, send, scalars, wide):
    back = lax.ppermute(send, "wide", [(i, i ^ 1) for i in range(wide)])
    four = shaped((4, keep.shape[1], 128), bf16)
    return call(add_cores, (four, four), (keep, back), scalars)


def add_far_units(own, across, scalars, wide):
    back = lax.ppermute(across, "wide", [(i, i ^ 2) for i in range(wide)])
    one = shaped((own.shape[1], 128), bf16)
    parts = call(add_sides, (one,) * 4, (own, back), scalars)
    return [parts[0]] + [
        lax.ppermute(parts[step], "wide", [(i, i ^ (4 * step)) for i in range(wide)])
        for step in (1, 2, 3)
    ]


def apart_along_depth(parts, wide):
    return [parts[0]] + [
        lax.ppermute(parts[step], "wide", [(i, i ^ (4 * step)) for i in range(wide)])
        for step in (1, 2, 3)
    ]


def pack_vectors(at, here_ref, core_ref, side_ref, out_ref):
    samples = (here_ref[...], core_ref[...], side_ref[0], side_ref[1])
    out_ref[0:16, :] = samples[0] + samples[1] + samples[2] + samples[3]
    for index, rows in enumerate(samples):
        out_ref[16 + 2 * index : 18 + 2 * index, :] = rows[11:13]


def gather_vectors(rows, scalars, wide):
    core = lax.ppermute(rows, "wide", [(i, i ^ 1) for i in range(wide)])
    side = lax.ppermute(jnp.stack((rows, core)), "wide", [(i, i ^ 2) for i in range(wide)])
    (packed,) = call(pack_vectors, (shaped((24, 256), f32),), (rows, core, side), scalars)
    return along_depth(packed, wide)


def per_device(
    features,
    embedding,
    valid_mask,
    cotangent,
    conv_first,
    conv_first_moment,
    conv_first_square,
    conv_second,
    conv_second_moment,
    conv_second_square,
    film_weight,
    film_weight_moment,
    film_weight_square,
    attend_in,
    attend_in_moment,
    attend_in_square,
    attend_out,
    attend_out_moment,
    attend_out_square,
    vectors,
    vectors_moment,
    vectors_square,
):
    wide = lax.axis_size("wide")
    unit_path = wide == 16
    narrow_at = lax.axis_index("narrow").astype(jnp.int32)
    wide_at = lax.axis_index("wide").astype(jnp.int32)
    scalars = jnp.stack((narrow_at, wide_at & 1, (wide_at >> 1) & 1, wide_at >> 2))
    flip = [(0, 1), (1, 0)]
    plane = shaped((PIX, C), f32)
    low_plane = shaped((PIX, C), bf16)
    taps = shaped((PADDED, 3 * C), bf16)
    back_half = shaped((PADDED, 256), bf16)
    kernel = shaped((9 * C, C), bf16)
    stats = shaped((8, C), f32)
    vec_rows = shaped((16, C), f32)
    half_plane = shaped((HALF, PIX), bf16)
    rows_scratch = pltpu.VMEM((PIX + 16, C), f32)

    mask = jnp.broadcast_to(valid_mask[0].astype(f32)[:, None], (PIX, 128))
    own_features = features[0]
    own_cotangent = cotangent[0]
    (exchange,) = call(
        pack_exchange,
        (shaped((2 * HALF + 16, PIX), bf16),),
        (own_features, vectors, own_cotangent),
        scalars,
    )
    exchanged = lax.ppermute(exchange, "narrow", flip)

    if unit_path:
        weights = (
            jnp.transpose(conv_first),
            jnp.transpose(conv_second),
            film_weight,
            jnp.transpose(attend_in, (1, 0, 2)),
            attend_out,
        )
        (unit,) = call(
            pack_weights,
            (shaped((FIRST_ROWS + SECOND_ROWS, 128), bf16),),
            (embedding,),
            scalars,
            tuple(pltpu.VMEM(v.shape, f32) for v in weights) + (pltpu.SemaphoreType.DMA((5,)),),
            far=weights,
        )
        first_stack, second_stack = call(
            stack_all,
            tuple(shaped((4, rows, 128), bf16) for rows in (FIRST_ROWS, SECOND_ROWS)),
            along_depth(unit, wide),
            scalars,
        )
        first_units = both_cores(along_plane(first_stack, wide), wide)
    else:

        def whole(array, axis):
            array = lax.all_gather(array.astype(bf16), "wide", axis=0, tiled=True)
            return lax.all_gather(array, "narrow", axis=axis, tiled=True)

        first_full, second_full = whole(conv_first, 1), whole(conv_second, 1)
        film_full = whole(film_weight, 2).reshape(EMB, 2 * C)
        in_full = whole(attend_in, 2).reshape(C, 3 * C)
        out_full = whole(attend_out, 1)

    turned, taps_one, stat_one, vecs = call(
        first_norm,
        (low_plane, taps, stats, vec_rows),
        (own_features, exchanged, mask, vectors),
        scalars,
        (rows_scratch, pltpu.VMEM((PIX, C), f32)),
        far=(first_stack,) if unit_path else (),
    )
    if unit_path:
        second_parts = along_plane(second_stack, wide)
        out_one, kernel_one, stat_two = call(
            first_conv,
            (plane, kernel, stats),
            (taps_one, mask, vecs),
            scalars,
            (
                pltpu.VMEM((8, 4, FIRST_ROWS, 128), bf16),
                pltpu.SemaphoreType.DMA((8,)),
            ),
            far=(*first_units, second_stack),
        )
        arrived = [tie((part,), (stat_two,), scalars)[0] for part in second_parts[1:4]]
        second_units = both_cores([second_parts[0], *arrived], wide)
    else:
        kernel_one = first_full
        out_one, stat_two = call(
            first_conv_plain, (plane, stats), (taps_one, mask, vecs, kernel_one), scalars
        )
    common = (out_one, stat_two, turned, mask, vecs, embedding)
    attention_scratch = (
        pltpu.VMEM((C, 3 * C), f32),
        pltpu.VMEM((C, C), f32),
        pltpu.VMEM((C, 1536), bf16),
        pltpu.VMEM((512, C), bf16),
        *([pltpu.VMEM((PIX, 512), bf16)] * 3),
        *([pltpu.VMEM((512, PIX), bf16)] * 5),
        pltpu.VMEM((PIX, 128), f32),
        pltpu.VMEM((PIX, 128), f32),
        pltpu.VMEM((PIX, C), bf16),
        rows_scratch,
        pltpu.VMEM((9 * C, 256), f32),
        pltpu.VMEM((PIX, 256), bf16),
    )
    back_scratch = (pltpu.VMEM((PIX, C), f32), rows_scratch)
    terms_scratch = (pltpu.VMEM((PADDED, 256), bf16), pltpu.VMEM((9 * C, 256), f32))
    if unit_path:
        units = shaped((8, 512, 128), bf16)
        (
            output, direct, taps_back, vec_grad, film_rows, kernel_two, soft_all, keep, send,
        ) = call(
            middle_of_block,
            (
                half_plane, plane, taps, vec_rows, stats, kernel, shaped((16, EMB), f32),
                units, units,
            ),
            common + (own_cotangent, exchanged),
            scalars,
            (
                pltpu.VMEM((PADDED, 3 * C), bf16),
                pltpu.VMEM((PIX, C), f32),
                pltpu.VMEM((PIX, C), bf16),
                pltpu.VMEM((8, C), f32),
                pltpu.VMEM((16, EMB), f32),
                pltpu.VMEM((EMB, 2 * C), bf16),
                pltpu.VMEM((8, 4, SECOND_ROWS, 128), bf16),
                pltpu.SemaphoreType.DMA((8,)),
                pltpu.VMEM((PADDED, 256), bf16),
                *attention_scratch,
            ),
            far=second_units,
            flops=4 * 10**10,
        )
        own_second, across_second = add_core_units(keep, send, scalars, wide)
        units = shaped((8, 336, 128), bf16)
        taps_back_one, vec_grad, keep, send = call(
            second_back,
            (taps, vec_rows, units, units),
            (
                taps_back, kernel_two, out_one, stat_two, film_rows, mask, vecs, vec_grad,
                taps_one,
            ),
            scalars,
            back_scratch + terms_scratch,
            far=(across_second,),
        )
        parts_second = add_far_units(own_second, across_second, scalars, wide)
        back = lax.ppermute(send, "wide", [(i, i ^ 1) for i in range(wide)])
        sums_first = call(
            add_cores_depth, (shaped((2, FIRST_ROWS, 128), bf16),) * 4, (keep, back), scalars
        )
        one = shaped((FIRST_ROWS, 128), bf16)
        mine_first, across_first = call(
            add_depths, (one, one), apart_along_depth(sums_first, wide), scalars
        )
        parts_first = (
            mine_first,
            lax.ppermute(across_first, "wide", [(i, i ^ 2) for i in range(wide)]),
        )
        started = (sums_first[1],)
    else:
        kernel_two = second_full
        taps_two, residual, hidden, stat_three, film_rows = call(
            second_conv_plain,
            (taps, plane, low_plane, stats, stats),
            common + (kernel_two, film_full),
            scalars,
            (pltpu.VMEM((16, EMB), f32), rows_scratch),
        )
        output, direct, taps_back, back_two, vec_grad, in_term, out_term = call(
            attention_plain,
            (
                half_plane, plane, taps, back_half, vec_rows,
                shaped((C, 768), f32), shaped((C, 256), f32),
            ),
            (
                hidden, residual, stat_three, mask, vecs, own_cotangent, exchanged,
                in_full, out_full,
            ),
            scalars,
            attention_scratch,
        )
        (second_term,) = call(
            conv_terms_plain, (shaped((9 * C, 256), f32),), (taps_two, back_two), scalars
        )
        taps_back_one, back_one, vec_grad = call(
            second_back_plain,
            (taps, back_half, vec_rows),
            (taps_back, kernel_two, out_one, stat_two, film_rows, mask, vecs, vec_grad),
            scalars,
            back_scratch,
        )
        (first_term,) = call(
            conv_terms_plain, (shaped((9 * C, 256), f32),), (taps_one, back_one), scalars
        )
        started = ()
    input_gradient, vec_half = call(
        first_back,
        (half_plane, shaped((16, 256), f32)),
        (taps_back_one, kernel_one, turned, stat_one, direct, mask, vecs, vec_grad),
        scalars,
        (pltpu.VMEM((PIX, C), f32), pltpu.VMEM((C, PIX), f32)),
        far=started,
    )
    if unit_path:
        vec_shape, film_shape = shaped((13, HALF), f32), shaped(film_weight.shape, f32)
        small = call(
            finish_small,
            (vec_shape,) * 4 + (film_shape,) * 4,
            (
                *gather_vectors(vec_half, scalars, wide),
                soft_all,
                vectors,
                vectors_moment,
                vectors_square,
                film_weight,
                film_weight_moment,
                film_weight_square,
            ),
            scalars,
            (pltpu.VMEM((EMB, 512), f32),),
        )
        vec_results, film_results = small[:4], small[4:]
    else:
        vec_half = vec_half[:13, :HALF]
        vec_sum = lax.psum(vec_half, "wide")
        soft = jax.nn.silu(embedding.astype(f32)).astype(bf16)
        soft_all = lax.all_gather(soft, "wide", axis=0, tiled=True)
        rows_here = film_weight.shape[0]
        soft_here = lax.dynamic_slice_in_dim(soft_all, wide_at * rows_here, rows_here, axis=1)
        film_all = lax.all_gather(vec_half[11:13].astype(bf16)[None], "wide", axis=0, tiled=True)
        film_gradient = jnp.einsum("se,stj->etj", soft_here, film_all, preferred_element_type=f32)

    rates = step_rates()
    shard = shaped((HALF, ROWS), f32)

    def turned_shards(*shards):
        return tuple(jnp.transpose(v) for v in shards)

    if unit_path:
        in_shape, out_shape = shaped((3, 24, HALF), f32), shaped((24, HALF), f32)
        in_given = tuple(
            jnp.transpose(v, (1, 0, 2)) for v in (attend_in, attend_in_moment, attend_in_square)
        )
        second_results = call(
            finish_second,
            (shard,) * 4 + (in_shape,) * 4 + (out_shape,) * 4,
            (
                *parts_second,
                *turned_shards(conv_second, conv_second_moment, conv_second_square),
                *in_given,
                attend_out,
                attend_out_moment,
                attend_out_square,
            ),
            scalars,
        )
        in_results = tuple(jnp.transpose(v, (1, 0, 2)) for v in second_results[4:8])
        out_results = second_results[8:12]
        second_results = turned_shards(*second_results[:4])
        first_results = call(
            finish_first,
            (shard,) * 4,
            (*parts_first, *turned_shards(conv_first, conv_first_moment, conv_first_square)),
            scalars,
        )
        first_results = turned_shards(*first_results)
    else:

        def scatter(term):
            return lax.psum_scatter(term, "wide", scatter_dimension=0, tiled=True)

        first_gradient = scatter(first_term[:, :HALF])
        second_gradient = scatter(second_term[:, :HALF])
        in_gradient = scatter(in_term.reshape(C, 3, 256)[:, :, :HALF])
        out_gradient = scatter(out_term[:, :HALF])

        def finish(weight, gradient, moment, square, rate):
            return (gradient,) + adam_update(weight, gradient, moment, square, rate)

        first_results = finish(
            conv_first, first_gradient, conv_first_moment, conv_first_square, rates[0]
        )
        second_results = finish(
            conv_second, second_gradient, conv_second_moment, conv_second_square, rates[1]
        )
        film_results = finish(
            film_weight, film_gradient, film_weight_moment, film_weight_square, rates[2]
        )
        in_results = finish(
            attend_in, in_gradient, attend_in_moment, attend_in_square, rates[3]
        )
        out_results = finish(
            attend_out, out_gradient, attend_out_moment, attend_out_square, rates[4]
        )
        vec_results = finish(vectors, vec_sum, vectors_moment, vectors_square, rates[5])

    return (
        output[None],
        input_gradient[None],
        *first_results,
        *second_results,
        *film_results,
        *in_results,
        *out_results,
        *vec_results,
    )


def solution(mesh):
    in_specs = (
        P("wide", "narrow", None),
        P("wide", None),
        P("wide", None),
        P("wide", "narrow", None),
        P("wide", "narrow"),
        P("wide", "narrow"),
        P("wide", "narrow"),
        P("wide", "narrow"),
        P("wide", "narrow"),
        P("wide", "narrow"),
        P("wide", None, "narrow"),
        P("wide", None, "narrow"),
        P("wide", None, "narrow"),
        P("wide", None, "narrow"),
        P("wide", None, "narrow"),
        P("wide", None, "narrow"),
        P("wide", "narrow"),
        P("wide", "narrow"),
        P("wide", "narrow"),
        P(None, "narrow"),
        P(None, "narrow"),
        P(None, "narrow"),
    )
    out_specs = (
        P("wide", "narrow", None),
        P("wide", "narrow", None),
        P("wide", "narrow"),
        P("wide", "narrow"),
        P("wide", "narrow"),
        P("wide", "narrow"),
        P("wide", "narrow"),
        P("wide", "narrow"),
        P("wide", "narrow"),
        P("wide", "narrow"),
        P("wide", None, "narrow"),
        P("wide", None, "narrow"),
        P("wide", None, "narrow"),
        P("wide", None, "narrow"),
        P("wide", None, "narrow"),
        P("wide", None, "narrow"),
        P("wide", None, "narrow"),
        P("wide", None, "narrow"),
        P("wide", "narrow"),
        P("wide", "narrow"),
        P("wide", "narrow"),
        P("wide", "narrow"),
        P(None, "narrow"),
        P(None, "narrow"),
        P(None, "narrow"),
        P(None, "narrow"),
    )
    return jax.shard_map(
        per_device, mesh=mesh, in_specs=in_specs, out_specs=out_specs, check_vma=False
    )
```

```python
import jax
import jax.numpy as jnp
from jax import lax
from jax.experimental import pallas as pl
from jax.experimental.pallas import tpu as pltpu
from jax.sharding import PartitionSpec as P

C = 384
HEADS = 4
GROUPS = 32
EMB = 768
SIDE = 32
STEP = 10
PIX = SIDE * SIDE
HALF = C // 2
PADDED = PIX + 2 * SIDE
HEAD = C // HEADS
ROWS = 216
CHUNK = 64

beta_one = 0.9
beta_two = 0.999
adam_eps = 1e-08
decay_rate = 0.01
norm_eps = 1e-05
masked_score = -1e30
score_scale = HEAD ** (-0.5)
exponent_scale = score_scale * 1.4426950408889634

f32 = jnp.float32
bf16 = jnp.bfloat16
ON_LAST = (((1,), (1,)), ((), ()))
ON_FIRST = (((0,), (0,)), ((), ()))
VMEM_BYTES = 46 * 1024 * 1024


def step_rates():
    return (
        2.0 * (9 * C) ** (-0.5),
        2.0 * (9 * C) ** (-0.5),
        2.0 * EMB ** (-0.5),
        2.0 * C ** (-0.5),
        2.0 * (C // 64) ** (-0.5),
        0.5,
    )


def spec():
    return pl.BlockSpec(memory_space=pltpu.VMEM)


def call(body, outs, ins, scalars, scratch=(), far=(), aliases=None, flops=0):
    far = tuple(pltpu.with_memory_space_constraint(v, pltpu.HBM) for v in far)
    ins = tuple(ins) + far
    limit = VMEM_BYTES if body in (middle_of_block, attention_plain) else VMEM_BYTES // 3
    return pl.pallas_call(
        body,
        out_shape=tuple(outs),
        in_specs=[pl.BlockSpec(memory_space=pltpu.SMEM)]
        + [spec() for _ in ins[: len(ins) - len(far)]]
        + [pl.BlockSpec(memory_space=pltpu.HBM) for _ in far],
        out_specs=tuple(spec() for _ in outs),
        scratch_shapes=list(scratch),
        input_output_aliases=aliases or {},
        compiler_params=pltpu.CompilerParams(vmem_limit_bytes=limit),
        cost_estimate=pl.CostEstimate(flops=flops, bytes_accessed=1024, transcendentals=0),
    )(scalars, *ins)


def shaped(shape, kind):
    return jax.ShapeDtypeStruct(shape, kind)


def aligned(value, by):
    return pl.multiple_of(value, by)


def wide_mask(mask_ref, start, count):
    part = mask_ref[pl.ds(start, count), :]
    return jnp.concatenate((part, part, part), axis=1)


def group_sum(row):
    first = (lax.broadcasted_iota(jnp.int32, (C, C), 0) * 5462) >> 16
    second = (lax.broadcasted_iota(jnp.int32, (C, C), 1) * 5462) >> 16
    member = jnp.where(first == second, 1.0, 0.0).astype(f32)
    spread = jnp.broadcast_to(row, (8, C))
    return jnp.dot(
        spread, member, preferred_element_type=f32, precision=lax.Precision.HIGHEST
    )[0:1]


def fold(block):
    return jnp.sum(block.reshape(block.shape[0] // 8, 8, block.shape[1]), axis=0)


def total(acc):
    return jnp.sum(acc, axis=0, keepdims=True)


def chunks(step, init):
    def body(index, carry):
        return step(aligned(index * CHUNK, CHUNK), carry)

    return lax.fori_loop(0, PIX // CHUNK, body, init, unroll=2)


def norm_stats(source_ref, mask_ref):
    zero = jnp.zeros((8, C), f32)

    def first(start, carry):
        sums, count = carry
        valid = wide_mask(mask_ref, start, CHUNK)
        return (sums + fold(source_ref[pl.ds(start, CHUNK), :] * valid), count + fold(valid))

    sums, count = chunks(first, (zero, zero))
    tally = total(count) * float(C // GROUPS)
    mean = group_sum(total(sums)) / tally

    def second(start, carry):
        valid = wide_mask(mask_ref, start, CHUNK)
        centred = source_ref[pl.ds(start, CHUNK), :] - mean
        return carry + fold(centred * centred * valid)

    variance = group_sum(total(chunks(second, zero))) / tally
    return mean, lax.rsqrt(variance + norm_eps), tally


def keep_stats(stat_ref, mean, inverse, tally):
    stat_ref[0:1, :] = mean
    stat_ref[1:2, :] = inverse
    stat_ref[2:3, :] = tally


def column_index(count):
    return lax.broadcasted_iota(jnp.int32, (count, 1), 0) & (SIDE - 1)


def write_taps(rows_ref, taps_ref):
    blank = jnp.zeros((SIDE, 3 * C), bf16)
    taps_ref[0:SIDE, :] = blank
    taps_ref[SIDE + PIX : PADDED, :] = blank
    column = column_index(CHUNK)
    for index in range(PIX // CHUNK):
        start = index * CHUNK
        here = pl.ds(SIDE + start, CHUNK)
        left = rows_ref[pl.ds(7 + start, CHUNK), :]
        right = rows_ref[pl.ds(9 + start, CHUNK), :]
        taps_ref[here, 0:C] = jnp.where(column == 0, 0.0, left).astype(bf16)
        taps_ref[here, C : 2 * C] = rows_ref[pl.ds(8 + start, CHUNK), :].astype(bf16)
        taps_ref[here, 2 * C : 3 * C] = jnp.where(column == SIDE - 1, 0.0, right).astype(bf16)


def lane(count):
    return lax.broadcasted_iota(jnp.int32, (count, 128), 1)


def own_half(block, narrow):
    one, two, three = block[:, 0:128], block[:, 128:256], block[:, 256:384]
    turned_two, turned_three = pltpu.roll(two, 64, 1), pltpu.roll(three, 64, 1)
    upper = jnp.where(lane(block.shape[0]) < 64, turned_two, turned_three)
    return jnp.concatenate(
        (jnp.where(narrow == 0, one, upper), jnp.where(narrow == 0, two, turned_three)), axis=1
    )


def write_own(rows_ref, own_ref, narrow):
    blank = jnp.zeros((SIDE, 256), bf16)
    own_ref[0:SIDE, :] = blank
    own_ref[SIDE + PIX : PADDED, :] = blank
    for index in range(PIX // CHUNK):
        start = index * CHUNK
        block = rows_ref[pl.ds(8 + start, CHUNK), :]
        own_ref[pl.ds(SIDE + start, CHUNK), :] = own_half(block, narrow).astype(bf16)


def convolve(taps_ref, kernel_ref, done, block=512):
    for index in range(PIX // block):
        start = index * block
        acc = None
        for tap in range(3):
            part = jnp.dot(
                taps_ref[pl.ds(start + SIDE * tap, block), :],
                kernel_ref[tap * 3 * C : (tap + 1) * 3 * C, :],
                preferred_element_type=f32,
            )
            acc = part if acc is None else acc + part
        done(start, block, acc)


def convolve_back(taps_ref, kernel_ref, done, block=512):
    for index in range(PIX // block):
        start = index * block
        acc = None
        for tap in range(9):
            tap_row, tap_col = tap // 3, tap % 3
            flipped = 8 - tap
            part = lax.dot_general(
                taps_ref[pl.ds(start + SIDE * tap_row, block), tap_col * C : (tap_col + 1) * C],
                kernel_ref[flipped * C : (flipped + 1) * C, :],
                ON_LAST,
                preferred_element_type=f32,
            )
            acc = part if acc is None else acc + part
        done(start, block, acc)


def kernel_terms(taps_ref, own_ref, terms_ref):
    for tap_col in range(3):
        for tap_row in range(3):
            tap = 3 * tap_row + tap_col
            first = 2 * SIDE - SIDE * tap_row
            terms_ref[tap * C : (tap + 1) * C, :] = lax.dot_general(
                taps_ref[SIDE : SIDE + PIX, tap_col * C : (tap_col + 1) * C],
                own_ref[first : first + PIX, :],
                ON_FIRST,
                preferred_element_type=f32,
            )


def slope(value):
    logistic = lax.logistic(value)
    return logistic * (1.0 + value * (1.0 - logistic))


def tile_parts(block, narrow):
    rows = block.shape[0]
    one = block[:, 0:128]
    two = jnp.concatenate((block[:, 128:192], jnp.zeros((rows, 64), f32)), axis=1)
    turned = jnp.where(lane(rows) < 64, pltpu.roll(one, 64, 1), pltpu.roll(two, 64, 1))
    return jnp.where(narrow == 0, one, turned), jnp.where(narrow == 0, two, one)


def pair_rows(block, top):
    rows = block.shape[0]
    low = block[top:rows]
    if rows < 2 * top:
        low = jnp.concatenate((low, jnp.zeros((2 * top - rows, 128), f32)), axis=0)
    return jnp.where(lane(top) < 64, block[0:top], pltpu.roll(low, 64, 1))


def pad_rows(block, rows):
    if block.shape[0] == rows:
        return block
    return jnp.concatenate((block, jnp.zeros((rows - block.shape[0], block.shape[1]), f32)), axis=0)


def middle(first, second, top, rows):
    one = jnp.where(lane(top) < 64, first, pltpu.roll(second, 64, 1))
    two = jnp.where(lane(top) < 64, pltpu.roll(first, 64, 1), second)
    return jnp.concatenate((one, two[0 : rows - top]), axis=0)


def pack_exchange(at, features_ref, vec_ref, cot_ref, out_ref):
    out_ref[HALF + 16 : 2 * HALF + 16, :] = cot_ref[...]
    out_ref[0:HALF, :] = features_ref[...]
    vec = jnp.concatenate((vec_ref[...], jnp.zeros((3, HALF), f32)), axis=0)
    coarse = vec.astype(bf16)
    out_ref[HALF : HALF + 16, :] = jnp.zeros((16, PIX), bf16)
    out_ref[HALF : HALF + 16, 0:HALF] = coarse
    out_ref[HALF : HALF + 16, 256 : 256 + HALF] = (vec - coarse.astype(f32)).astype(bf16)


FIRST_ROWS = 336
FILM_AT, FILM_SHARED, EMBED_AT, IN_AT, IN_SHARED, OUT_AT, OUT_SHARED, SECOND_ROWS = 336, 432, 480, 496, 576, 624, 656, 672


def stack_all(at, *refs):
    first_ref, second_ref = refs[4:6]
    for step in range(4):
        first_ref[step] = refs[step][0:FIRST_ROWS, :]
        second_ref[step] = refs[step][FIRST_ROWS : FIRST_ROWS + SECOND_ROWS, :]


def pass_on(at, *refs):
    pass


def put_rows(out_ref, start, block):
    rows = -(-block.shape[0] // 16) * 16
    out_ref[start : start + rows, :] = pad_rows(block, rows).astype(bf16)


def pack_weights(at, embed_ref, *refs):
    unit_ref, first_ref, second_ref, film_ref, in_ref, out_ref, sems = refs[5:]
    narrow = at[0]
    copies = [
        pltpu.make_async_copy(source, target, sems.at[index])
        for index, (source, target) in enumerate(
            zip(refs[0:5], (first_ref, second_ref, film_ref, in_ref, out_ref))
        )
    ]
    for copy in copies:
        copy.start()
    embed = embed_ref[...].astype(f32)
    put_rows(
        unit_ref,
        FIRST_ROWS + EMBED_AT,
        jnp.concatenate([embed[:, 128 * i : 128 * i + 128] for i in range(EMB // 128)], axis=0),
    )
    copies[0].wait()
    part, shared = tile_parts(first_ref[...].T, narrow)
    put_rows(unit_ref, 0, part)
    put_rows(unit_ref, 224, pair_rows(shared, 112))
    for copy in copies[1:]:
        copy.wait()
    for block, start, shared_start, top in (
        (second_ref[...].T, 0, 224, 112),
        (
            jnp.concatenate((film_ref[:, 0, :], film_ref[:, 1, :]), axis=0),
            FILM_AT, FILM_SHARED, 48,
        ),
        (jnp.concatenate((in_ref[0], in_ref[1], in_ref[2]), axis=0), IN_AT, IN_SHARED, 40),
        (out_ref[...], OUT_AT, OUT_SHARED, 16),
    ):
        part, shared = tile_parts(block, narrow)
        put_rows(unit_ref, FIRST_ROWS + start, part)
        put_rows(unit_ref, FIRST_ROWS + shared_start, pair_rows(shared, top))


class Gathered:
    def __init__(self, at, refs, held_ref, sems):
        self.narrow, self.core, self.side, self.depth = at[0], at[1], at[2], at[3]
        self.held = held_ref
        self.copies = {}
        for differs in (0, 1):
            for index in range(differs, 8, 2):
                copy = pltpu.make_async_copy(refs[index], held_ref.at[index], sems.at[index])
                copy.start()
                self.copies[index] = copy

    def part(self, other, differs, across, step):
        return self.held.at[4 * other + 2 * across + differs, step]

    def wait(self, differs):
        for index in range(differs, 8, 2):
            self.copies[index].wait()

    def chips(self):
        for differs in (0, 1):
            for step in range(4):
                yield differs, step, (self.depth ^ step) * 2 + (self.side ^ differs)

    def cores(self, differs, step, start, rows):
        upto = -(-rows // 16) * 16
        found = []
        for across in (0, 1):
            own = self.part(0, differs, across, step)[start : start + upto, :].astype(f32)[0:rows]
            other = self.part(1, differs, across, step)[start : start + upto, :].astype(f32)[0:rows]
            found.append(
                (jnp.where(self.core == 0, own, other), jnp.where(self.core == 0, other, own))
            )
        here, there = found
        return tuple(
            tuple(
                jnp.where((self.narrow == 0) == (tile == 0), here[core], there[core])
                for core in (0, 1)
            )
            for tile in (0, 1)
        )


def place_conv(units, kernel_ref):
    for differs, step, chip in units.chips():
        if step == 0:
            units.wait(differs)
        rows = pl.ds(aligned(chip * (2 * ROWS), 16), 2 * ROWS)
        low, high = units.cores(differs, step, 0, ROWS)
        kernel_ref[rows, 0:128] = jnp.concatenate(low, axis=0).astype(bf16)
        kernel_ref[rows, 256:384] = jnp.concatenate(high, axis=0).astype(bf16)
        low, high = units.cores(differs, step, 224, 112)
        kernel_ref[rows, 128:256] = jnp.concatenate(
            [middle(low[core], high[core], 112, ROWS) for core in (0, 1)], axis=0
        ).astype(bf16)


def place_film(units, film_ref):
    for differs, step, chip in units.chips():
        rows = pl.ds(aligned(chip * 96, 16), 96)
        low, high = units.cores(differs, step, FILM_AT, 96)
        for index in (0, 1):
            part = slice(48 * index, 48 * index + 48)
            film_ref[rows, index * C : index * C + 128] = jnp.concatenate(
                [low[core][part] for core in (0, 1)], axis=0
            ).astype(bf16)
            film_ref[rows, index * C + 256 : index * C + 384] = jnp.concatenate(
                [high[core][part] for core in (0, 1)], axis=0
            ).astype(bf16)
        low, high = units.cores(differs, step, FILM_SHARED, 48)
        both = [middle(low[core], high[core], 48, 96) for core in (0, 1)]
        for index in (0, 1):
            part = slice(48 * index, 48 * index + 48)
            film_ref[rows, index * C + 128 : index * C + 256] = jnp.concatenate(
                [both[core][part] for core in (0, 1)], axis=0
            ).astype(bf16)


def place_embeddings(shared, soft_ref):
    for differs, step, chip in shared.chips():
        for other in (0, 1):
            row = 4 * step + 2 * differs + other
            part = shared.part(other, differs, 0, step)[EMBED_AT : EMBED_AT + 16, :].astype(f32)
            part = (part * lax.logistic(part)).astype(bf16).astype(f32)
            for index in range(EMB // 128):
                soft_ref[row : row + 1, 128 * index : 128 * index + 128] = part[index : index + 1]


def place_attention(units, in_ref, out_ref):
    for differs, step, chip in units.chips():
        rows = pl.ds(aligned(chip * 48, 16), 48)
        low, high = units.cores(differs, step, IN_AT, 72)
        near, far = units.cores(differs, step, IN_SHARED, 40)
        both = [middle(near[core], far[core], 40, 72) for core in (0, 1)]
        for index in range(3):
            part = slice(24 * index, 24 * index + 24)
            for tile, source in ((0, low), (1, both), (2, high)):
                in_ref[rows, index * C + 128 * tile : index * C + 128 * tile + 128] = (
                    jnp.concatenate([source[core][part] for core in (0, 1)], axis=0)
                )
        low, high = units.cores(differs, step, OUT_AT, 24)
        near, far = units.cores(differs, step, OUT_SHARED, 16)
        both = [middle(near[core], far[core], 16, 24) for core in (0, 1)]
        for tile, source in ((0, low), (1, both), (2, high)):
            out_ref[rows, 128 * tile : 128 * tile + 128] = jnp.concatenate(source, axis=0)


def spread_heads(block):
    one, two, three = block[:, 0:128], block[:, 128:256], block[:, 256:384]
    place = lane(block.shape[0])

    def cut(value):
        return jnp.where(place < HEAD, value, 0.0)

    return jnp.concatenate(
        (
            cut(one),
            cut(jnp.where(place < 32, pltpu.roll(one, 32, 1), pltpu.roll(two, 32, 1))),
            cut(jnp.where(place < 64, pltpu.roll(two, 64, 1), pltpu.roll(three, 64, 1))),
            cut(pltpu.roll(three, 96, 1)),
        ),
        axis=1,
    )


def join_heads(block):
    one, two = block[:, 0:128], pltpu.roll(block[:, 128:256], HEAD, 1)
    return jnp.concatenate((jnp.where(lane(block.shape[0]) < HEAD, one, two), two), axis=1)


def first_norm(at, own_ref, other_ref, mask_ref, vec_own_ref, *refs):
    turned_ref, taps_ref, stat_ref, vec_ref, rows_ref, raw_ref = refs[-6:]
    narrow = at[0]
    own = vec_own_ref[...]
    other = (
        other_ref[HALF : HALF + 16, 0:HALF].astype(f32)
        + other_ref[HALF : HALF + 16, 256 : 256 + HALF].astype(f32)
    )[0:13]
    vec_ref[0:13, 0:HALF] = jnp.where(narrow == 0, own, other)
    vec_ref[0:13, HALF:C] = jnp.where(narrow == 0, other, own)
    vec_ref[13:16, :] = jnp.zeros((3, C), f32)
    own = own_ref[...].astype(f32)
    other = other_ref[0:HALF, :].astype(f32)
    low = jnp.where(narrow == 0, own, other)
    high = jnp.where(narrow == 0, other, own)
    for index in range(PIX // 128):
        here = slice(128 * index, 128 * index + 128)
        block = jnp.concatenate((low[:, here], high[:, here]), axis=0).T
        raw_ref[here, :] = block
        turned_ref[here, :] = block.astype(bf16)
    mean, inverse, tally = norm_stats(raw_ref, mask_ref)
    keep_stats(stat_ref, mean, inverse, tally)
    gain, shift = vec_ref[0:1, :], vec_ref[1:2, :]

    def apply(start, carry):
        valid = wide_mask(mask_ref, start, CHUNK)
        normed = (raw_ref[pl.ds(start, CHUNK), :] - mean) * inverse
        value = (normed * gain + shift) * valid
        rows_ref[pl.ds(start + 8, CHUNK), :] = value * lax.logistic(value)
        return carry

    chunks(apply, 0)
    write_taps(rows_ref, taps_ref)


def conv_then_stats(taps_ref, kernel_ref, mask_ref, vec_ref, out_ref, stat_ref):
    bias = vec_ref[2:3, :]

    def done(start, count, acc):
        out_ref[pl.ds(start, count), :] = acc + bias

    convolve(taps_ref, kernel_ref, done)
    keep_stats(stat_ref, *norm_stats(out_ref, mask_ref))


def first_conv(at, taps_ref, mask_ref, vec_ref, *refs):
    out_ref, kernel_ref, stat_ref, held_ref, sems = refs[-5:]
    units = Gathered(at, refs[0:8], held_ref, sems)
    place_conv(units, kernel_ref)
    conv_then_stats(taps_ref, kernel_ref, mask_ref, vec_ref, out_ref, stat_ref)


def first_conv_plain(at, taps_ref, mask_ref, vec_ref, kernel_ref, out_ref, stat_ref):
    conv_then_stats(taps_ref, kernel_ref, mask_ref, vec_ref, out_ref, stat_ref)


def film_to_third_norm(
    one_ref, stat_two_ref, turned_ref, mask_ref, vec_ref, embed_ref, kernel_ref, film_ref,
    taps_ref, residual_ref, hidden_ref, stat_ref, film_rows_ref, soft_ref, rows_ref,
):
    embed = embed_ref[...].astype(f32)
    soft = (embed * lax.logistic(embed)).astype(bf16)
    soft_ref[...] = jnp.broadcast_to(soft.astype(f32), soft_ref.shape)
    rounded = soft_ref[...].astype(bf16)
    scale = 1.0 + (
        jnp.dot(rounded, film_ref[:, 0:C], preferred_element_type=f32)[0:1] + vec_ref[11:12, :]
    )
    shift = jnp.dot(rounded, film_ref[:, C : 2 * C], preferred_element_type=f32)[0:1] + vec_ref[12:13, :]
    film_rows_ref[0:1, :] = scale
    film_rows_ref[1:2, :] = shift
    mean, inverse = stat_two_ref[0:1, :], stat_two_ref[1:2, :]
    gain_two, shift_two = vec_ref[3:4, :], vec_ref[4:5, :]

    def modulate(start, carry):
        valid = wide_mask(mask_ref, start, CHUNK)
        normed = (one_ref[pl.ds(start, CHUNK), :] - mean) * inverse
        value = (normed * gain_two + shift_two) * valid * scale + shift
        rows_ref[pl.ds(start + 8, CHUNK), :] = value * lax.logistic(value) * valid
        return carry

    chunks(modulate, 0)
    write_taps(rows_ref, taps_ref)
    bias = vec_ref[5:6, :]

    def done(start, count, acc):
        here = pl.ds(start, count)
        valid = wide_mask(mask_ref, start, count)
        residual_ref[here, :] = (turned_ref[here, :].astype(f32) + (acc + bias)) * valid

    convolve(taps_ref, kernel_ref, done)
    mean, inverse, tally = norm_stats(residual_ref, mask_ref)
    keep_stats(stat_ref, mean, inverse, tally)
    gain, shift_three = vec_ref[6:7, :], vec_ref[7:8, :]

    def apply(start, carry):
        valid = wide_mask(mask_ref, start, CHUNK)
        normed = (residual_ref[pl.ds(start, CHUNK), :] - mean) * inverse
        hidden_ref[pl.ds(start, CHUNK), :] = ((normed * gain + shift_three) * valid).astype(bf16)
        return carry

    chunks(apply, 0)


def second_conv_plain(
    at, one_ref, stat_two_ref, turned_ref, mask_ref, vec_ref, embed_ref, kernel_ref, film_ref,
    taps_ref, residual_ref, hidden_ref, stat_ref, film_rows_ref, soft_ref, rows_ref,
):
    film_to_third_norm(
        one_ref, stat_two_ref, turned_ref, mask_ref, vec_ref, embed_ref, kernel_ref, film_ref,
        taps_ref, residual_ref, hidden_ref, stat_ref, film_rows_ref, soft_ref, rows_ref,
    )


QUERY = 256


def attention_both(q_ref, k_ref, v_ref, kt_ref, vt_ref, upt_ref, outt_ref, dqt_ref, dk_acc, dv_acc):
    place = lax.broadcasted_iota(jnp.int32, (128, QUERY), 0)
    steps = PIX // QUERY

    def where(item):
        head, step = divmod(item, steps)
        return slice(128 * head, 128 * head + 128), slice(step * QUERY, step * QUERY + QUERY), step

    def raise_scores(item):
        columns, rows, _ = where(item)
        scores = lax.dot_general(
            k_ref[:, columns], q_ref[rows, columns], ON_LAST, preferred_element_type=f32
        )
        highest = jnp.max(scores, axis=0, keepdims=True)
        return jnp.exp2((scores - highest) * exponent_scale)

    def score_slopes(item, raised):
        columns, rows, _ = where(item)
        low = raised.astype(bf16)
        mixture = jnp.dot(vt_ref[columns, :], low, preferred_element_type=f32)
        inverse = 1.0 / mixture[HEAD : HEAD + 1, :]
        mixture = mixture * inverse
        outt_ref[columns, rows] = mixture.astype(bf16)
        up = (upt_ref[columns, rows].astype(f32) * inverse).astype(bf16)
        wide_up = up.astype(f32)
        both = jnp.sum(wide_up * mixture, axis=0, keepdims=True)
        coarse = both.astype(bf16).astype(f32)
        wide_up = jnp.where(place == HEAD, -coarse, wide_up)
        wide_up = jnp.where(place == HEAD + 1, coarse - both, wide_up)
        slopes = jnp.dot(v_ref[:, columns], wide_up.astype(bf16), preferred_element_type=f32)
        return low, up, (raised * slopes).astype(bf16)

    def gradients(item, low, up, slopes):
        columns, rows, step = where(item)
        dqt_ref[columns, rows] = (
            jnp.dot(kt_ref[columns, :], slopes, preferred_element_type=f32) * score_scale
        ).astype(bf16)
        dk = jnp.dot(slopes, q_ref[rows, columns], preferred_element_type=f32)
        dv = lax.dot_general(low, up, ON_LAST, preferred_element_type=f32)
        if step == 0:
            dk_acc[...] = dk
            dv_acc[...] = dv
        elif step < steps - 1:
            dk_acc[...] += dk
            dv_acc[...] += dv
        else:
            k_ref[:, columns] = ((dk_acc[...] + dk) * score_scale).astype(bf16)
            v_ref[:, columns] = (dv_acc[...] + dv).astype(bf16)

    count = HEADS * steps
    raised, waiting = raise_scores(0), None
    for item in range(count):
        following = raise_scores(item + 1) if item + 1 < count else None
        found = score_slopes(item, raised)
        if waiting is not None:
            gradients(*waiting)
        waiting = (item, *found)
        raised = following
    gradients(*waiting)


def attention_body(
    at, hidden_ref, residual_ref, stat_ref, mask_ref, vec_ref, own_ref, other_ref,
    out_ref, direct_ref, taps_ref, back_ref, vec_grad_ref, in_nat, out_nat,
    in_ref, weight_ref, q_ref, k_ref, v_ref, kt_ref, vt_ref, upt_ref, mixt_ref, dqt_ref,
    dk_acc, dv_acc, cot_ref, rows_ref, terms_ref, own_cot,
):
    narrow = at[0]
    for index in range(3):
        in_ref[:, 512 * index : 512 * index + 512] = spread_heads(
            in_nat[:, C * index : C * index + C]
        ).astype(bf16)
    blank = jnp.zeros((32, C), bf16)
    for head in range(HEADS):
        weight_ref[128 * head : 128 * head + HEAD, :] = out_nat[HEAD * head : HEAD * head + HEAD, :].astype(bf16)
        weight_ref[128 * head + HEAD : 128 * head + 128, :] = blank
    own = own_ref[...].astype(f32)
    other = other_ref[...].astype(f32)
    low = jnp.where(narrow == 0, own, other)
    high = jnp.where(narrow == 0, other, own)
    zero = jnp.zeros((8, C), f32)
    bias_out = zero
    for index in range(PIX // 128):
        here = slice(128 * index, 128 * index + 128)
        block = jnp.concatenate((low[:, here], high[:, here]), axis=0).T
        rows_ref[pl.ds(8 + 128 * index, 128), :] = block
        part = block * wide_mask(mask_ref, 128 * index, 128)
        bias_out = bias_out + fold(part)
        cot_ref[here, :] = part.astype(bf16)
        own_cot[here, :] = own_half(part, narrow).astype(bf16)
    bias_q = spread_heads(jnp.broadcast_to(vec_ref[8:9, :], (8, C)))[0:1]
    bias_v = spread_heads(jnp.broadcast_to(vec_ref[9:10, :], (8, C)))[0:1]
    block_rows = 256
    spare = lax.broadcasted_iota(jnp.int32, (block_rows, 512), 1) & 127
    for index in range(PIX // block_rows):
        here = slice(block_rows * index, block_rows * index + block_rows)
        hidden = hidden_ref[here, :]
        value = jnp.dot(hidden, in_ref[:, 0:512], preferred_element_type=f32) + bias_q
        q_ref[here, :] = jnp.where(spare == HEAD, 1.0, value).astype(bf16)
        value = jnp.dot(hidden, in_ref[:, 512:1024], preferred_element_type=f32)
        valid = mask_ref[here, :]
        barred = jnp.where(valid > 0, 0.0, masked_score)
        barred = jnp.concatenate((barred, barred, barred, barred), axis=1)
        value = jnp.where(spare == HEAD, barred, value).astype(bf16)
        k_ref[here, :] = value
        kt_ref[:, here] = value.T
        value = jnp.dot(hidden, in_ref[:, 1024:1536], preferred_element_type=f32) + bias_v
        value = jnp.where((spare == HEAD) | (spare == HEAD + 1), 1.0, value).astype(bf16)
        v_ref[here, :] = value
        vt_ref[:, here] = value.T
        upt_ref[:, here] = lax.dot_general(
            weight_ref[...], cot_ref[here, :], ON_LAST, preferred_element_type=f32
        ).astype(bf16)
    attention_both(q_ref, k_ref, v_ref, kt_ref, vt_ref, upt_ref, mixt_ref, dqt_ref, dk_acc, dv_acc)
    dk_ref, dv_ref = k_ref, v_ref
    bias = vec_ref[10:11, :]
    for index in range(PIX // 128):
        here = slice(128 * index, 128 * index + 128)
        value = jnp.dot(mixt_ref[:, here].T, weight_ref[...], preferred_element_type=f32) + bias
        valid = wide_mask(mask_ref, 128 * index, 128)
        quarter, side = divmod(index, 2)
        terms_ref[quarter * C : quarter * C + C, 128 * side : 128 * side + 128] = (
            residual_ref[here, :] + value * valid
        ).T
    for quarter in range(4):
        out_ref[:, 256 * quarter : 256 * quarter + 256] = terms_ref[
            pl.ds(aligned(quarter * C + narrow * HALF, 16), HALF), :
        ].astype(bf16)
    heads_here = pl.ds(aligned(narrow * 256, 128), 256)
    terms = jnp.dot(mixt_ref[...], own_cot[...], preferred_element_type=f32)
    for head in range(HEADS):
        out_nat[HEAD * head : HEAD * head + HEAD, 0:256] = terms[128 * head : 128 * head + HEAD]
    terms = jnp.dot(
        dqt_ref[pl.ds(aligned(narrow * 256, 128), 256), :],
        hidden_ref[...],
        preferred_element_type=f32,
    )
    in_nat[:, 0:256] = join_heads(terms.T)
    for index, source in ((1, dk_ref), (2, dv_ref)):
        terms = lax.dot_general(
            hidden_ref[...], source[:, heads_here], ON_FIRST, preferred_element_type=f32
        )
        in_nat[:, 256 * index : 256 * index + 256] = join_heads(terms)
    ones = jnp.ones((8, PIX), bf16)
    sums = (
        lax.dot_general(ones, dqt_ref[...], ON_LAST, preferred_element_type=f32),
        jnp.dot(ones, dv_ref[...], preferred_element_type=f32),
    )
    mean, inverse, tally = stat_ref[0:1, :], stat_ref[1:2, :], stat_ref[2:3, :]
    gain = vec_ref[6:7, :]
    acc_shift, acc_gain = zero, zero
    for index in range(PIX // 256):
        here = slice(256 * index, 256 * index + 256)
        value = None
        for part, source in enumerate((dqt_ref[:, here].T, dk_ref[here, :], dv_ref[here, :])):
            term = lax.dot_general(
                source, in_ref[:, 512 * part : 512 * part + 512], ON_LAST,
                preferred_element_type=f32,
            )
            value = term if value is None else value + term
        value = value * wide_mask(mask_ref, 256 * index, 256)
        normed = (residual_ref[here, :] - mean) * inverse
        acc_shift = acc_shift + fold(value)
        acc_gain = acc_gain + fold(value * normed)
        direct_ref[here, :] = value
    shift_grad, gain_grad = total(acc_shift), total(acc_gain)
    first_mean = group_sum(gain * shift_grad) / tally
    second_mean = group_sum(gain * gain_grad) / tally

    def back(start, carry):
        valid = wide_mask(mask_ref, start, CHUNK)
        here = pl.ds(start, CHUNK)
        normed = (residual_ref[here, :] - mean) * inverse
        extra = (direct_ref[here, :] * gain - first_mean - normed * second_mean) * inverse
        value = (rows_ref[pl.ds(start + 8, CHUNK), :] + extra) * valid
        direct_ref[here, :] = value
        low = value.astype(bf16).astype(f32)
        rows_ref[pl.ds(start + 8, CHUNK), :] = low
        return carry + fold(low)

    bias_two = chunks(back, zero)
    write_taps(rows_ref, taps_ref)
    write_own(rows_ref, back_ref, narrow)
    vec_grad_ref[...] = jnp.zeros_like(vec_grad_ref)
    vec_grad_ref[5:6, :] = total(bias_two)
    vec_grad_ref[6:7, :] = gain_grad
    vec_grad_ref[7:8, :] = shift_grad
    for row, acc in ((8, sums[0]), (9, sums[1])):
        pair_one, pair_two = join_heads(acc[:, 0:256]), join_heads(acc[:, 256:512])
        turned = pltpu.roll(pair_two[:, 0:128], 64, 1)
        natural = jnp.concatenate(
            (
                pair_one[:, 0:128],
                jnp.where(lane(8) < 64, pair_one[:, 128:256], turned),
                jnp.where(lane(8) < 64, turned, pltpu.roll(pair_two[:, 128:256], 64, 1)),
            ),
            axis=1,
        )
        vec_grad_ref[row : row + 1, :] = natural[0:1]
    vec_grad_ref[10:11, :] = total(bias_out)


def unit_rows(grad, chip, core):
    return pl.ds(aligned(chip * 2 * grad + core * grad, 8), grad)


def middle_of_block(
    at, stat_two_ref, turned_ref, mask_ref, vec_ref, embed_ref, *refs
):
    (
        out_ref, direct_ref, back_taps_ref, vec_grad_ref, film_rows_ref, kernel_ref, soft_all_ref,
        keep_ref, send_ref,
    ) = refs[11:20]
    (
        taps_ref, residual_ref, hidden_ref, stat_ref, soft_ref, film_ref, held_ref, sems, back_ref,
        one_ref, own_ref, other_ref, late_sems,
    ) = refs[20:33]
    attention_refs = refs[33:]
    in_nat, out_nat = attention_refs[0:2]
    rows_ref, terms_ref = attention_refs[-3:-1]
    units = Gathered(at, refs[0:8], held_ref, sems)
    one_far, own_far, exchanged_far = refs[8:11]
    late = [
        pltpu.make_async_copy(source, target, late_sems.at[index])
        for index, (source, target) in enumerate(
            (
                (one_far, one_ref),
                (own_far, own_ref),
                (exchanged_far.at[pl.ds(HALF + 16, HALF)], other_ref),
            )
        )
    ]
    for copy in late:
        copy.start()
    place_conv(units, kernel_ref)
    place_film(units, film_ref)
    place_embeddings(units, soft_all_ref)
    for copy in late:
        copy.wait()
    film_to_third_norm(
        one_ref, stat_two_ref, turned_ref, mask_ref, vec_ref, embed_ref, kernel_ref, film_ref,
        taps_ref, residual_ref, hidden_ref, stat_ref, film_rows_ref, soft_ref, rows_ref,
    )
    place_attention(units, in_nat, out_nat)
    attention_body(
        at, hidden_ref, residual_ref, stat_ref, mask_ref, vec_ref, own_ref, other_ref,
        out_ref, direct_ref, back_taps_ref, back_ref, vec_grad_ref, *attention_refs,
    )
    for chip in range(8):
        for target, core in ((keep_ref, at[1]), (send_ref, 1 - at[1])):
            rows = unit_rows(24, chip, core)
            block = jnp.concatenate(
                [in_nat[rows, 256 * index : 256 * index + 256] for index in range(3)], axis=0
            )
            target[chip, 336:416, :] = pad_rows(block[:, 0:128], 80).astype(bf16)
            target[chip, 416:464, :] = pad_rows(pair_rows(block[:, 128:256], 40), 48).astype(bf16)
            block = out_nat[rows, 0:256]
            target[chip, 464:496, :] = pad_rows(block[:, 0:128], 32).astype(bf16)
            target[chip, 496:512, :] = pair_rows(block[:, 128:256], 16).astype(bf16)
    kernel_terms(taps_ref, back_ref, terms_ref)
    pack_units(terms_ref, at, keep_ref, send_ref)


def attention_plain(
    at, hidden_ref, residual_ref, stat_ref, mask_ref, vec_ref, own_ref, other_ref,
    in_given, out_given, out_ref, direct_ref, taps_ref, back_ref, vec_grad_ref,
    in_term_ref, out_term_ref, *refs,
):
    in_nat, out_nat = refs[0:2]
    in_nat[...] = in_given[...].astype(f32)
    out_nat[...] = out_given[...].astype(f32)
    attention_body(
        at, hidden_ref, residual_ref, stat_ref, mask_ref, vec_ref, own_ref,
        other_ref.at[pl.ds(HALF + 16, HALF)], out_ref, direct_ref, taps_ref, back_ref, vec_grad_ref, *refs,
    )
    in_term_ref[...] = in_nat[:, 0:768]
    out_term_ref[...] = out_nat[:, 0:256]


def pack_units(terms_ref, at, keep_ref, send_ref):
    for chip in range(8):
        for target, core in ((keep_ref, at[1]), (send_ref, 1 - at[1])):
            rows = unit_rows(ROWS, chip, core)
            target[chip, 0:224, :] = pad_rows(terms_ref[rows, 0:128], 224).astype(bf16)
            target[chip, 224:336, :] = pair_rows(terms_ref[rows, 128:256], 112).astype(bf16)


def conv_terms_plain(at, taps_ref, own_ref, terms_ref):
    kernel_terms(taps_ref, own_ref, terms_ref)


def second_back(at, *refs):
    back_taps_ref, vec_grad_ref, keep_ref, send_ref = refs[-11:-7]
    grad_ref, rows_ref, back_ref, terms_ref, one_ref, taps_one_ref, sems = refs[-7:]
    copies = [
        pltpu.make_async_copy(source, target, sems.at[index])
        for index, (source, target) in enumerate(zip(refs[7:9], (one_ref, taps_one_ref)))
    ]
    for copy in copies:
        copy.start()
    second_back_body(
        at, *refs[:2], one_ref, *refs[2:7], back_taps_ref, back_ref, vec_grad_ref, grad_ref, rows_ref,
        copies[0].wait,
    )
    copies[1].wait()
    kernel_terms(taps_one_ref, back_ref, terms_ref)
    pack_units(terms_ref, at, keep_ref, send_ref)


def second_back_plain(at, *refs):
    second_back_body(at, *refs)


def second_back_body(
    at, taps_ref, kernel_ref, one_ref, stat_ref, film_rows_ref, mask_ref, vec_ref, vec_in_ref,
    back_taps_ref, back_ref, vec_grad_ref, grad_ref, rows_ref, ready=None,
):
    def done(start, count, acc):
        grad_ref[pl.ds(start, count), :] = acc

    convolve_back(taps_ref, kernel_ref, done)
    if ready is not None:
        ready()
    mean, inverse, tally = stat_ref[0:1, :], stat_ref[1:2, :], stat_ref[2:3, :]
    gain, shift = vec_ref[3:4, :], vec_ref[4:5, :]
    scale, offset = film_rows_ref[0:1, :], film_rows_ref[1:2, :]
    zero = jnp.zeros((8, C), f32)

    def gather(start, carry):
        plain, with_normed = carry
        valid = wide_mask(mask_ref, start, CHUNK)
        here = pl.ds(start, CHUNK)
        normed = (one_ref[here, :] - mean) * inverse
        value = grad_ref[here, :] * valid * slope((normed * gain + shift) * valid * scale + offset)
        grad_ref[here, :] = value
        return (plain + fold(value), with_normed + fold(value * normed))

    plain, with_normed = chunks(gather, (zero, zero))
    plain, with_normed = total(plain), total(with_normed)
    gain_grad, shift_grad = scale * with_normed, scale * plain
    first_mean = group_sum(gain * shift_grad) / tally
    second_mean = group_sum(gain * gain_grad) / tally
    joint = scale * gain

    def back(start, carry):
        valid = wide_mask(mask_ref, start, CHUNK)
        here = pl.ds(start, CHUNK)
        normed = (one_ref[here, :] - mean) * inverse
        value = (grad_ref[here, :] * joint - first_mean - normed * second_mean) * inverse * valid
        low = value.astype(bf16).astype(f32)
        rows_ref[pl.ds(start + 8, CHUNK), :] = low
        return carry + fold(low)

    bias = chunks(back, zero)
    write_taps(rows_ref, back_taps_ref)
    write_own(rows_ref, back_ref, at[0])
    vec_grad_ref[...] = vec_in_ref[...]
    vec_grad_ref[2:3, :] = total(bias)
    vec_grad_ref[3:4, :] = gain_grad
    vec_grad_ref[4:5, :] = shift_grad
    vec_grad_ref[11:12, :] = (gain * with_normed + shift * plain).astype(bf16).astype(f32)
    vec_grad_ref[12:13, :] = plain.astype(bf16).astype(f32)


def first_back(
    at, taps_ref, kernel_ref, turned_ref, stat_ref, direct_ref, mask_ref, vec_ref, vec_in_ref, *refs,
):
    out_ref, vec_grad_ref, grad_ref, turn_ref = refs[-4:]

    def done(start, count, acc):
        grad_ref[pl.ds(start, count), :] = acc

    convolve_back(taps_ref, kernel_ref, done)
    mean, inverse, tally = stat_ref[0:1, :], stat_ref[1:2, :], stat_ref[2:3, :]
    gain, shift = vec_ref[0:1, :], vec_ref[1:2, :]
    zero = jnp.zeros((8, C), f32)

    def gather(start, carry):
        plain, with_normed = carry
        valid = wide_mask(mask_ref, start, CHUNK)
        here = pl.ds(start, CHUNK)
        normed = (turned_ref[here, :].astype(f32) - mean) * inverse
        value = grad_ref[here, :] * slope((normed * gain + shift) * valid) * valid
        grad_ref[here, :] = value
        return (plain + fold(value), with_normed + fold(value * normed))

    plain, with_normed = chunks(gather, (zero, zero))
    shift_grad, gain_grad = total(plain), total(with_normed)
    first_mean = group_sum(gain * shift_grad) / tally
    second_mean = group_sum(gain * gain_grad) / tally
    for index in range(PIX // 128):
        here = slice(128 * index, 128 * index + 128)
        valid = wide_mask(mask_ref, 128 * index, 128)
        normed = (turned_ref[here, :].astype(f32) - mean) * inverse
        value = (grad_ref[here, :] * gain - first_mean - normed * second_mean) * inverse * valid
        turn_ref[:, here] = (value + direct_ref[here, :]).T
    out_ref[...] = turn_ref[pl.ds(aligned(at[0] * HALF, 16), HALF), :].astype(bf16)
    place = lax.broadcasted_iota(jnp.int32, (16, 1), 0)
    rows = jnp.where(place == 0, gain_grad, jnp.where(place == 1, shift_grad, vec_in_ref[...]))
    vec_grad_ref[...] = own_half(rows, at[0])


def add_cores(at, keep_ref, back_ref, own_ref, across_ref):
    for depth in range(4):
        for target, side in ((own_ref, at[2]), (across_ref, 1 - at[2])):
            chip = depth * 2 + side
            target[depth] = (keep_ref[chip].astype(f32) + back_ref[chip].astype(f32)).astype(bf16)


def add_sides(at, own_ref, back_ref, mine_ref, *across):
    for step, target in enumerate((mine_ref,) + across):
        depth = at[3] ^ step
        target[...] = (own_ref[depth].astype(f32) + back_ref[depth].astype(f32)).astype(bf16)


def add_cores_depth(at, keep_ref, back_ref, *targets):
    for step, target in enumerate(targets):
        for side in (0, 1):
            chip = (at[3] ^ step) * 2 + side
            target[side] = (keep_ref[chip].astype(f32) + back_ref[chip].astype(f32)).astype(bf16)


def add_depths(at, *refs):
    mine_ref, across_ref = refs[4:6]
    for target, side in ((mine_ref, at[2]), (across_ref, 1 - at[2])):
        terms = [ref[side].astype(f32) for ref in refs[0:4]]
        target[...] = (terms[0] + terms[1] + terms[2] + terms[3]).astype(bf16)


def adam_update(weight, gradient, moment, square, step_rate):
    moment_new = beta_one * moment + (1.0 - beta_one) * gradient
    square_new = beta_two * square + (1.0 - beta_two) * gradient * gradient
    ratio = (
        moment_new
        / (1.0 - beta_one**STEP)
        / (jnp.sqrt(square_new / (1.0 - beta_two**STEP)) + adam_eps)
    )
    return (weight - step_rate * (ratio + decay_rate * weight), moment_new, square_new)


def unpair_rows(block, rows):
    top = block.shape[0]
    return jnp.concatenate((block, pltpu.roll(block, 64, 1)[0 : rows - top]), axis=0)


def adam_into(gradient, given, outs, rate, where):
    weight, moment, square = (ref[where] for ref in given)
    results = adam_update(weight, gradient, moment, square, rate)
    for out, value in zip(outs, (gradient,) + results):
        out[where] = value


def conv_adam(parts, weight_ref, moment_ref, square_ref, outs, rate):
    def summed(start, stop):
        return sum(part[start:stop, :].astype(f32) for part in parts[1:]) + parts[0][
            start:stop, :
        ].astype(f32)

    low = summed(0, 224)[0:ROWS]
    high = unpair_rows(summed(224, 336), ROWS)
    gradient = jnp.concatenate((low, high[:, 0:64]), axis=1).T
    results = adam_update(weight_ref[...], gradient, moment_ref[...], square_ref[...], rate)
    for out, value in zip(outs, (gradient,) + results):
        out[...] = value
    return summed


def finish_first(at, *refs):
    conv_adam(refs[0:2], *refs[2:5], refs[5:9], step_rates()[0])


def finish_second(at, *refs):
    given, results = refs[4:13], refs[13:]
    summed = conv_adam(refs[0:4], *given[0:3], results[0:4], step_rates()[1])
    gradient = jnp.concatenate(
        (summed(336, 416)[0:72], unpair_rows(summed(416, 464)[0:40], 72)[:, 0:64]), axis=1
    )
    for index in range(3):
        adam_into(
            gradient[24 * index : 24 * index + 24], given[3:6], results[4:8], step_rates()[3], index
        )
    gradient = jnp.concatenate(
        (summed(464, 496)[0:24], unpair_rows(summed(496, 512), 24)[:, 0:64]), axis=1
    )
    adam_into(gradient, given[6:9], results[8:12], step_rates()[4], Ellipsis)


def finish_small(at, own_ref, one_ref, two_ref, three_ref, soft_ref, *refs):
    wide = (at[3] * 2 + at[2]) * 2 + at[1]
    given, results, grad_ref = refs[0:6], refs[6:14], refs[14]
    sums, films = None, []
    for ref in (own_ref, one_ref, two_ref, three_ref):
        rows = ref[...]
        sums = rows[0:16] if sums is None else sums + rows[0:16]
        for start in range(16, 24, 2):
            films.append(
                jnp.concatenate((rows[start : start + 1], rows[start + 1 : start + 2]), axis=1)
            )
    adam_into(sums[0:13, 0:HALF], given[0:3], results[0:4], step_rates()[5], Ellipsis)
    grad_ref[...] = lax.dot_general(
        soft_ref[...].astype(bf16), jnp.concatenate(films, axis=0).astype(bf16), ON_FIRST,
        preferred_element_type=f32,
    )
    here = pl.ds(aligned(wide * 48, 8), 48)
    for index in (0, 1):
        gradient = grad_ref[here, 256 * index : 256 * index + HALF]
        adam_into(
            gradient, given[3:6], results[4:8], step_rates()[2], (slice(None), index, slice(None))
        )


def along_depth(unit, wide):
    return [unit] + [
        lax.ppermute(unit, "wide", [(i, i ^ (4 * step)) for i in range(wide)])
        for step in (1, 2, 3)
    ]


def along_plane(stack, wide):
    diagonal = [(2 * i + x, 2 * (i ^ 2) + 1 - x) for i in range(wide) for x in (0, 1)]
    return [
        stack,
        lax.ppermute(stack, "wide", [(i, i ^ 2) for i in range(wide)]),
        lax.ppermute(stack, "narrow", [(0, 1), (1, 0)]),
        lax.ppermute(stack, ("wide", "narrow"), diagonal),
    ]


def both_cores(parts, wide):
    return list(parts) + [
        lax.ppermute(v, "wide", [(i, i ^ 1) for i in range(wide)]) for v in parts
    ]


def tie(values, after, scalars):
    ins = [pltpu.with_memory_space_constraint(v, pltpu.HBM) for v in (*values, *after)]
    return pl.pallas_call(
        pass_on,
        out_shape=tuple(shaped(v.shape, v.dtype) for v in values),
        in_specs=[pl.BlockSpec(memory_space=pltpu.SMEM)]
        + [pl.BlockSpec(memory_space=pltpu.HBM) for _ in ins],
        out_specs=tuple(pl.BlockSpec(memory_space=pltpu.HBM) for _ in values),
        input_output_aliases={index + 1: index for index in range(len(values))},
    )(scalars, *ins)


def add_core_units(keep, send, scalars, wide):
    back = lax.ppermute(send, "wide", [(i, i ^ 1) for i in range(wide)])
    four = shaped((4, keep.shape[1], 128), bf16)
    return call(add_cores, (four, four), (keep, back), scalars)


def add_far_units(own, across, scalars, wide):
    back = lax.ppermute(across, "wide", [(i, i ^ 2) for i in range(wide)])
    one = shaped((own.shape[1], 128), bf16)
    parts = call(add_sides, (one,) * 4, (own, back), scalars)
    return [parts[0]] + [
        lax.ppermute(parts[step], "wide", [(i, i ^ (4 * step)) for i in range(wide)])
        for step in (1, 2, 3)
    ]


def apart_along_depth(parts, wide):
    return [parts[0]] + [
        lax.ppermute(parts[step], "wide", [(i, i ^ (4 * step)) for i in range(wide)])
        for step in (1, 2, 3)
    ]


def pack_vectors(at, here_ref, core_ref, side_ref, out_ref):
    samples = (here_ref[...], core_ref[...], side_ref[0], side_ref[1])
    out_ref[0:16, :] = samples[0] + samples[1] + samples[2] + samples[3]
    for index, rows in enumerate(samples):
        out_ref[16 + 2 * index : 18 + 2 * index, :] = rows[11:13]


def gather_vectors(rows, scalars, wide):
    core = lax.ppermute(rows, "wide", [(i, i ^ 1) for i in range(wide)])
    side = lax.ppermute(jnp.stack((rows, core)), "wide", [(i, i ^ 2) for i in range(wide)])
    (packed,) = call(pack_vectors, (shaped((24, 256), f32),), (rows, core, side), scalars)
    return along_depth(packed, wide)


def per_device(
    features,
    embedding,
    valid_mask,
    cotangent,
    conv_first,
    conv_first_moment,
    conv_first_square,
    conv_second,
    conv_second_moment,
    conv_second_square,
    film_weight,
    film_weight_moment,
    film_weight_square,
    attend_in,
    attend_in_moment,
    attend_in_square,
    attend_out,
    attend_out_moment,
    attend_out_square,
    vectors,
    vectors_moment,
    vectors_square,
):
    wide = lax.axis_size("wide")
    unit_path = wide == 16
    narrow_at = lax.axis_index("narrow").astype(jnp.int32)
    wide_at = lax.axis_index("wide").astype(jnp.int32)
    scalars = jnp.stack((narrow_at, wide_at & 1, (wide_at >> 1) & 1, wide_at >> 2))
    flip = [(0, 1), (1, 0)]
    plane = shaped((PIX, C), f32)
    low_plane = shaped((PIX, C), bf16)
    taps = shaped((PADDED, 3 * C), bf16)
    back_half = shaped((PADDED, 256), bf16)
    kernel = shaped((9 * C, C), bf16)
    stats = shaped((8, C), f32)
    vec_rows = shaped((16, C), f32)
    half_plane = shaped((HALF, PIX), bf16)
    rows_scratch = pltpu.VMEM((PIX + 16, C), f32)

    mask = jnp.broadcast_to(valid_mask[0].astype(f32)[:, None], (PIX, 128))
    own_features = features[0]
    own_cotangent = cotangent[0]
    (exchange,) = call(
        pack_exchange,
        (shaped((2 * HALF + 16, PIX), bf16),),
        (own_features, vectors, own_cotangent),
        scalars,
    )
    exchanged = lax.ppermute(exchange, "narrow", flip)

    if unit_path:
        weights = (
            jnp.transpose(conv_first),
            jnp.transpose(conv_second),
            film_weight,
            jnp.transpose(attend_in, (1, 0, 2)),
            attend_out,
        )
        (unit,) = call(
            pack_weights,
            (shaped((FIRST_ROWS + SECOND_ROWS, 128), bf16),),
            (embedding,),
            scalars,
            tuple(pltpu.VMEM(v.shape, f32) for v in weights) + (pltpu.SemaphoreType.DMA((5,)),),
            far=weights,
        )
        first_stack, second_stack = call(
            stack_all,
            tuple(shaped((4, rows, 128), bf16) for rows in (FIRST_ROWS, SECOND_ROWS)),
            along_depth(unit, wide),
            scalars,
        )
        first_units = both_cores(along_plane(first_stack, wide), wide)
    else:

        def whole(array, axis):
            array = lax.all_gather(array.astype(bf16), "wide", axis=0, tiled=True)
            return lax.all_gather(array, "narrow", axis=axis, tiled=True)

        first_full, second_full = whole(conv_first, 1), whole(conv_second, 1)
        film_full = whole(film_weight, 2).reshape(EMB, 2 * C)
        in_full = whole(attend_in, 2).reshape(C, 3 * C)
        out_full = whole(attend_out, 1)

    turned, taps_one, stat_one, vecs = call(
        first_norm,
        (low_plane, taps, stats, vec_rows),
        (own_features, exchanged, mask, vectors),
        scalars,
        (rows_scratch, pltpu.VMEM((PIX, C), f32)),
        far=(first_stack,) if unit_path else (),
    )
    if unit_path:
        second_parts = along_plane(second_stack, wide)
        out_one, kernel_one, stat_two = call(
            first_conv,
            (plane, kernel, stats),
            (taps_one, mask, vecs),
            scalars,
            (
                pltpu.VMEM((8, 4, FIRST_ROWS, 128), bf16),
                pltpu.SemaphoreType.DMA((8,)),
            ),
            far=(*first_units, second_stack),
        )
        arrived = [tie((part,), (stat_two,), scalars)[0] for part in second_parts[1:4]]
        second_units = both_cores([second_parts[0], *arrived], wide)
    else:
        kernel_one = first_full
        out_one, stat_two = call(
            first_conv_plain, (plane, stats), (taps_one, mask, vecs, kernel_one), scalars
        )
    common = (out_one, stat_two, turned, mask, vecs, embedding)
    attention_scratch = (
        pltpu.VMEM((C, 3 * C), f32),
        pltpu.VMEM((C, C), f32),
        pltpu.VMEM((C, 1536), bf16),
        pltpu.VMEM((512, C), bf16),
        *([pltpu.VMEM((PIX, 512), bf16)] * 3),
        *([pltpu.VMEM((512, PIX), bf16)] * 5),
        pltpu.VMEM((PIX, 128), f32),
        pltpu.VMEM((PIX, 128), f32),
        pltpu.VMEM((PIX, C), bf16),
        rows_scratch,
        pltpu.VMEM((9 * C, 256), f32),
        pltpu.VMEM((PIX, 256), bf16),
    )
    back_scratch = (pltpu.VMEM((PIX, C), f32), rows_scratch)
    terms_scratch = (pltpu.VMEM((PADDED, 256), bf16), pltpu.VMEM((9 * C, 256), f32))
    if unit_path:
        units = shaped((8, 512, 128), bf16)
        (
            output, direct, taps_back, vec_grad, film_rows, kernel_two, soft_all, keep, send,
        ) = call(
            middle_of_block,
            (
                half_plane, plane, taps, vec_rows, stats, kernel, shaped((16, EMB), f32),
                units, units,
            ),
            common[1:],
            scalars,
            (
                pltpu.VMEM((PADDED, 3 * C), bf16),
                pltpu.VMEM((PIX, C), f32),
                pltpu.VMEM((PIX, C), bf16),
                pltpu.VMEM((8, C), f32),
                pltpu.VMEM((16, EMB), f32),
                pltpu.VMEM((EMB, 2 * C), bf16),
                pltpu.VMEM((8, 4, SECOND_ROWS, 128), bf16),
                pltpu.SemaphoreType.DMA((8,)),
                pltpu.VMEM((PADDED, 256), bf16),
                pltpu.VMEM((PIX, C), f32),
                pltpu.VMEM((HALF, PIX), bf16),
                pltpu.VMEM((HALF, PIX), bf16),
                pltpu.SemaphoreType.DMA((3,)),
                *attention_scratch,
            ),
            far=(*second_units, out_one, own_cotangent, exchanged),
            flops=4 * 10**10,
        )
        own_second, across_second = add_core_units(keep, send, scalars, wide)
        units = shaped((8, 336, 128), bf16)
        taps_back_one, vec_grad, keep, send = call(
            second_back,
            (taps, vec_rows, units, units),
            (taps_back, kernel_two, stat_two, film_rows, mask, vecs, vec_grad),
            scalars,
            back_scratch
            + terms_scratch
            + (
                pltpu.VMEM((PIX, C), f32),
                pltpu.VMEM((PADDED, 3 * C), bf16),
                pltpu.SemaphoreType.DMA((2,)),
            ),
            far=(out_one, taps_one, across_second),
        )
        parts_second = add_far_units(own_second, across_second, scalars, wide)
        back = lax.ppermute(send, "wide", [(i, i ^ 1) for i in range(wide)])
        sums_first = call(
            add_cores_depth, (shaped((2, FIRST_ROWS, 128), bf16),) * 4, (keep, back), scalars
        )
        one = shaped((FIRST_ROWS, 128), bf16)
        mine_first, across_first = call(
            add_depths, (one, one), apart_along_depth(sums_first, wide), scalars
        )
        parts_first = (
            mine_first,
            lax.ppermute(across_first, "wide", [(i, i ^ 2) for i in range(wide)]),
        )
        started = (sums_first[1],)
    else:
        kernel_two = second_full
        taps_two, residual, hidden, stat_three, film_rows = call(
            second_conv_plain,
            (taps, plane, low_plane, stats, stats),
            common + (kernel_two, film_full),
            scalars,
            (pltpu.VMEM((16, EMB), f32), rows_scratch),
        )
        output, direct, taps_back, back_two, vec_grad, in_term, out_term = call(
            attention_plain,
            (
                half_plane, plane, taps, back_half, vec_rows,
                shaped((C, 768), f32), shaped((C, 256), f32),
            ),
            (
                hidden, residual, stat_three, mask, vecs, own_cotangent, exchanged,
                in_full, out_full,
            ),
            scalars,
            attention_scratch,
        )
        (second_term,) = call(
            conv_terms_plain, (shaped((9 * C, 256), f32),), (taps_two, back_two), scalars
        )
        taps_back_one, back_one, vec_grad = call(
            second_back_plain,
            (taps, back_half, vec_rows),
            (taps_back, kernel_two, out_one, stat_two, film_rows, mask, vecs, vec_grad),
            scalars,
            back_scratch,
        )
        (first_term,) = call(
            conv_terms_plain, (shaped((9 * C, 256), f32),), (taps_one, back_one), scalars
        )
        started = ()
    input_gradient, vec_half = call(
        first_back,
        (half_plane, shaped((16, 256), f32)),
        (taps_back_one, kernel_one, turned, stat_one, direct, mask, vecs, vec_grad),
        scalars,
        (pltpu.VMEM((PIX, C), f32), pltpu.VMEM((C, PIX), f32)),
        far=started,
    )
    if unit_path:
        vec_shape, film_shape = shaped((13, HALF), f32), shaped(film_weight.shape, f32)
        small = call(
            finish_small,
            (vec_shape,) * 4 + (film_shape,) * 4,
            (
                *gather_vectors(vec_half, scalars, wide),
                soft_all,
                vectors,
                vectors_moment,
                vectors_square,
                film_weight,
                film_weight_moment,
                film_weight_square,
            ),
            scalars,
            (pltpu.VMEM((EMB, 512), f32),),
        )
        vec_results, film_results = small[:4], small[4:]
    else:
        vec_half = vec_half[:13, :HALF]
        vec_sum = lax.psum(vec_half, "wide")
        soft = jax.nn.silu(embedding.astype(f32)).astype(bf16)
        soft_all = lax.all_gather(soft, "wide", axis=0, tiled=True)
        rows_here = film_weight.shape[0]
        soft_here = lax.dynamic_slice_in_dim(soft_all, wide_at * rows_here, rows_here, axis=1)
        film_all = lax.all_gather(vec_half[11:13].astype(bf16)[None], "wide", axis=0, tiled=True)
        film_gradient = jnp.einsum("se,stj->etj", soft_here, film_all, preferred_element_type=f32)

    rates = step_rates()
    shard = shaped((HALF, ROWS), f32)

    def turned_shards(*shards):
        return tuple(jnp.transpose(v) for v in shards)

    if unit_path:
        in_shape, out_shape = shaped((3, 24, HALF), f32), shaped((24, HALF), f32)
        in_given = tuple(
            jnp.transpose(v, (1, 0, 2)) for v in (attend_in, attend_in_moment, attend_in_square)
        )
        second_results = call(
            finish_second,
            (shard,) * 4 + (in_shape,) * 4 + (out_shape,) * 4,
            (
                *parts_second,
                *turned_shards(conv_second, conv_second_moment, conv_second_square),
                *in_given,
                attend_out,
                attend_out_moment,
                attend_out_square,
            ),
            scalars,
        )
        in_results = tuple(jnp.transpose(v, (1, 0, 2)) for v in second_results[4:8])
        out_results = second_results[8:12]
        second_results = turned_shards(*second_results[:4])
        first_results = call(
            finish_first,
            (shard,) * 4,
            (*parts_first, *turned_shards(conv_first, conv_first_moment, conv_first_square)),
            scalars,
        )
        first_results = turned_shards(*first_results)
    else:

        def scatter(term):
            return lax.psum_scatter(term, "wide", scatter_dimension=0, tiled=True)

        first_gradient = scatter(first_term[:, :HALF])
        second_gradient = scatter(second_term[:, :HALF])
        in_gradient = scatter(in_term.reshape(C, 3, 256)[:, :, :HALF])
        out_gradient = scatter(out_term[:, :HALF])

        def finish(weight, gradient, moment, square, rate):
            return (gradient,) + adam_update(weight, gradient, moment, square, rate)

        first_results = finish(
            conv_first, first_gradient, conv_first_moment, conv_first_square, rates[0]
        )
        second_results = finish(
            conv_second, second_gradient, conv_second_moment, conv_second_square, rates[1]
        )
        film_results = finish(
            film_weight, film_gradient, film_weight_moment, film_weight_square, rates[2]
        )
        in_results = finish(
            attend_in, in_gradient, attend_in_moment, attend_in_square, rates[3]
        )
        out_results = finish(
            attend_out, out_gradient, attend_out_moment, attend_out_square, rates[4]
        )
        vec_results = finish(vectors, vec_sum, vectors_moment, vectors_square, rates[5])

    return (
        output[None],
        input_gradient[None],
        *first_results,
        *second_results,
        *film_results,
        *in_results,
        *out_results,
        *vec_results,
    )


def solution(mesh):
    in_specs = (
        P("wide", "narrow", None),
        P("wide", None),
        P("wide", None),
        P("wide", "narrow", None),
        P("wide", "narrow"),
        P("wide", "narrow"),
        P("wide", "narrow"),
        P("wide", "narrow"),
        P("wide", "narrow"),
        P("wide", "narrow"),
        P("wide", None, "narrow"),
        P("wide", None, "narrow"),
        P("wide", None, "narrow"),
        P("wide", None, "narrow"),
        P("wide", None, "narrow"),
        P("wide", None, "narrow"),
        P("wide", "narrow"),
        P("wide", "narrow"),
        P("wide", "narrow"),
        P(None, "narrow"),
        P(None, "narrow"),
        P(None, "narrow"),
    )
    out_specs = (
        P("wide", "narrow", None),
        P("wide", "narrow", None),
        P("wide", "narrow"),
        P("wide", "narrow"),
        P("wide", "narrow"),
        P("wide", "narrow"),
        P("wide", "narrow"),
        P("wide", "narrow"),
        P("wide", "narrow"),
        P("wide", "narrow"),
        P("wide", None, "narrow"),
        P("wide", None, "narrow"),
        P("wide", None, "narrow"),
        P("wide", None, "narrow"),
        P("wide", None, "narrow"),
        P("wide", None, "narrow"),
        P("wide", None, "narrow"),
        P("wide", None, "narrow"),
        P("wide", "narrow"),
        P("wide", "narrow"),
        P("wide", "narrow"),
        P("wide", "narrow"),
        P(None, "narrow"),
        P(None, "narrow"),
        P(None, "narrow"),
        P(None, "narrow"),
    )
    return jax.shard_map(
        per_device, mesh=mesh, in_specs=in_specs, out_specs=out_specs, check_vma=False
    )
```
